32 devices in a mesh: groups: 2 (over x), slab: 4 (over y, core), rep: 4 (over z).
Axes of the slice: x: 2, y: 2, z: 4, core: 2. Of those that a mesh axis runs over, the one named last changes fastest.
Arguments:
- fields: float32 [8, 5, 8, 4, 128], P(('groups', 'rep'), None, 'slab'), parts along dimension 0, may hold values from -6 to 6
- drop_mass: float32 [8, 4096], P(('groups', 'rep'), 'slab'), parts along dimension 0, may hold values from 0.2 to 2
- drop_vel: float32 [8, 3, 4096], P(('groups', 'rep'), None, 'slab'), parts along dimension 0, may hold values from -6 to 6
- drop_cell: int32 [8, 4096], P(('groups', 'rep'), 'slab'), parts along dimension 0, may hold values from 0 to 1023
- cross_list: int32 [8, 1024], P(('groups', 'rep'), 'slab'), parts along dimension 0, may hold values from 0 to 1023, as said below
- cross_count: int32 [8, 8], P(('groups', 'rep'), 'slab'), parts along dimension 0, may hold values from 0 to 128, as said below
- w_in: bfloat16 [27, 9, 256], replicated, may hold values from -0.375 to 0.375
- w_mid: bfloat16 [27, 256, 256], replicated, may hold values from -0.078125 to 0.078125
- w_out: bfloat16 [256, 5], replicated, may hold values from -0.375 to 0.375
- cotangent: float32 [8, 5, 8, 4, 128], P(('groups', 'rep'), None, 'slab'), parts along dimension 0, may hold values from -6 to 6
Outputs:
- new_fields: float32 [8, 5, 8, 4, 128], P(('groups', 'rep'), None, 'slab'), parts along dimension 0
- grad_first: float32 [54, 9, 256], P('groups'), parts along dimension 0
- grad_middle: float32 [54, 256, 256], P('groups'), parts along dimension 0
- grad_last: float32 [512, 5], P('groups'), parts along dimension 0
The draws below stay inside these ranges and needn't reach their ends.
There are 2 independent parts, one for each index of `groups`. The reference program is written for one: setup_inputs(seed, part) draws one part's arguments, and reference() takes and returns one part's arrays. A program takes and returns all parts, laid end to end along the dimension named above; an argument that names none is the same for every part. Nothing has to cross between parts.
Inputs may be any that keep to these rules, and one draw needn't show every extreme that they name: `cross_list`: within the 256 entries of one slab (up list, then down list) all entries are distinct local droplet numbers. `cross_count`: entries 2j and 2j+1 count the valid leading entries of slab j's up and down lists. In every sample some slab's up count and some slab's down count are 128, and one slab receives 128 droplets from each side. `drop_cell`: A cell is numbered (x * 4 + y) * 128 + z in the local coordinates of the slab the droplet belongs to after the step.
All inputs are finite; a program needn't handle non-finite values.
Results may differ from the reference program's by a relative error of at most 0.0063.
Values may be sent and summed in bfloat16 or wider, within the bound.
No kernel may reach another device: no remote copies, remote signals or barrier semaphores. Data moves between devices by JAX's collectives and lax.ppermute only.
A program may use at most 128 MiB of HBM per device.

```python
import math
import jax
import jax.numpy as jnp
from jax import lax

CIN = 9
COUT = 5
HID = 256
CAP = 128
CX = 2
NY = 4
NZ = 128
DROP_DEV = 1024
NX = 8
SAMPLES = 4
DROPS = 4096
N_SLAB = 4


def draw_cross_list(key, part):
    key = jax.random.fold_in(key, 7)
    keys = jax.random.split(key, SAMPLES * N_SLAB)
    orders = jax.vmap(lambda sub_key: jax.random.permutation(sub_key, DROP_DEV)[:2 * CAP])(keys)
    return orders.reshape(SAMPLES, N_SLAB * 2 * CAP).astype(jnp.int32)


def draw_cross_count(key, part):
    key = jax.random.fold_in(key, 19)
    first_key, second_key = jax.random.split(key)
    crossed = jax.random.randint(first_key, (SAMPLES, N_SLAB, 2), 0, CAP // 2 + 1)
    chosen = jax.random.randint(second_key, (SAMPLES, 1, 1), 0, N_SLAB)
    target = jnp.concatenate([chosen, (chosen + 2) % N_SLAB], axis=2)
    slabs = jnp.arange(N_SLAB)[None, :, None]
    crossed = jnp.where(slabs == target, CAP, crossed)
    return crossed.reshape(SAMPLES, N_SLAB * 2).astype(jnp.int32)


def touch_ends(values, stream_key, least, top_value):
    shape = values.shape
    spot = [jax.random.randint(jax.random.fold_in(stream_key, axis), (), 0, shape[axis]) for axis in range(len(shape))]
    values = values.at[tuple(spot)].set(least)
    longest = shape.index(max(shape))
    spot[longest] = (spot[longest] + 1) % shape[longest]
    return values.at[tuple(spot)].set(top_value)


def levels(stream_key, dims, cuts, low, high):
    factor_of, own = 1.0, jax.random.fold_in(stream_key, 6)
    for position, parts in cuts:
        draws = jnp.exp(jax.random.uniform(jax.random.fold_in(own, position), (parts,), jnp.float32, low / len(cuts), high / len(cuts)))
        factor_of = factor_of * jnp.repeat(draws, dims[position] // parts).reshape([-1 if axis == position else 1 for axis in range(len(dims))])
    return factor_of


def noise(key, dims, deviation, limit, pieces=(), held_as=jnp.bfloat16):
    loudness = levels(key, dims, pieces, -0.22, 0.18) if pieces else 1.0
    drawn = jax.random.normal(key, dims, jnp.float32) * deviation * loudness
    return jnp.minimum(jnp.maximum(drawn, -limit), limit).astype(held_as)


def setup_inputs(seed: int = 0, part: int = 0) -> dict:
    seeds = jax.random.split(jax.random.key(seed), 11)
    part_splits = jax.random.split(jax.random.fold_in(seeds[10], part), 11)
    return {
        "fields": noise(part_splits[0], (SAMPLES, 5, NX, NY, NZ), 1.0, 6.0, ((0, 4), (2, 4)), jnp.float32),
        "drop_mass": jnp.clip(jnp.exp(math.log(2.0) - 2.3025851 * jax.random.uniform(part_splits[1], (SAMPLES, DROPS), jnp.float32) ** levels(part_splits[1], (SAMPLES, DROPS), ((0, 4), (1, 4)), -0.2, 0.2)), 0.2, 2.0),
        "drop_vel": noise(part_splits[2], (SAMPLES, 3, DROPS), 1.0, 6.0, ((0, 4), (2, 4)), jnp.float32),
        "drop_cell": touch_ends(jax.random.randint(part_splits[3], (SAMPLES, DROPS), 0, CX * NY * NZ), jax.random.fold_in(part_splits[3], 1), 0, (CX * NY * NZ) - 1).astype(jnp.int32),
        "cross_list": draw_cross_list(jax.random.fold_in(jax.random.fold_in(seeds[10], part), 71), part),
        "cross_count": draw_cross_count(jax.random.fold_in(jax.random.fold_in(seeds[10], part), 71), part),
        "w_in": noise(seeds[6], (27, CIN, HID), (27 * CIN) ** -0.5, 0.375),
        "w_mid": noise(seeds[7], (27, HID, HID), (27 * HID) ** -0.5, 0.078125),
        "w_out": noise(seeds[8], (HID, COUT), HID ** -0.5, 0.375),
        "cotangent": noise(part_splits[9], (SAMPLES, 5, NX, NY, NZ), 1.0, 6.0, ((0, 4), (2, 4)), jnp.float32),
    }


dt_step = 0.2
viscosity = 0.05
drag_rate = 0.5
clip_rms = 0.5

def to_bf16(values):
    return lax.optimization_barrier(values.astype(jnp.bfloat16)).astype(jnp.float32)

def tap_offsets():
    return [(x_off - 1, y_off - 1, z_off - 1) for x_off in range(3) for y_off in range(3) for z_off in range(3)]

def shifted(values, offsets):
    for along, offset in enumerate(offsets):
        values = jnp.roll(values, -offset, along)
    return values

def conv_full(inputs, weights):
    summed = jnp.zeros(inputs.shape[:3] + (weights.shape[2],), jnp.float32)
    for tap_index, offsets in enumerate(tap_offsets()):
        summed = summed + jnp.einsum('xyzc,ch->xyzh', shifted(inputs, offsets), weights[tap_index].astype(jnp.float32))
    return summed

def silu_slope(preact):
    logistic = jax.nn.sigmoid(preact)
    return logistic * (1.0 + preact * (1.0 - logistic))

def deposit_sample(masses, velocity, cell_index, crossing, crossed):
    lists = crossing.reshape(N_SLAB, 2, CAP)
    counted = crossed.reshape(N_SLAB, 2)
    in_list = (jnp.arange(CAP, dtype=jnp.int32)[None, None, :] < counted[:, :, None]).astype(jnp.int32)
    signs = jnp.array([1, -1], jnp.int32)[None, :, None]
    owners = jnp.broadcast_to(jnp.arange(N_SLAB, dtype=jnp.int32)[:, None, None], lists.shape)
    moves = jnp.zeros((N_SLAB, DROP_DEV), jnp.int32).at[owners, lists].add(in_list * signs)
    target_slab = (jnp.arange(N_SLAB, dtype=jnp.int32)[:, None] + moves) % N_SLAB
    targets = (target_slab.reshape(-1) * (CX * NY * NZ) + cell_index).astype(jnp.int32)
    charges = jnp.concatenate([masses[None], masses[None] * velocity], 0)
    grid = jax.vmap(lambda row: jax.ops.segment_sum(row, targets, num_segments=NX * NY * NZ))(charges)
    return grid.reshape(4, NX, NY, NZ)

def sample_step(fields, masses, velocity, cell_index, crossing, crossed, cotangent, w_in, w_mid, w_out):
    deposit = deposit_sample(masses, velocity, cell_index, crossing, crossed)
    wind = fields[0:3]
    laplace = -6.0 * fields
    advect = jnp.zeros_like(fields)
    for along in (1, 2, 3):
        ahead = jnp.roll(fields, -1, along)
        behind = jnp.roll(fields, 1, along)
        laplace = laplace + ahead + behind
        advect = advect - wind[along - 1][None] * (ahead - behind) * 0.5
    drag_force = drag_rate * (deposit[1:4] - deposit[0][None] * wind)
    features = to_bf16(jnp.concatenate([fields, deposit[0:1], drag_force], 0))
    feat_last = jnp.moveaxis(features, 0, 3)
    pre_one = conv_full(feat_last, w_in)
    hidden_one = to_bf16(jax.nn.silu(pre_one))
    pre_two = conv_full(hidden_one, w_mid)
    hidden_two = to_bf16(jax.nn.silu(pre_two))
    closure = jnp.einsum('xyzh,hc->cxyz', hidden_two, w_out.astype(jnp.float32))
    momentum = jnp.concatenate([drag_force, jnp.zeros((2,) + fields.shape[1:], jnp.float32)], 0)
    new_fields = fields + dt_step * (viscosity * laplace + advect + closure + momentum)
    closure_grad = to_bf16(dt_step * cotangent)
    raw_last = jnp.einsum('xyzh,cxyz->hc', hidden_two, closure_grad)
    hidden_grad = jnp.einsum('cxyz,hc->xyzh', closure_grad, w_out.astype(jnp.float32))
    pre_two_grad = to_bf16(hidden_grad * silu_slope(pre_two))
    raw_middle = jnp.stack([jnp.einsum('xyzi,xyzo->io', shifted(hidden_one, offsets), pre_two_grad) for offsets in tap_offsets()])
    first_grad = jnp.zeros(hidden_one.shape, jnp.float32)
    for tap_index, offsets in enumerate(tap_offsets()):
        back = (-offsets[0], -offsets[1], -offsets[2])
        first_grad = first_grad + jnp.einsum('xyzo,io->xyzi', shifted(pre_two_grad, back), w_mid[tap_index].astype(jnp.float32))
    pre_one_grad = to_bf16(first_grad * silu_slope(pre_one))
    raw_first = jnp.stack([jnp.einsum('xyzc,xyzh->ch', shifted(feat_last, offsets), pre_one_grad) for offsets in tap_offsets()])
    return (new_fields, raw_first, raw_middle, raw_last)

def reference(fields, drop_mass, drop_vel, drop_cell, cross_list, cross_count, w_in, w_mid, w_out, cotangent):

    def one_sample(inputs):
        return sample_step(inputs[0], inputs[1], inputs[2], inputs[3], inputs[4], inputs[5], inputs[6], w_in, w_mid, w_out)
    new_fields, raw_first, raw_middle, raw_last = lax.map(one_sample, (fields, drop_mass, drop_vel, drop_cell, cross_list, cross_count, cotangent))
    raw_first = lax.optimization_barrier(jnp.sum(raw_first, 0))
    raw_middle = lax.optimization_barrier(jnp.sum(raw_middle, 0))
    raw_last = lax.optimization_barrier(jnp.sum(raw_last, 0))
    weight_count = raw_first.size + raw_middle.size + raw_last.size
    squares = jnp.sum(raw_first * raw_first) + jnp.sum(raw_middle * raw_middle) + jnp.sum(raw_last * raw_last)
    factor = jnp.minimum(1.0, clip_rms * math.sqrt(weight_count) / jnp.sqrt(squares + 1e-06))
    return (new_fields, raw_first * factor, raw_middle * factor, raw_last * factor)
```

```python
import functools
import math

import jax
import jax.numpy as jnp
from jax import lax
from jax.experimental import pallas as pl
from jax.experimental.pallas import tpu as pltpu
from jax.sharding import PartitionSpec as P

dt_step = 0.2
viscosity = 0.05
drag_rate = 0.5
clip_rms = 0.5

F32 = jnp.float32
BF16 = jnp.bfloat16
VMEM_BYTES = 58 * 2**20
offsets = [(x, y, z) for x in (-1, 0, 1) for y in (-1, 0, 1) for z in (-1, 0, 1)]


def dot(a, b):
    return lax.dot_general(a, b, (((1,), (0,)), ((), ())), preferred_element_type=F32)


def dot_nt(a, b):
    return lax.dot_general(a, b, (((1,), (1,)), ((), ())), preferred_element_type=F32)


def logistic(p):
    return 0.5 * jnp.tanh(0.5 * p) + 0.5


def roll_z(v, by, nz):
    return jnp.concatenate(
        [pltpu.roll(v[:, k : k + nz], by % nz, 1) for k in range(0, v.shape[1], nz)], 1
    )


def ahead_y(v, by, nz):
    if by == 0:
        return v
    cut = (by * nz) % v.shape[1]
    return jnp.concatenate([v[:, cut:], v[:, :cut]], 1)


def flat_cells(ref):
    planes, rows = ref.shape[2], ref.shape[3]
    return jnp.concatenate([ref[0, :, x, y, :] for x in range(planes) for y in range(rows)], 1)


def deposit_kernel(mass, vel, cell, listed, counts, stay, up, down):
    drops = mass.shape[1]
    slots = listed.shape[1]
    half = slots // 2
    k = lax.broadcasted_iota(jnp.int32, (1, slots), 1)
    valid = k < jnp.where(k < half, counts[0, 0], half + counts[0, 1])
    chosen = jnp.where(valid, listed[...], -1)
    member = (lax.broadcasted_iota(jnp.int32, (drops, slots), 0) == chosen).astype(F32).astype(BF16)
    row = lax.broadcasted_iota(jnp.int32, (16, slots), 0)
    column = lax.broadcasted_iota(jnp.int32, (16, slots), 1)
    which = (row == (column >= half).astype(jnp.int32)).astype(F32).astype(BF16)
    mask = dot_nt(which, member)
    goes_up, goes_down = mask[0:1], mask[1:2]
    m = mass[...]
    charges = jnp.concatenate([m, m * vel[0]], 0)
    high = charges.astype(BF16).astype(F32)
    both = jnp.concatenate([high, charges - high], 0)
    rows = jnp.concatenate(
        [both * (1.0 - goes_up - goes_down), both * goes_up, both * goes_down, jnp.zeros_like(both)], 0
    ).astype(BF16)
    chunk = 256
    for start in range(0, stay.shape[1], chunk):
        here = lax.broadcasted_iota(jnp.int32, (chunk, drops), 0) + start
        onehot = (here == cell[...]).astype(F32).astype(BF16)
        got = dot_nt(rows, onehot)
        for i, out in enumerate((stay, up, down)):
            out[:, start : start + chunk] = got[8 * i : 8 * i + 4] + got[8 * i + 4 : 8 * i + 8]


def feature_kernel(stay, below, above, fields, cotangent, feats, drag):
    deposit = stay[...] + below[...] + above[...]
    state = flat_cells(fields)
    force = drag_rate * (deposit[1:4] - deposit[0:1] * state[0:3])
    drag[...] = force
    cells = state.shape[1]
    feats[...] = jnp.concatenate(
        [
            dt_step * flat_cells(cotangent),
            force[2:3],
            jnp.zeros((2, cells), F32),
            state,
            deposit[0:1],
            force[0:2],
        ],
        0,
    ).astype(BF16)


def gather_taps(g2z, x, planes, nz, lead):
    pieces = []
    for ox, oy, oz in offsets:
        xi = lax.rem(x - ox + planes, planes)
        pieces.append(ahead_y(g2z[lead + (oz + 1, xi)], -oy, nz))
    return jnp.concatenate(pieces, 0)


def closure_kernel(
    nz, place, feats, wk, wt, wo, wc, piece, closure, g2z, fcol, w_first, fz, hidden, sums, mid, last
):
    s = pl.program_id(0)
    samples = pl.num_programs(0)
    slabs = feats.shape[0] // samples
    planes = hidden.shape[0]
    per = planes // slabs
    lanes = hidden.shape[2]
    block = wo.shape[0]

    @pl.when(s == 0)
    def _():
        mid[...] = jnp.zeros_like(mid)
        last[...] = jnp.zeros_like(last)
        w_first[...] = wk[...].astype(F32).T.astype(BF16)

    sums[...] = jnp.zeros_like(sums)

    def spread(j, carry):
        f = feats[place[j * samples + s]].astype(F32)
        for h in range(per):
            plane = f[:, h * lanes : (h + 1) * lanes]
            fz[0, j * per + h] = roll_z(plane, 1, nz)
            fz[1, j * per + h] = plane
            fz[2, j * per + h] = roll_z(plane, -1, nz)
        return carry

    lax.fori_loop(0, slabs, spread, 0)

    def first_two(x, carry):
        pieces, ninth = [], []
        for ox, oy, oz in offsets:
            xi = lax.rem(x + ox + planes, planes)
            v = ahead_y(fz[oz + 1, xi], oy, nz)
            pieces.append(v[8:16])
            ninth.append(v[5:6])
        pad = jnp.zeros((256 - 9 * len(offsets), lanes), F32)
        column = jnp.concatenate(pieces + ninth + [pad], 0).astype(BF16)
        fcol[0, x] = column
        pre = dot(w_first[...], column)
        hid = (pre * logistic(pre)).astype(BF16)
        hidden[x] = hid
        prod = dot(wt[...], hid)
        for ox in (-1, 0, 1):
            xi = lax.rem(x - ox + planes, planes)
            for oz in (-1, 0, 1):
                total = None
                for oy in (-1, 0, 1):
                    t = 9 * (ox + 1) + 3 * (oy + 1) + oz + 1
                    v = ahead_y(prod[t * block : (t + 1) * block], oy, nz)
                    total = v if total is None else total + v
                sums[oz + 1, xi] += total
        return carry

    lax.fori_loop(0, planes, first_two, 0)

    def second(j, carry):
        f = feats[place[j * samples + s]]
        for h in range(per):
            x = j * per + h
            here = f[:, h * lanes : (h + 1) * lanes]
            pre = sums[1, x] + roll_z(sums[0, x], 1, nz) + roll_z(sums[2, x], -1, nz)
            sig = logistic(pre)
            hid = (pre * sig).astype(BF16)
            out = dot(wc[...], hid)
            closure[0, x] = jnp.concatenate([out[0:8, : lanes // 2], out[0:8, lanes // 2 :]], 0).astype(BF16)
            grad = dot(wo[...], here) * (sig * (1.0 + pre * (1.0 - sig)))
            last[...] += dot_nt(hid, here)
            rounded = grad.astype(BF16)
            grad = rounded.astype(F32)
            g2z[0, 0, x] = roll_z(grad, -1, nz).astype(BF16)
            g2z[0, 1, x] = rounded
            g2z[0, 2, x] = roll_z(grad, 1, nz).astype(BF16)
        return carry

    lax.fori_loop(0, slabs, second, 0)

    def third(x, carry):
        mid[...] += dot_nt(gather_taps(g2z, x, planes, nz, (0,)), hidden[x])
        return carry

    lax.fori_loop(0, planes, third, 0)

    @pl.when(s == samples - 1)
    def _():
        total = mid[...]
        taps = total.shape[0]
        piece[0:taps] = total.astype(BF16)
        squares = jnp.sum(total * total, keepdims=True)
        high = squares.astype(BF16).astype(F32)
        width = total.shape[1]
        row = lax.broadcasted_iota(jnp.int32, (block, width), 0)
        column = lax.broadcasted_iota(jnp.int32, (block, width), 1)
        extra = jnp.concatenate([last[...], jnp.zeros((block, width - block), F32)], 1)
        extra = jnp.where(column < 5, extra, 0.0)
        extra = jnp.where((row == 0) & (column == 16), high, extra)
        extra = jnp.where((row == 0) & (column == 17), squares - high, extra)
        piece[taps:] = extra.astype(BF16)


def first_kernel(nz, wk, wt, fcol, g2z, out, w_first, w_back):
    planes = fcol.shape[1]

    @pl.when(pl.program_id(0) == 0)
    def _():
        out[...] = jnp.zeros_like(out)
        w_first[...] = wk[...].astype(F32).T.astype(BF16)
        w_back[...] = wt[...].astype(F32).T.astype(BF16)

    def body(x, carry):
        back = dot(w_back[...], gather_taps(g2z, x, planes, nz, (0,)))
        column = fcol[0, x]
        pre = dot(w_first[...], column)
        sig = logistic(pre)
        grad = (back * (sig * (1.0 + pre * (1.0 - sig)))).astype(BF16)
        out[...] += dot_nt(column, grad)
        return carry

    lax.fori_loop(0, planes, body, 0)


def step_kernel(nz, place, fields, drag, closure, feats, out):
    state = flat_cells(fields)
    cells = state.shape[1]
    planes, rows = fields.shape[2], fields.shape[3]
    lanes = cells // planes
    lower = feats[place[0]][8:13, cells - lanes :].astype(F32)
    upper = feats[place[1]][8:13, :lanes].astype(F32)
    wide = jnp.concatenate([lower, state, upper], 1)
    next_x, last_x = wide[:, 2 * lanes :], wide[:, :cells]
    parts = [state[:, i * lanes : (i + 1) * lanes] for i in range(planes)]
    next_y = jnp.concatenate([ahead_y(v, 1, nz) for v in parts], 1)
    last_y = jnp.concatenate([ahead_y(v, -1, nz) for v in parts], 1)
    next_z, last_z = roll_z(state, -1, nz), roll_z(state, 1, nz)
    laplace = next_x + last_x + next_y + last_y + next_z + last_z - 6.0 * state
    advect = -0.5 * (
        state[0:1] * (next_x - last_x) + state[1:2] * (next_y - last_y) + state[2:3] * (next_z - last_z)
    )
    momentum = jnp.concatenate([drag[...], jnp.zeros((2, cells), F32)], 0)
    new = state + dt_step * (viscosity * laplace + advect + closure[0:5, :] + momentum)
    for x in range(planes):
        for y in range(rows):
            at = (x * rows + y) * nz
            out[0, :, x, y, :] = new[:, at : at + nz]


def finish_kernel(count, weight_count, place, *refs):
    pieces, (first, mid_out, first_out, last_out, held, sems, factor) = refs[:count], refs[count:]
    step = pl.program_id(0)
    taps_here = mid_out.shape[0]
    slots = held.shape[0]
    block = mid_out.shape[1] // slots
    rows = held.shape[1] - 16

    @pl.when(step == 0)
    def _():
        copies, at = [], 0
        for i, ref in enumerate(pieces):
            copies.append(pltpu.make_async_copy(ref, held.at[at : at + ref.shape[0]], sems.at[i]))
            at += ref.shape[0]
        for copy in copies:
            copy.start()
        for copy in copies:
            copy.wait()
        raw = first[...]
        squares = jnp.sum(raw * raw, keepdims=True)
        last = []
        for d in range(slots):
            extra = held[place[d], rows:].astype(F32)
            last.append(extra[:, 0:5])
            squares = squares + jnp.sum(extra[0:1, 16:18], keepdims=True)
        last = jnp.concatenate(last, 0)
        squares = squares + jnp.sum(last * last, keepdims=True)
        clip = jnp.minimum(1.0, clip_rms * math.sqrt(weight_count) / jnp.sqrt(squares + 1e-06))
        factor[...] = jnp.broadcast_to(clip, factor.shape)
        last_out[...] = last * clip
        scaled = raw * clip
        for t in range(27):
            first_out[t, 0:8] = scaled[8 * t : 8 * t + 8]
            first_out[t, 8:9] = scaled[216 + t : 217 + t]

    width = mid_out.shape[1]
    eye = (
        lax.broadcasted_iota(jnp.int32, (width, width), 0) == lax.broadcasted_iota(jnp.int32, (width, width), 1)
    ).astype(F32).astype(BF16)
    clip = factor[0:1, 0:1]
    for i in range(taps_here):
        start = pl.multiple_of((step * taps_here + i) * block, block)
        flipped = jnp.concatenate([held[place[d], pl.ds(start, block)] for d in range(slots)], 0)
        mid_out[i] = dot_nt(eye, flipped) * clip


def whole_spec(shape):
    return pl.BlockSpec(shape, lambda *unused: (0,) * len(shape))


SMEM = pl.BlockSpec(memory_space=pltpu.SMEM)
VMEM = pl.BlockSpec(memory_space=pltpu.VMEM)
ANY = pl.BlockSpec(memory_space=pl.ANY)


def params(**more):
    return pltpu.CompilerParams(vmem_limit_bytes=VMEM_BYTES, **more)


def shards(
    fields, drop_mass, drop_vel, drop_cell, cross_list, cross_count, w_in, w_mid, w_out, cotangent
):
    shape = jax.ShapeDtypeStruct
    n_slab, n_rep = lax.axis_size("slab"), lax.axis_size("rep")
    planes, ny, nz = fields.shape[2:]
    cells = planes * ny * nz
    lanes = ny * nz
    hid, cout = w_out.shape
    joined = n_slab * n_rep * 16 <= hid
    team = ("slab", "rep") if joined else ("slab",)
    samples = n_rep if joined else 1
    size = n_slab * samples
    block = hid // size
    fast = joined and n_slab == 4 and n_rep == 4
    slab, rep = lax.axis_index("slab"), lax.axis_index("rep")
    sample = rep if joined else jnp.zeros((), jnp.int32)
    me = slab * samples + sample
    all_planes = n_slab * planes
    everyone = jnp.arange(size, dtype=jnp.int32)

    def trade(v, mask):
        return lax.ppermute(v, team, [(d, d ^ mask) for d in range(size)])

    dense = shape((4, cells), F32)
    stay, up, down = pl.pallas_call(
        deposit_kernel,
        out_shape=(dense, dense, dense),
        in_specs=[VMEM] * 4 + [SMEM],
        out_specs=(VMEM,) * 3,
        compiler_params=params(),
        name="deposit",
    )(drop_mass, drop_vel, drop_cell, cross_list, cross_count)
    from_below = lax.ppermute(up, "slab", [(i, (i + 1) % n_slab) for i in range(n_slab)])
    from_above = lax.ppermute(down, "slab", [((i + 1) % n_slab, i) for i in range(n_slab)])
    own_feats, drag = pl.pallas_call(
        feature_kernel,
        out_shape=(shape((16, cells), BF16), shape((3, cells), F32)),
        in_specs=[VMEM] * 5,
        out_specs=(VMEM,) * 2,
        compiler_params=params(),
        name="features",
    )(stay, from_below, from_above, fields, cotangent)

    if fast:
        order = (8, 1, 2, 4)
        feats = own_feats[None]
        for mask in order:
            feats = jnp.concatenate([feats, trade(feats, mask)], 0)
        apart = me ^ everyone
        feat_place = sum(((apart & mask) != 0).astype(jnp.int32) << i for i, mask in enumerate(order))
    else:
        feats = lax.all_gather(own_feats, team)
        feat_place = everyone

    w_block = lax.dynamic_slice(w_mid, (0, 0, me * block), (27, hid, block))
    wt = jnp.transpose(w_block, (0, 2, 1)).reshape(27 * block, hid)
    wk = jnp.concatenate([w_in[:, :8].reshape(216, hid), w_in[:, 8], jnp.zeros((13, hid), BF16)], 0)
    out_block = lax.dynamic_slice(w_out, (me * block, 0), (block, cout))
    wo = jnp.pad(out_block, ((0, 0), (0, 16 - cout)))
    wc = jnp.pad(out_block.T, ((0, 16 - cout), (0, 0)))

    rows = 27 * block
    piece, closure, g2z, fcol = pl.pallas_call(
        functools.partial(closure_kernel, nz),
        grid=(samples,),
        out_shape=(
            shape((rows + 16, hid), BF16),
            shape((samples, all_planes, 16, lanes // 2), BF16),
            shape((samples, 3, all_planes, block, lanes), BF16),
            shape((samples, all_planes, 256, lanes), BF16),
        ),
        in_specs=[SMEM] + [VMEM] * 5,
        out_specs=(
            whole_spec((rows + 16, hid)),
            pl.BlockSpec((1, all_planes, 16, lanes // 2), lambda s: (s, 0, 0, 0)),
            pl.BlockSpec((1, 3, all_planes, block, lanes), lambda s: (s, 0, 0, 0, 0)),
            pl.BlockSpec((1, all_planes, 256, lanes), lambda s: (s, 0, 0, 0)),
        ),
        scratch_shapes=[
            pltpu.VMEM((hid, 256), BF16),
            pltpu.VMEM((3, all_planes, 16, lanes), F32),
            pltpu.VMEM((all_planes, hid, lanes), BF16),
            pltpu.VMEM((3, all_planes, block, lanes), F32),
            pltpu.VMEM((rows, hid), F32),
            pltpu.VMEM((block, 16), F32),
        ],
        compiler_params=params(),
        name="closure",
    )(feat_place, feats, wk, wt, wo, wc)

    raw_first = pl.pallas_call(
        functools.partial(first_kernel, nz),
        grid=(samples,),
        out_shape=shape((256, hid), F32),
        in_specs=[
            whole_spec((256, hid)),
            whole_spec((rows, hid)),
            pl.BlockSpec((1, all_planes, 256, lanes), lambda s: (s, 0, 0, 0)),
            pl.BlockSpec((1, 3, all_planes, block, lanes), lambda s: (s, 0, 0, 0, 0)),
        ],
        out_specs=whole_spec((256, hid)),
        scratch_shapes=[pltpu.VMEM((hid, 256), BF16), pltpu.VMEM((hid, rows), BF16)],
        compiler_params=params(),
        name="first",
    )(wk, wt, fcol, g2z)

    closure = closure.reshape(samples, n_slab, planes, 16, lanes // 2)
    if fast:
        z = rep
        outer = (z == 0) | (z == 3)

        def line(v, pairs):
            return lax.ppermute(v, "rep", pairs)

        def tie(*values):
            return lax.optimization_barrier(values)

        y0 = trade(piece, 8)
        p1 = line(piece, [(0, 1), (1, 0), (2, 3), (3, 2)])
        p2 = line(piece, [(1, 2), (2, 1)])
        y0, p1, p2 = tie(y0, p1, p2)
        y1 = trade(p1, 8)
        p4 = line(p2, [(1, 0), (2, 3)])
        p3 = line(p1, [(1, 2), (2, 1)])
        y1, p3, p4 = tie(y1, p3, p4)
        q2 = jnp.where(outer, p4, p2)
        y2 = trade(q2, 8)
        p5 = line(p3, [(1, 0), (2, 3)])
        c0 = trade(jnp.stack([piece, y0, p1, y1]), 4)
        y2, p5, c0 = tie(y2, p5, c0)
        q3 = jnp.where(outer, p5, p3)
        y3 = trade(q3, 8)
        c1 = trade(jnp.stack([q2, y2, q3]), 4)
        c2 = trade(y3, 4)
        pieces = [v[None] for v in (piece, y0, p1, y1, q2, y2, q3, y3)] + [c0, c1, c2[None]]
        m2 = jnp.where(outer, 2, 3)
        masks = jnp.stack([jnp.int32(0), jnp.int32(8), jnp.int32(1), jnp.int32(9), m2, m2 | 8, m2 ^ 1, (m2 ^ 1) | 8])
        masks = jnp.concatenate([masks, masks | 4])
        piece_place = jnp.argmax((me ^ everyone)[:, None] == masks[None, :], axis=1).astype(jnp.int32)

        core, y = slab & 1, slab >> 1

        def halves(v, axis, bit):
            low, high = lax.index_in_dim(v, 0, axis, False), lax.index_in_dim(v, 1, axis, False)
            return jnp.where(bit == 0, low, high), jnp.where(bit == 0, high, low)

        raw_keep, raw_send = halves(raw_first.reshape(2, 128, hid), 0, core)
        part = closure.reshape(2, 2, 2, 2, planes * 16, lanes // 2).astype(F32)
        first_stage = True
        for mask, axis, bit in ((4, 3, core), (8, 2, y), (1, 1, z & 1), (2, 0, z >> 1)):
            keep, send = halves(part, axis, bit)
            if not first_stage:
                raw_send = raw_keep = raw_keep.astype(BF16)
            message = jnp.concatenate(
                [raw_send.astype(BF16), send.astype(BF16).reshape(-1, lanes // 2)], 0
            )
            got = trade(message, mask).astype(F32)
            raw_keep = raw_keep.astype(F32) + got[:128]
            part = keep + got[128:].reshape(keep.shape)
            first_stage = False
        other = trade(raw_keep, 4)
        low, high = jnp.where(core == 0, raw_keep, other), jnp.where(core == 0, other, raw_keep)
        raw_first = jnp.concatenate([low, high], 0)
        own_closure = part.reshape(planes, 2, 8, lanes // 2)
    else:
        if not joined:
            raw_first = lax.psum(raw_first, "rep")
            body = lax.psum(piece[:rows].astype(F32), "rep")
            extra = lax.psum(piece[rows:].astype(F32), "rep")
            squares = jnp.sum(body * body)
            high = squares.astype(BF16).astype(F32)
            extra = extra.at[0, 16].set(high).at[0, 17].set(squares - high)
            piece = jnp.concatenate([body, extra], 0).astype(BF16)
        raw_first = lax.psum(raw_first, team)
        pieces = [lax.all_gather(piece, team)]
        piece_place = everyone
        part = jnp.swapaxes(closure, 0, 1).reshape((size,) + closure.shape[2:]).astype(F32)
        own_closure = lax.psum_scatter(part, team, scatter_dimension=0).reshape(planes, 2, 8, lanes // 2)
    own_closure = jnp.transpose(own_closure, (2, 0, 1, 3)).reshape(8, cells)

    near = jnp.stack([(slab + n_slab - 1) % n_slab, (slab + 1) % n_slab]) * samples + sample
    new_fields = pl.pallas_call(
        functools.partial(step_kernel, nz),
        out_shape=shape(fields.shape, F32),
        in_specs=[SMEM] + [VMEM] * 4,
        out_specs=VMEM,
        compiler_params=params(),
        name="step",
    )(jnp.take(feat_place, near), fields, drag, own_closure, feats)

    weight_count = w_in.size + w_mid.size + w_out.size
    step_taps = 3
    grads = pl.pallas_call(
        functools.partial(finish_kernel, len(pieces), weight_count),
        grid=(27 // step_taps,),
        out_shape=(shape((27, hid, hid), F32), shape(w_in.shape, F32), shape(w_out.shape, F32)),
        in_specs=[SMEM] + [ANY] * len(pieces) + [whole_spec((256, hid))],
        out_specs=(
            pl.BlockSpec((step_taps, hid, hid), lambda i: (i, 0, 0)),
            whole_spec(w_in.shape),
            whole_spec(w_out.shape),
        ),
        scratch_shapes=[
            pltpu.VMEM((size, rows + 16, hid), BF16),
            pltpu.SemaphoreType.DMA((len(pieces),)),
            pltpu.VMEM((8, 128), F32),
        ],
        compiler_params=params(),
        name="finish",
    )(piece_place, *pieces, raw_first)
    grad_middle, grad_first, grad_last = grads
    return (new_fields, grad_first, grad_middle, grad_last)


def solution(mesh):
    placed = (
        P(("groups", "rep"), None, "slab", None, None),
        P(("groups", "rep"), "slab"),
        P(("groups", "rep"), None, "slab"),
        P(("groups", "rep"), "slab"),
        P(("groups", "rep"), "slab"),
        P(("groups", "rep"), "slab"),
        P(),
        P(),
        P(),
        P(("groups", "rep"), None, "slab", None, None),
    )
    return jax.shard_map(
        shards,
        mesh=mesh,
        in_specs=placed,
        out_specs=(
            P(("groups", "rep"), None, "slab", None, None),
            P("groups", None, None),
            P("groups", None, None),
            P("groups", None),
        ),
        check_vma=False,
    )
```

```python
import functools
import math

import jax
import jax.numpy as jnp
from jax import lax
from jax.experimental import pallas as pl
from jax.experimental.pallas import tpu as pltpu
from jax.sharding import PartitionSpec as P

dt_step = 0.2
viscosity = 0.05
drag_rate = 0.5
clip_rms = 0.5

F32 = jnp.float32
BF16 = jnp.bfloat16
VMEM_BYTES = 58 * 2**20
offsets = [(x, y, z) for x in (-1, 0, 1) for y in (-1, 0, 1) for z in (-1, 0, 1)]


def dot(a, b):
    return lax.dot_general(a, b, (((1,), (0,)), ((), ())), preferred_element_type=F32)


def dot_nt(a, b):
    return lax.dot_general(a, b, (((1,), (1,)), ((), ())), preferred_element_type=F32)


def logistic(p):
    return 0.5 * jnp.tanh(0.5 * p) + 0.5


def roll_z(v, by, nz):
    return jnp.concatenate(
        [pltpu.roll(v[:, k : k + nz], by % nz, 1) for k in range(0, v.shape[1], nz)], 1
    )


def ahead_y(v, by, nz):
    if by == 0:
        return v
    cut = (by * nz) % v.shape[1]
    return jnp.concatenate([v[:, cut:], v[:, :cut]], 1)


def flat_cells(ref):
    planes, rows = ref.shape[2], ref.shape[3]
    return jnp.concatenate([ref[0, :, x, y, :] for x in range(planes) for y in range(rows)], 1)


def deposit_kernel(mass, vel, cell, listed, counts, stay, up, down):
    drops = mass.shape[1]
    slots = listed.shape[1]
    half = slots // 2
    k = lax.broadcasted_iota(jnp.int32, (1, slots), 1)
    valid = k < jnp.where(k < half, counts[0, 0], half + counts[0, 1])
    chosen = jnp.where(valid, listed[...], -1)
    member = (lax.broadcasted_iota(jnp.int32, (drops, slots), 0) == chosen).astype(F32).astype(BF16)
    row = lax.broadcasted_iota(jnp.int32, (16, slots), 0)
    column = lax.broadcasted_iota(jnp.int32, (16, slots), 1)
    which = (row == (column >= half).astype(jnp.int32)).astype(F32).astype(BF16)
    mask = dot_nt(which, member)
    goes_up, goes_down = mask[0:1], mask[1:2]
    m = mass[...]
    charges = jnp.concatenate([m] + [m * vel[i] for i in range(vel.shape[0])], 0)
    high = charges.astype(BF16).astype(F32)
    both = jnp.concatenate([high, charges - high], 0)
    rows = jnp.concatenate(
        [both * (1.0 - goes_up - goes_down), both * goes_up, both * goes_down, jnp.zeros_like(both)], 0
    ).astype(BF16)
    chunk = 256
    for start in range(0, stay.shape[1], chunk):
        here = lax.broadcasted_iota(jnp.int32, (chunk, drops), 0) + start
        onehot = (here == cell[...]).astype(F32).astype(BF16)
        got = dot_nt(rows, onehot)
        for i, out in enumerate((stay, up, down)):
            out[:, start : start + chunk] = got[8 * i : 8 * i + 4] + got[8 * i + 4 : 8 * i + 8]


def feature_kernel(stay, below, above, fields, cotangent, feats, drag):
    deposit = stay[...] + below[...] + above[...]
    state = flat_cells(fields)
    force = drag_rate * (deposit[1:4] - deposit[0:1] * state[0:3])
    drag[...] = force
    cells = state.shape[1]
    feats[...] = jnp.concatenate(
        [
            dt_step * flat_cells(cotangent),
            force[2:3],
            jnp.zeros((2, cells), F32),
            state,
            deposit[0:1],
            force[0:2],
        ],
        0,
    ).astype(BF16)


def tap_rows():
    r = lax.broadcasted_iota(jnp.int32, (288, 256), 0)
    k = lax.broadcasted_iota(jnp.int32, (288, 256), 1)
    c, t = r >> 5, r & 31
    ox = (t >= 9).astype(jnp.int32) + (t >= 18).astype(jnp.int32)
    q = t - 9 * ox
    ninth = jnp.where(q < 8, 216 + 8 * ox + q, 240 + ox)
    at = jnp.where(c < 8, 8 * t + c, ninth)
    return ((at == k) & (t < 27)).astype(F32).astype(BF16)


def weight_kernel(me, w_in, w_mid, w_out, wt, w_back, w_first, wo, wc):
    block, hid = wo.shape[0], wt.shape[1]
    row = lax.broadcasted_iota(jnp.int32, (block, hid), 0)
    column = lax.broadcasted_iota(jnp.int32, (block, hid), 1)
    chosen = (column == row + me[0] * block).astype(F32).astype(BF16)
    for t in range(27):
        wt[t * block : (t + 1) * block] = dot_nt(chosen, w_mid[t]).astype(BF16)
    w_back[...] = wt[...].astype(F32).T.astype(BF16)
    pad = jnp.zeros((5, hid), F32)
    tall = jnp.concatenate([v for c in range(9) for v in (w_in[c].astype(F32), pad)], 0)
    w_first[...] = dot(tall.T.astype(BF16), tap_rows()).astype(BF16)
    wide = w_out[...].astype(F32)
    wide = jnp.concatenate([wide, jnp.zeros((16 - wide.shape[0], hid), F32)], 0).astype(BF16)
    wo[...] = dot_nt(chosen, wide).astype(BF16)
    wc[...] = dot_nt(wide, chosen).astype(BF16)


def moved(v, ox, oy, nz, lanes):
    planes = v.shape[1] // lanes
    parts = []
    for x in range(planes):
        at = ((x + ox) % planes) * lanes
        parts.append(ahead_y(v[:, at : at + lanes], oy, nz))
    return parts


def all_taps(g2z, nz, lanes):
    taps = [moved(g2z[0, oz + 1], -ox, -oy, nz, lanes) for ox, oy, oz in offsets]
    return [jnp.concatenate([tap[x] for tap in taps], 0) for x in range(len(taps[0]))]


def closure_kernel(
    nz, lanes, place, feats, w_first, wt, wo, wc, piece, closure, g2z, fcol, fz, eighth, ninth, hidden, sums, mid, last
):
    s = pl.program_id(0)
    samples = pl.num_programs(0)
    slabs = feats.shape[0] // samples
    cells = hidden.shape[1]
    planes = cells // lanes
    per = planes // slabs
    block = wo.shape[0]
    group = 4

    @pl.when(s == 0)
    def _():
        mid[...] = jnp.zeros_like(mid)
        last[...] = jnp.zeros_like(last)

    sums[...] = jnp.zeros_like(sums)
    sub = lax.broadcasted_iota(jnp.int32, (8, lanes), 0)
    for j in range(slabs):
        f = feats[place[j * samples + s]].astype(F32)
        at = slice(j * per * lanes, (j + 1) * per * lanes)
        fz[0, :, at] = roll_z(f, 1, nz)
        fz[1, :, at] = f
        fz[2, :, at] = roll_z(f, -1, nz)
    for x in range(planes):
        at = slice(x * lanes, (x + 1) * lanes)
        rows = [jnp.broadcast_to(fz[oz + 1, 5:6, at], (8, lanes)) for oz in (-1, 0, 1)]
        tile = ahead_y(rows[0], -1, nz)
        for q in range(1, 8):
            tile = jnp.where(sub == q, ahead_y(rows[q % 3], q // 3 - 1, nz), tile)
        eighth[:, at] = tile
        ninth[:, at] = ahead_y(rows[2], 1, nz)

    for x in range(planes):
        at = slice(x * lanes, (x + 1) * lanes)
        near = [slice(((x + ox) % planes) * lanes, ((x + ox) % planes + 1) * lanes) for ox in (-1, 0, 1)]
        pieces = [ahead_y(fz[oz + 1, 8:16, near[ox + 1]], oy, nz) for ox, oy, oz in offsets]
        pieces += [eighth[:, n] for n in near]
        tail = jnp.where(sub == 0, ninth[:, near[0]], jnp.where(sub == 1, ninth[:, near[1]], ninth[:, near[2]]))
        pieces += [jnp.where(sub < 3, tail, 0.0), jnp.zeros((8, lanes), F32)]
        column = jnp.concatenate(pieces, 0).astype(BF16)
        fcol[0, :, at] = column
        pre = dot(w_first[...], column)
        hid = (pre * logistic(pre)).astype(BF16)
        hidden[:, at] = hid
        prod = dot(wt[...], hid)
        for ox in (-1, 0, 1):
            to = near[1 - ox]
            for oz in (-1, 0, 1):
                total = None
                for oy in (-1, 0, 1):
                    t = 9 * (ox + 1) + 3 * (oy + 1) + oz + 1
                    v = ahead_y(prod[t * block : (t + 1) * block], oy, nz)
                    total = v if total is None else total + v
                sums[oz + 1, :, to] += total

    for j in range(slabs):
        here = feats[place[j * samples + s]]
        at = slice(j * per * lanes, (j + 1) * per * lanes)
        pre = sums[1, :, at] + roll_z(sums[0, :, at], 1, nz) + roll_z(sums[2, :, at], -1, nz)
        sig = logistic(pre)
        hid = (pre * sig).astype(BF16)
        out = dot(wc[...], hid)
        for h in range(per):
            for k in range(2):
                start = h * lanes + k * (lanes // 2)
                closure[0, j * per + h, 8 * k : 8 * k + 8] = out[0:8, start : start + lanes // 2].astype(BF16)
        grad = dot(wo[...], here) * (sig * (1.0 + pre * (1.0 - sig)))
        last[...] += dot_nt(here, hid)
        rounded = grad.astype(BF16)
        grad = rounded.astype(F32)
        g2z[0, 0, :, at] = roll_z(grad, -1, nz).astype(BF16)
        g2z[0, 1, :, at] = rounded
        g2z[0, 2, :, at] = roll_z(grad, 1, nz).astype(BF16)

    columns = all_taps(g2z, nz, lanes)
    for x in range(0, planes, group):
        at = slice(x * lanes, (x + group) * lanes)
        mid[...] += dot_nt(jnp.concatenate(columns[x : x + group], 1), hidden[:, at])

    @pl.when(s == samples - 1)
    def _():
        total = mid[...]
        taps = total.shape[0]
        piece[0:taps] = total.astype(BF16)
        squares = jnp.sum(total * total, keepdims=True)
        high = squares.astype(BF16).astype(F32)
        width = total.shape[1]
        row = lax.broadcasted_iota(jnp.int32, (block, width), 0)
        column = lax.broadcasted_iota(jnp.int32, (block, width), 1)
        extra = jnp.concatenate([last[...], jnp.zeros((block, width - block), F32)], 1)
        extra = jnp.where(row < 5, extra, 0.0)
        extra = jnp.where((row == 8) & (column == 0), high, extra)
        extra = jnp.where((row == 8) & (column == 1), squares - high, extra)
        piece[taps:] = extra.astype(BF16)


def first_kernel(nz, lanes, w_first, w_back, fcol, g2z, out):
    @pl.when(pl.program_id(0) == 0)
    def _():
        out[...] = jnp.zeros_like(out)

    columns = all_taps(g2z, nz, lanes)
    group = 2
    for x in range(0, len(columns), group):
        at = slice(x * lanes, (x + group) * lanes)
        back = dot(w_back[...], jnp.concatenate(columns[x : x + group], 1))
        column = fcol[0, :, at]
        pre = dot(w_first[...], column)
        sig = logistic(pre)
        grad = (back * (sig * (1.0 + pre * (1.0 - sig)))).astype(BF16)
        out[...] += dot_nt(column, grad)


def split_kernel(core, one, two, closure, message, keep, kept):
    half = keep.shape[0]
    mine = pl.multiple_of(core[0] * half, half)
    theirs = pl.multiple_of((1 - core[0]) * half, half)
    keep[...] = one[pl.ds(mine, half)] + two[pl.ds(mine, half)]
    message[0:half] = (one[pl.ds(theirs, half)] + two[pl.ds(theirs, half)]).astype(BF16)
    samples, planes = closure.shape[:2]
    at = 0
    for s in range(samples):
        for y in range(planes // 4):
            for p in range(2):
                kept[at : at + 16] = closure[s, 4 * y + 2 * core[0] + p].astype(F32)
                message[half + at : half + at + 16] = closure[s, 4 * y + 2 * (1 - core[0]) + p]
                at += 16


def merge_kernel(bit, got, mine, kept, message, keep):
    half = 128
    message[0:half] = (mine[0:half].astype(F32) + got[0:half].astype(F32)).astype(BF16)
    for o in range(keep.shape[0] // 32):
        a = pl.multiple_of((2 * o + bit[0]) * 32, 32)
        b = pl.multiple_of((2 * o + 1 - bit[0]) * 32, 32)
        keep[o * 32 : o * 32 + 32] = kept[pl.ds(a, 32)] + got[pl.ds(half + a, 32)].astype(F32)
        message[half + o * 32 : half + o * 32 + 32] = (
            kept[pl.ds(b, 32)] + got[pl.ds(half + b, 32)].astype(F32)
        ).astype(BF16)


def total_kernel(got, mine, kept, half, closure):
    half[...] = (mine[0:128].astype(F32) + got[0:128].astype(F32)).astype(BF16)
    closure[...] = kept[...] + got[128:].astype(F32)


def step_kernel(nz, place, fields, drag, closure, feats, out):
    state = flat_cells(fields)
    cells = state.shape[1]
    planes, rows = fields.shape[2], fields.shape[3]
    lanes = cells // planes
    lower = feats[place[0]][8:13, cells - lanes :].astype(F32)
    upper = feats[place[1]][8:13, :lanes].astype(F32)
    wide = jnp.concatenate([lower, state, upper], 1)
    next_x, last_x = wide[:, 2 * lanes :], wide[:, :cells]
    parts = [state[:, i * lanes : (i + 1) * lanes] for i in range(planes)]
    next_y = jnp.concatenate([ahead_y(v, 1, nz) for v in parts], 1)
    last_y = jnp.concatenate([ahead_y(v, -1, nz) for v in parts], 1)
    next_z, last_z = roll_z(state, -1, nz), roll_z(state, 1, nz)
    laplace = next_x + last_x + next_y + last_y + next_z + last_z - 6.0 * state
    advect = -0.5 * (
        state[0:1] * (next_x - last_x) + state[1:2] * (next_y - last_y) + state[2:3] * (next_z - last_z)
    )
    momentum = jnp.concatenate([drag[...], jnp.zeros((2, cells), F32)], 0)
    closed = jnp.concatenate([closure[k : k + 5] for k in range(0, closure.shape[0], 8)], 1)
    new = state + dt_step * (viscosity * laplace + advect + closed + momentum)
    for x in range(planes):
        for y in range(rows):
            at = (x * rows + y) * nz
            out[0, :, x, y, :] = new[:, at : at + nz]


def finish_kernel(count, weight_count, place, core, *refs):
    pieces, (own, other, mid_out, first_out, last_out, held, sems, factor) = refs[:count], refs[count:]
    step = pl.program_id(0)
    taps_here = mid_out.shape[0]
    slots = held.shape[0]
    block = mid_out.shape[1] // slots
    rows = held.shape[1] - 16

    @pl.when(step == 0)
    def _():
        copies, at = [], 0
        for i, ref in enumerate(pieces):
            copies.append(pltpu.make_async_copy(ref, held.at[at : at + ref.shape[0]], sems.at[i]))
            at += ref.shape[0]
        for copy in copies:
            copy.start()
        a, b = own[...].astype(F32), other[...].astype(F32)
        swapped = core[0] == 1
        raw = jnp.concatenate([jnp.where(swapped, b, a), jnp.where(swapped, a, b)], 0)
        squares = jnp.sum(raw * raw, keepdims=True)
        ordered = dot(tap_rows(), raw.astype(BF16))
        for copy in copies:
            copy.wait()
        last = []
        for d in range(slots):
            extra = held[place[d], rows:].astype(F32)
            last.append(extra[0:5, 0:block])
            squares = squares + jnp.sum(extra[8:9, 0:2], keepdims=True)
        last = jnp.concatenate(last, 1)
        squares = squares + jnp.sum(last * last, keepdims=True)
        clip = jnp.minimum(1.0, clip_rms * math.sqrt(weight_count) / jnp.sqrt(squares + 1e-06))
        factor[...] = jnp.broadcast_to(clip, factor.shape)
        last_out[...] = last * clip
        ordered = ordered * clip
        for c in range(first_out.shape[0]):
            first_out[c] = ordered[32 * c : 32 * c + 27]

    width = mid_out.shape[1]
    eye = (
        lax.broadcasted_iota(jnp.int32, (width, width), 0) == lax.broadcasted_iota(jnp.int32, (width, width), 1)
    ).astype(F32).astype(BF16)
    clip = factor[0:1, 0:1]
    for i in range(taps_here):
        start = pl.multiple_of((step * taps_here + i) * block, block)
        flipped = jnp.concatenate([held[place[d], pl.ds(start, block)] for d in range(slots)], 0)
        mid_out[i] = dot_nt(eye, flipped) * clip


def whole_spec(shape):
    return pl.BlockSpec(shape, lambda *unused: (0,) * len(shape))


SMEM = pl.BlockSpec(memory_space=pltpu.SMEM)
VMEM = pl.BlockSpec(memory_space=pltpu.VMEM)
ANY = pl.BlockSpec(memory_space=pl.ANY)


def cost(flops):
    return pl.CostEstimate(flops=int(flops), bytes_accessed=2**22, transcendentals=0)


def params(**more):
    return pltpu.CompilerParams(vmem_limit_bytes=VMEM_BYTES, **more)


def shards(
    fields, drop_mass, drop_vel, drop_cell, cross_list, cross_count, w_in, w_mid, w_out, cotangent
):
    shape = jax.ShapeDtypeStruct
    n_slab, n_rep = lax.axis_size("slab"), lax.axis_size("rep")
    planes, ny, nz = fields.shape[2:]
    cells = planes * ny * nz
    lanes = ny * nz
    hid, cout = w_out.shape
    joined = n_slab * n_rep * 16 <= hid
    team = ("slab", "rep") if joined else ("slab",)
    samples = n_rep if joined else 1
    size = n_slab * samples
    block = hid // size
    fast = joined and n_slab == 4 and n_rep == 4
    slab, rep = lax.axis_index("slab"), lax.axis_index("rep")
    sample = rep if joined else jnp.zeros((), jnp.int32)
    me = slab * samples + sample
    all_planes = n_slab * planes
    everyone = jnp.arange(size, dtype=jnp.int32)

    def trade(v, mask):
        return lax.ppermute(v, team, [(d, d ^ mask) for d in range(size)])

    dense = shape((4, cells), F32)
    stay, up, down = pl.pallas_call(
        deposit_kernel,
        out_shape=(dense, dense, dense),
        in_specs=[VMEM] * 4 + [SMEM],
        out_specs=(VMEM,) * 3,
        compiler_params=params(),
        name="deposit",
    )(drop_mass, jnp.transpose(drop_vel, (1, 0, 2)), drop_cell, cross_list, cross_count)
    from_below = lax.ppermute(up, "slab", [(i, (i + 1) % n_slab) for i in range(n_slab)])
    from_above = lax.ppermute(down, "slab", [((i + 1) % n_slab, i) for i in range(n_slab)])
    own_feats, drag = pl.pallas_call(
        feature_kernel,
        out_shape=(shape((16, cells), BF16), shape((3, cells), F32)),
        in_specs=[VMEM] * 5,
        out_specs=(VMEM,) * 2,
        compiler_params=params(),
        name="features",
    )(stay, from_below, from_above, fields, cotangent)

    if fast:
        order = (8, 2, 1, 4)
        feats = own_feats[None]
        for mask in order:
            feats = jnp.concatenate([feats, trade(feats, mask)], 0)
        apart = me ^ everyone
        feat_place = sum(((apart & mask) != 0).astype(jnp.int32) << i for i, mask in enumerate(order))
    else:
        feats = lax.all_gather(own_feats, team)
        feat_place = everyone

    rows = 27 * block
    wt, w_back, w_first, wo, wc = pl.pallas_call(
        weight_kernel,
        out_shape=(
            shape((rows, hid), BF16),
            shape((hid, rows), BF16),
            shape((hid, 256), BF16),
            shape((block, 16), BF16),
            shape((16, block), BF16),
        ),
        in_specs=[SMEM] + [VMEM] * 3,
        out_specs=(VMEM,) * 5,
        compiler_params=params(),
        cost_estimate=cost(1.5e9),
        name="weights",
    )(me[None], jnp.transpose(w_in, (1, 0, 2)), w_mid, w_out.T)

    team_cells = all_planes * lanes
    piece, closure, g2z, fcol = pl.pallas_call(
        functools.partial(closure_kernel, nz, lanes),
        grid=(samples,),
        out_shape=(
            shape((rows + 16, hid), BF16),
            shape((samples, all_planes, 16, lanes // 2), BF16),
            shape((samples, 3, block, team_cells), BF16),
            shape((samples, 256, team_cells), BF16),
        ),
        in_specs=[SMEM] + [VMEM] * 5,
        out_specs=(
            whole_spec((rows + 16, hid)),
            pl.BlockSpec((1, all_planes, 16, lanes // 2), lambda s: (s, 0, 0, 0)),
            pl.BlockSpec((1, 3, block, team_cells), lambda s: (s, 0, 0, 0)),
            pl.BlockSpec((1, 256, team_cells), lambda s: (s, 0, 0)),
        ),
        scratch_shapes=[
            pltpu.VMEM((3, 16, team_cells), F32),
            pltpu.VMEM((8, team_cells), F32),
            pltpu.VMEM((8, team_cells), F32),
            pltpu.VMEM((hid, team_cells), BF16),
            pltpu.VMEM((3, block, team_cells), F32),
            pltpu.VMEM((rows, hid), F32),
            pltpu.VMEM((16, block), F32),
        ],
        compiler_params=params(),
        cost_estimate=cost(9e9),
        name="closure",
    )(feat_place, feats, w_first, wt, wo, wc)

    def first_part(lo, count, fcol, g2z):
        return pl.pallas_call(
            functools.partial(first_kernel, nz, lanes),
            grid=(count,),
            out_shape=shape((256, hid), F32),
            in_specs=[
                whole_spec((hid, 256)),
                whole_spec((hid, rows)),
                pl.BlockSpec((1, 256, team_cells), lambda s: (s + lo, 0, 0)),
                pl.BlockSpec((1, 3, block, team_cells), lambda s: (s + lo, 0, 0, 0)),
            ],
            out_specs=whole_spec((256, hid)),
            compiler_params=params(),
            cost_estimate=cost(7.6e9 * count / samples),
            name="first",
        )(w_first, w_back, fcol, g2z)

    if fast:
        z = rep
        outer = (z == 0) | (z == 3)

        def line(v, pairs):
            return lax.ppermute(v, "rep", pairs)

        def tie(*values):
            return lax.optimization_barrier(values)

        core, y = slab & 1, slab >> 1
        y0 = trade(piece, 8)
        p1 = line(piece, [(0, 1), (1, 0), (2, 3), (3, 2)])
        p2 = line(piece, [(1, 2), (2, 1)])
        half_one = first_part(0, samples // 2, fcol, g2z)
        y0, p1, p2, half_one, fcol, g2z = tie(y0, p1, p2, half_one, fcol, g2z)
        p4 = line(p2, [(1, 0), (2, 3)])
        p3 = line(p1, [(1, 2), (2, 1)])
        y1 = trade(p1, 8)
        half_two = first_part(samples // 2, samples - samples // 2, fcol, g2z)

        def exchanged(count):
            return (shape((128 + 32 * count, hid), BF16), shape((32 * count, hid), F32))

        message, keep, kept = pl.pallas_call(
            split_kernel,
            out_shape=(exchanged(8)[0], shape((128, hid), F32), exchanged(8)[1]),
            in_specs=[SMEM] + [VMEM] * 3,
            out_specs=(VMEM,) * 3,
            compiler_params=params(),
            name="split",
        )(core[None], half_one, half_two, closure)
        y1, p3, p4, message = tie(y1, p3, p4, message)
        got = trade(message, 4)
        q2 = jnp.where(outer, p4, p2)
        y2 = trade(q2, 8)
        p5 = line(p3, [(1, 0), (2, 3)])
        c0 = trade(jnp.stack([piece, y0, p1, y1]), 4)

        def merge(count, bit, got, mine, kept):
            return pl.pallas_call(
                merge_kernel,
                out_shape=exchanged(count),
                in_specs=[SMEM] + [VMEM] * 3,
                out_specs=(VMEM,) * 2,
                compiler_params=params(),
                name="merge",
            )(bit[None], got, mine, kept)

        message, kept = merge(4, y, got, keep, kept)
        got = trade(message, 8)
        y2, p5, c0, got = tie(y2, p5, c0, got)
        q3 = jnp.where(outer, p5, p3)
        y3 = trade(q3, 8)
        c1 = trade(jnp.stack([q2, y2, q3]), 4)
        message, kept = merge(2, z & 1, got, message, kept)
        got = trade(message, 1)
        message, kept = merge(1, z >> 1, got, message, kept)
        got = trade(message, 2)
        own, own_closure = pl.pallas_call(
            total_kernel,
            out_shape=(shape((128, hid), BF16), shape((32, hid), F32)),
            in_specs=[VMEM] * 3,
            out_specs=(VMEM,) * 2,
            compiler_params=params(),
            name="total",
        )(got, message, kept)
        other = trade(own, 4)
        c2 = trade(y3, 4)
        pieces = [v[None] for v in (piece, y0, p1, y1, q2, y2, q3, y3)] + [c0, c1, c2[None]]
        m2 = jnp.where(outer, 2, 3)
        masks = jnp.stack([jnp.int32(0), jnp.int32(8), jnp.int32(1), jnp.int32(9), m2, m2 | 8, m2 ^ 1, (m2 ^ 1) | 8])
        masks = jnp.concatenate([masks, masks | 4])
        piece_place = jnp.argmax((me ^ everyone)[:, None] == masks[None, :], axis=1).astype(jnp.int32)
    else:
        raw_first = first_part(0, samples, fcol, g2z)
        core = jnp.zeros((), jnp.int32)
        if not joined:
            raw_first = lax.psum(raw_first, "rep")
            body = lax.psum(piece[:rows].astype(F32), "rep")
            extra = lax.psum(piece[rows:].astype(F32), "rep")
            squares = jnp.sum(body * body)
            high = squares.astype(BF16).astype(F32)
            extra = extra.at[8, 0].set(high).at[8, 1].set(squares - high)
            piece = jnp.concatenate([body, extra], 0).astype(BF16)
        raw_first = lax.psum(raw_first, team).astype(BF16)
        own, other = raw_first[:128], raw_first[128:]
        pieces = [lax.all_gather(piece, team)]
        piece_place = everyone
        part = closure.reshape(samples, n_slab, planes * 16, lanes // 2)
        part = jnp.swapaxes(part, 0, 1).reshape(size, planes * 16, lanes // 2).astype(F32)
        own_closure = lax.psum_scatter(part, team, scatter_dimension=0)

    near = jnp.stack([(slab + n_slab - 1) % n_slab, (slab + 1) % n_slab]) * samples + sample
    new_fields = pl.pallas_call(
        functools.partial(step_kernel, nz),
        out_shape=shape(fields.shape, F32),
        in_specs=[SMEM] + [VMEM] * 4,
        out_specs=VMEM,
        compiler_params=params(),
        name="step",
    )(jnp.take(feat_place, near), fields, drag, own_closure, feats)

    weight_count = w_in.size + w_mid.size + w_out.size
    step_taps = 3
    grad_middle, grad_first, grad_last = pl.pallas_call(
        functools.partial(finish_kernel, len(pieces), weight_count),
        grid=(27 // step_taps,),
        out_shape=(shape((27, hid, hid), F32), shape((9, 27, hid), F32), shape((cout, hid), F32)),
        in_specs=[SMEM] * 2 + [ANY] * len(pieces) + [whole_spec((128, hid))] * 2,
        out_specs=(
            pl.BlockSpec((step_taps, hid, hid), lambda i: (i, 0, 0)),
            whole_spec((9, 27, hid)),
            whole_spec((cout, hid)),
        ),
        scratch_shapes=[
            pltpu.VMEM((size, rows + 16, hid), BF16),
            pltpu.SemaphoreType.DMA((len(pieces),)),
            pltpu.VMEM((8, 128), F32),
        ],
        compiler_params=params(),
        name="finish",
    )(piece_place, core[None], *pieces, own, other)
    return (new_fields, jnp.transpose(grad_first, (1, 0, 2)), grad_middle, grad_last.T)


def solution(mesh):
    placed = (
        P(("groups", "rep"), None, "slab", None, None),
        P(("groups", "rep"), "slab"),
        P(("groups", "rep"), None, "slab"),
        P(("groups", "rep"), "slab"),
        P(("groups", "rep"), "slab"),
        P(("groups", "rep"), "slab"),
        P(),
        P(),
        P(),
        P(("groups", "rep"), None, "slab", None, None),
    )
    return jax.shard_map(
        shards,
        mesh=mesh,
        in_specs=placed,
        out_specs=(
            P(("groups", "rep"), None, "slab", None, None),
            P("groups", None, None),
            P("groups", None, None),
            P("groups", None),
        ),
        check_vma=False,
    )
```

```python
import functools
import math

import jax
import jax.numpy as jnp
from jax import lax
from jax.experimental import pallas as pl
from jax.experimental.pallas import tpu as pltpu
from jax.sharding import PartitionSpec as P

dt_step = 0.2
viscosity = 0.05
drag_rate = 0.5
clip_rms = 0.5

F32 = jnp.float32
BF16 = jnp.bfloat16
VMEM_BYTES = 58 * 2**20
offsets = [(x, y, z) for x in (-1, 0, 1) for y in (-1, 0, 1) for z in (-1, 0, 1)]


def dot(a, b):
    return lax.dot_general(a, b, (((1,), (0,)), ((), ())), preferred_element_type=F32)


def dot_nt(a, b):
    return lax.dot_general(a, b, (((1,), (1,)), ((), ())), preferred_element_type=F32)


def logistic(p):
    return 0.5 * jnp.tanh(0.5 * p) + 0.5


def roll_z(v, by, nz):
    return jnp.concatenate(
        [pltpu.roll(v[:, k : k + nz], by % nz, 1) for k in range(0, v.shape[1], nz)], 1
    )


def ahead_y(v, by, nz):
    if by == 0:
        return v
    cut = (by * nz) % v.shape[1]
    return jnp.concatenate([v[:, cut:], v[:, :cut]], 1)


def flat_cells(ref):
    planes, rows = ref.shape[2], ref.shape[3]
    return jnp.concatenate([ref[0, :, x, y, :] for x in range(planes) for y in range(rows)], 1)


def deposit_kernel(mass, vel, cell, listed, counts, stay, up, down):
    drops = mass.shape[1]
    slots = listed.shape[1]
    half = slots // 2
    k = lax.broadcasted_iota(jnp.int32, (1, slots), 1)
    valid = k < jnp.where(k < half, counts[0, 0], half + counts[0, 1])
    chosen = jnp.where(valid, listed[...], -1)
    member = (lax.broadcasted_iota(jnp.int32, (drops, slots), 0) == chosen).astype(F32).astype(BF16)
    row = lax.broadcasted_iota(jnp.int32, (16, slots), 0)
    column = lax.broadcasted_iota(jnp.int32, (16, slots), 1)
    which = (row == (column >= half).astype(jnp.int32)).astype(F32).astype(BF16)
    mask = dot_nt(which, member)
    goes_up, goes_down = mask[0:1], mask[1:2]
    m = mass[...]
    charges = jnp.concatenate([m] + [m * vel[i] for i in range(vel.shape[0])], 0)
    high = charges.astype(BF16).astype(F32)
    both = jnp.concatenate([high, charges - high], 0)
    rows = jnp.concatenate(
        [both * (1.0 - goes_up - goes_down), both * goes_up, both * goes_down, jnp.zeros_like(both)], 0
    ).astype(BF16)
    chunk = 256
    for start in range(0, stay.shape[1], chunk):
        here = lax.broadcasted_iota(jnp.int32, (chunk, drops), 0) + start
        onehot = (here == cell[...]).astype(F32).astype(BF16)
        got = dot_nt(rows, onehot)
        for i, out in enumerate((stay, up, down)):
            out[:, start : start + chunk] = got[8 * i : 8 * i + 4] + got[8 * i + 4 : 8 * i + 8]


def feature_kernel(stay, below, above, fields, cotangent, feats, drag):
    deposit = stay[...] + below[...] + above[...]
    state = flat_cells(fields)
    force = drag_rate * (deposit[1:4] - deposit[0:1] * state[0:3])
    drag[...] = force
    cells = state.shape[1]
    feats[...] = jnp.concatenate(
        [
            dt_step * flat_cells(cotangent),
            force[2:3],
            jnp.zeros((2, cells), F32),
            state,
            deposit[0:1],
            force[0:2],
        ],
        0,
    ).astype(BF16)


def tap_rows():
    r = lax.broadcasted_iota(jnp.int32, (288, 256), 0)
    k = lax.broadcasted_iota(jnp.int32, (288, 256), 1)
    c, t = r >> 5, r & 31
    ox = (t >= 9).astype(jnp.int32) + (t >= 18).astype(jnp.int32)
    q = t - 9 * ox
    ninth = jnp.where(q < 8, 216 + 8 * ox + q, 240 + ox)
    at = jnp.where(c < 8, 8 * t + c, ninth)
    return ((at == k) & (t < 27)).astype(F32).astype(BF16)


def weight_kernel(me, w_in, w_mid, w_out, wt, w_back, w_first, wo, wc):
    block, hid = wo.shape[0], wt.shape[1]
    row = lax.broadcasted_iota(jnp.int32, (block, hid), 0)
    column = lax.broadcasted_iota(jnp.int32, (block, hid), 1)
    chosen = (column == row + me[0] * block).astype(F32).astype(BF16)
    for t in range(27):
        wt[t * block : (t + 1) * block] = dot_nt(chosen, w_mid[t]).astype(BF16)
    w_back[...] = wt[...].astype(F32).T.astype(BF16)
    pad = jnp.zeros((5, hid), F32)
    tall = jnp.concatenate([v for c in range(9) for v in (w_in[c].astype(F32), pad)], 0)
    w_first[...] = (0.5 * dot(tall.T.astype(BF16), tap_rows())).astype(BF16)
    wide = w_out[...].astype(F32)
    wide = jnp.concatenate([wide, jnp.zeros((16 - wide.shape[0], hid), F32)], 0).astype(BF16)
    wo[...] = dot_nt(chosen, wide).astype(BF16)
    wc[...] = dot_nt(wide, chosen).astype(BF16)


def span(x, lanes, count=1):
    return slice(x * lanes, (x + count) * lanes)


def plane_taps(g2z, x, planes, nz, lanes):
    parts = []
    for ox, oy, oz in offsets:
        parts.append(ahead_y(g2z[0, oz + 1, :, span((x - ox) % planes, lanes)], -oy, nz))
    return jnp.concatenate(parts, 0)


def closure_kernel(nz, lanes, sources, place, w_first, wt, wo, wc, *refs):
    arrived, refs = refs[:sources], refs[sources:]
    piece, closure, g2z, fcol, feats, fz, eighth, ninth, hidden, sums, mid, last = refs
    s = pl.program_id(0)
    samples = pl.num_programs(0)
    slabs = place.shape[0]
    cells = hidden.shape[1]
    planes = cells // lanes
    per = planes // slabs
    block = wo.shape[0]
    group = 4

    @pl.when(s == 0)
    def _():
        mid[...] = jnp.zeros_like(mid)
        last[...] = jnp.zeros_like(last)
        at = 0
        for ref in arrived:
            feats[at : at + ref.shape[0]] = ref[...]
            at += ref.shape[0]

    sums[...] = jnp.zeros_like(sums)
    sub = lax.broadcasted_iota(jnp.int32, (8, lanes), 0)

    def spread(j):
        f = feats[place[j] + s].astype(F32)
        at = span(j, per * lanes)
        fz[0, :, at] = roll_z(f, 1, nz)
        fz[1, :, at] = f
        fz[2, :, at] = roll_z(f, -1, nz)

    for j in range(slabs):
        spread(j)

    def around(x):
        return [span((x + ox) % planes, lanes) for ox in (-1, 0, 1)]

    def ninth_rows(x):
        at = span(x, lanes)
        rows = [jnp.broadcast_to(fz[oz + 1, 5:6, at], (8, lanes)) for oz in (-1, 0, 1)]
        tile = ahead_y(rows[0], -1, nz)
        for q in range(1, 8):
            tile = jnp.where(sub == q, ahead_y(rows[q % 3], q // 3 - 1, nz), tile)
        eighth[:, at] = tile
        ninth[:, at] = ahead_y(rows[2], 1, nz)

    for x in range(planes):
        ninth_rows(x)

    def patches(x):
        near = around(x)
        pieces = [ahead_y(fz[oz + 1, 8:16, near[ox + 1]], oy, nz) for ox, oy, oz in offsets]
        pieces += [eighth[:, n] for n in near]
        tail = jnp.where(sub == 0, ninth[:, near[0]], jnp.where(sub == 1, ninth[:, near[1]], ninth[:, near[2]]))
        pieces += [jnp.where(sub < 3, tail, 0.0), jnp.zeros((8, lanes), F32)]
        fcol[0, :, near[1]] = jnp.concatenate(pieces, 0).astype(BF16)

    for x in range(planes):
        patches(x)

    def first(x):
        at = span(x, lanes)
        half = dot(w_first[...], fcol[0, :, at])
        hidden[:, at] = (half * jnp.tanh(half) + half).astype(BF16)

    for x in range(planes):
        first(x)

    def second(x):
        near = around(x)
        prod = dot(wt[...], hidden[:, near[1]])
        for ox in (-1, 0, 1):
            to = near[1 - ox]
            for oz in (-1, 0, 1):
                total = None
                for oy in (-1, 0, 1):
                    t = 9 * (ox + 1) + 3 * (oy + 1) + oz + 1
                    v = ahead_y(prod[t * block : (t + 1) * block], oy, nz)
                    total = v if total is None else total + v
                sums[oz + 1, :, to] += total

    for x in range(planes):
        second(x)

    def gradient(j):
        here = feats[place[j] + s]
        at = span(j, per * lanes)
        pre = sums[1, :, at] + roll_z(sums[0, :, at], 1, nz) + roll_z(sums[2, :, at], -1, nz)
        sig = logistic(pre)
        hid = (pre * sig).astype(BF16)
        out = dot(wc[...], hid)
        for h in range(per):
            for k in range(2):
                start = h * lanes + k * (lanes // 2)
                closure[0, j * per + h, 8 * k : 8 * k + 8] = out[0:8, start : start + lanes // 2].astype(BF16)
        grad = dot(wo[...], here) * (sig * (1.0 + pre * (1.0 - sig)))
        last[...] += dot_nt(here, hid)
        rounded = grad.astype(BF16)
        grad = rounded.astype(F32)
        g2z[0, 0, :, at] = roll_z(grad, -1, nz).astype(BF16)
        g2z[0, 1, :, at] = rounded
        g2z[0, 2, :, at] = roll_z(grad, 1, nz).astype(BF16)

    for j in range(slabs):
        gradient(j)

    @pl.when(s >= 0)
    def _():
        for x in range(0, planes, group):
            columns = [plane_taps(g2z, x + h, planes, nz, lanes) for h in range(group)]
            mid[...] += dot_nt(jnp.concatenate(columns, 1), hidden[:, span(x, lanes, group)])

    @pl.when(s == samples - 1)
    def _():
        total = mid[...]
        taps = total.shape[0]
        piece[0:taps] = total.astype(BF16)
        squares = jnp.sum(total * total, keepdims=True)
        high = squares.astype(BF16).astype(F32)
        width = total.shape[1]
        row = lax.broadcasted_iota(jnp.int32, (block, width), 0)
        column = lax.broadcasted_iota(jnp.int32, (block, width), 1)
        extra = jnp.concatenate([last[...], jnp.zeros((block, width - block), F32)], 1)
        extra = jnp.where(row < 5, extra, 0.0)
        extra = jnp.where((row == 8) & (column == 0), high, extra)
        extra = jnp.where((row == 8) & (column == 1), squares - high, extra)
        piece[taps:] = extra.astype(BF16)


def first_kernel(nz, lanes, w_first, w_back, fcol, g2z, out):
    @pl.when(pl.program_id(0) == 0)
    def _():
        out[...] = jnp.zeros_like(out)

    planes = fcol.shape[2] // lanes
    group = 2
    for x in range(0, planes, group):
        at = span(x, lanes, group)
        columns = [plane_taps(g2z, x + h, planes, nz, lanes) for h in range(group)]
        back = dot(w_back[...], jnp.concatenate(columns, 1))
        column = fcol[0, :, at]
        half = dot(w_first[...], column)
        double = 1.0 + jnp.tanh(half)
        grad = (back * (double * (0.5 + half - 0.5 * half * double))).astype(BF16)
        out[...] += dot_nt(column, grad)


def split_kernel(core, one, two, closure, message, keep, kept):
    half = keep.shape[0]
    mine = pl.multiple_of(core[0] * half, half)
    theirs = pl.multiple_of((1 - core[0]) * half, half)
    keep[...] = one[pl.ds(mine, half)] + two[pl.ds(mine, half)]
    message[0:half] = one[pl.ds(theirs, half)] + two[pl.ds(theirs, half)]
    samples, planes = closure.shape[:2]
    at = 0
    for s in range(samples):
        for y in range(planes // 4):
            for p in range(2):
                kept[at : at + 16] = closure[s, 4 * y + 2 * core[0] + p].astype(F32)
                message[half + at : half + at + 16] = closure[s, 4 * y + 2 * (1 - core[0]) + p].astype(F32)
                at += 16


def merge_kernel(bit, got, mine, kept, message, keep):
    half = 128
    message[0:half] = (mine[...] + got[0:half]).astype(BF16)
    for o in range(keep.shape[0] // 32):
        a = pl.multiple_of((2 * o + bit[0]) * 32, 32)
        b = pl.multiple_of((2 * o + 1 - bit[0]) * 32, 32)
        keep[o * 32 : o * 32 + 32] = kept[pl.ds(a, 32)] + got[pl.ds(half + a, 32)]
        message[half + o * 32 : half + o * 32 + 32] = (kept[pl.ds(b, 32)] + got[pl.ds(half + b, 32)]).astype(BF16)


def fan_kernel(got, mine, kept, keep, *messages):
    half = 128
    raw = (mine[0:half].astype(F32) + got[0:half].astype(F32)).astype(BF16)
    for o in range(4):
        rows = kept[o * 32 : o * 32 + 32] + got[half + o * 32 : half + o * 32 + 32].astype(F32)
        if o == 0:
            keep[...] = rows
        else:
            messages[o - 1][0:half] = raw
            messages[o - 1][half:] = rows.astype(BF16)


def total_kernel(mine, kept, one, two, three, half, closure):
    pair = mine[0:128].astype(F32) + one[0:128].astype(F32)
    half[...] = pair + (two[0:128].astype(F32) + three[0:128].astype(F32))
    closure[...] = kept[...] + (one[128:].astype(F32) + two[128:].astype(F32) + three[128:].astype(F32))


def step_kernel(nz, place, fields, drag, closure, *refs):
    sources, out = refs[:-1], refs[-1]
    state = flat_cells(fields)
    cells = state.shape[1]
    planes, rows = fields.shape[2], fields.shape[3]
    lanes = cells // planes
    lower, upper = (sources[0][place[i] if len(sources) == 1 else 0].astype(F32) for i in range(2))
    for g in range(1, len(sources)):
        other = sources[g][0].astype(F32)
        lower, upper = (jnp.where(place[i] == g, other, v) for i, v in enumerate((lower, upper)))
    lower, upper = lower[8:13, cells - lanes :], upper[8:13, :lanes]
    wide = jnp.concatenate([lower, state, upper], 1)
    next_x, last_x = wide[:, 2 * lanes :], wide[:, :cells]
    parts = [state[:, i * lanes : (i + 1) * lanes] for i in range(planes)]
    next_y = jnp.concatenate([ahead_y(v, 1, nz) for v in parts], 1)
    last_y = jnp.concatenate([ahead_y(v, -1, nz) for v in parts], 1)
    next_z, last_z = roll_z(state, -1, nz), roll_z(state, 1, nz)
    laplace = next_x + last_x + next_y + last_y + next_z + last_z - 6.0 * state
    advect = -0.5 * (
        state[0:1] * (next_x - last_x) + state[1:2] * (next_y - last_y) + state[2:3] * (next_z - last_z)
    )
    momentum = jnp.concatenate([drag[...], jnp.zeros((2, cells), F32)], 0)
    closed = jnp.concatenate([closure[k : k + 5] for k in range(0, closure.shape[0], 8)], 1)
    new = state + dt_step * (viscosity * laplace + advect + closed + momentum)
    for x in range(planes):
        for y in range(rows):
            at = (x * rows + y) * nz
            out[0, :, x, y, :] = new[:, at : at + nz]


def finish_kernel(count, weight_count, place, core, own, other, *refs):
    pieces, (mid_out, first_out, last_out, held, done, arrive, leave) = refs[:count], refs[count:]
    slots = held.shape[0]
    block = done.shape[1] // slots
    rows = held.shape[1] - 16
    width = done.shape[1]

    copies, at = [], 0
    for i, ref in enumerate(pieces):
        copies.append(pltpu.make_async_copy(ref, held.at[at : at + ref.shape[0]], arrive.at[i]))
        at += ref.shape[0]
    for copy in copies:
        copy.start()
    a, b = own[...], other[...]
    swapped = core[0] == 1
    raw = jnp.concatenate([jnp.where(swapped, b, a), jnp.where(swapped, a, b)], 0)
    squares = jnp.sum(raw * raw, keepdims=True)
    high = raw.astype(BF16)
    ordered = dot(tap_rows(), high) + dot(tap_rows(), (raw - high.astype(F32)).astype(BF16))
    for copy in copies:
        copy.wait()
    last = []
    for d in range(slots):
        extra = held[place[d], rows:].astype(F32)
        last.append(extra[0:5, 0:block])
        squares = squares + jnp.sum(extra[8:9, 0:2], keepdims=True)
    last = jnp.concatenate(last, 1)
    squares = squares + jnp.sum(last * last, keepdims=True)
    clip = jnp.minimum(1.0, clip_rms * math.sqrt(weight_count) / jnp.sqrt(squares + 1e-06))
    last_out[...] = last * clip
    ordered = ordered * clip
    for c in range(first_out.shape[0]):
        first_out[c] = ordered[32 * c : 32 * c + 27]

    eye = (
        lax.broadcasted_iota(jnp.int32, (width, width), 0) == lax.broadcasted_iota(jnp.int32, (width, width), 1)
    ).astype(F32).astype(BF16)

    def leaving(t):
        return pltpu.make_async_copy(done.at[t], mid_out.at[t], leave.at[t])

    def flip(i, carry):
        for k in range(3):
            t = 3 * i + k
            start = pl.multiple_of(t * block, block)
            flipped = jnp.concatenate([held[place[d], pl.ds(start, block)] for d in range(slots)], 0)
            done[t] = dot_nt(eye, flipped) * clip
            leaving(t).start()
        return carry

    lax.fori_loop(0, 9, flip, 0)
    for t in range(27):
        leaving(t).wait()


def whole_spec(shape):
    return pl.BlockSpec(shape, lambda *unused: (0,) * len(shape))


SMEM = pl.BlockSpec(memory_space=pltpu.SMEM)
VMEM = pl.BlockSpec(memory_space=pltpu.VMEM)
ANY = pl.BlockSpec(memory_space=pl.ANY)


def cost(flops):
    return pl.CostEstimate(flops=int(flops), bytes_accessed=2**22, transcendentals=0)


def params(**more):
    return pltpu.CompilerParams(vmem_limit_bytes=VMEM_BYTES, **more)


def shards(
    fields, drop_mass, drop_vel, drop_cell, cross_list, cross_count, w_in, w_mid, w_out, cotangent
):
    shape = jax.ShapeDtypeStruct
    n_slab, n_rep = lax.axis_size("slab"), lax.axis_size("rep")
    planes, ny, nz = fields.shape[2:]
    cells = planes * ny * nz
    lanes = ny * nz
    hid, cout = w_out.shape
    joined = n_slab * n_rep * 16 <= hid
    team = ("slab", "rep") if joined else ("slab",)
    samples = n_rep if joined else 1
    size = n_slab * samples
    block = hid // size
    fast = joined and n_slab == 4 and n_rep == 4
    slab, rep = lax.axis_index("slab"), lax.axis_index("rep")
    sample = rep if joined else jnp.zeros((), jnp.int32)
    me = slab * samples + sample
    all_planes = n_slab * planes
    everyone = jnp.arange(size, dtype=jnp.int32)

    def trade(v, mask):
        return lax.ppermute(v, team, [(d, d ^ mask) for d in range(size)])

    dense = shape((4, cells), F32)
    stay, up, down = pl.pallas_call(
        deposit_kernel,
        out_shape=(dense, dense, dense),
        in_specs=[VMEM] * 4 + [SMEM],
        out_specs=(VMEM,) * 3,
        compiler_params=params(),
        name="deposit",
    )(drop_mass, jnp.transpose(drop_vel, (1, 0, 2)), drop_cell, cross_list, cross_count)
    from_below = lax.ppermute(up, "slab", [(i, (i + 1) % n_slab) for i in range(n_slab)])
    from_above = lax.ppermute(down, "slab", [((i + 1) % n_slab, i) for i in range(n_slab)])
    own_feats, drag = pl.pallas_call(
        feature_kernel,
        out_shape=(shape((16, cells), BF16), shape((3, cells), F32)),
        in_specs=[VMEM] * 5,
        out_specs=(VMEM,) * 2,
        compiler_params=params(),
        name="features",
    )(stay, from_below, from_above, fields, cotangent)

    if fast:
        near_z = [trade(own_feats, mask) for mask in (1, 2, 3)]
        mine = jnp.stack([own_feats] + near_z)
        across = trade(mine, 8)
        sources = [mine, across, trade(mine, 4), trade(across, 4)]
        slabs = jnp.arange(n_slab, dtype=jnp.int32)
        group = 2 * ((slabs ^ slab) & 1) + (((slabs ^ slab) >> 1) & 1)
        place = group * samples
    else:
        sources = [lax.all_gather(own_feats, team)]
        group = jnp.arange(n_slab, dtype=jnp.int32)
        place = group * samples

    rows = 27 * block
    wt, w_back, w_first, wo, wc = pl.pallas_call(
        weight_kernel,
        out_shape=(
            shape((rows, hid), BF16),
            shape((hid, rows), BF16),
            shape((hid, 256), BF16),
            shape((block, 16), BF16),
            shape((16, block), BF16),
        ),
        in_specs=[SMEM] + [VMEM] * 3,
        out_specs=(VMEM,) * 5,
        compiler_params=params(),
        cost_estimate=cost(1.5e9),
        name="weights",
    )(me[None], jnp.transpose(w_in, (1, 0, 2)), w_mid, w_out.T)

    team_cells = all_planes * lanes
    piece, closure, g2z, fcol = pl.pallas_call(
        functools.partial(closure_kernel, nz, lanes, len(sources)),
        grid=(samples,),
        out_shape=(
            shape((rows + 16, hid), BF16),
            shape((samples, all_planes, 16, lanes // 2), BF16),
            shape((samples, 3, block, team_cells), BF16),
            shape((samples, 256, team_cells), BF16),
        ),
        in_specs=[SMEM] + [VMEM] * (4 + len(sources)),
        out_specs=(
            whole_spec((rows + 16, hid)),
            pl.BlockSpec((1, all_planes, 16, lanes // 2), lambda s: (s, 0, 0, 0)),
            pl.BlockSpec((1, 3, block, team_cells), lambda s: (s, 0, 0, 0)),
            pl.BlockSpec((1, 256, team_cells), lambda s: (s, 0, 0)),
        ),
        scratch_shapes=[
            pltpu.VMEM((size, 16, cells), BF16),
            pltpu.VMEM((3, 16, team_cells), F32),
            pltpu.VMEM((8, team_cells), F32),
            pltpu.VMEM((8, team_cells), F32),
            pltpu.VMEM((hid, team_cells), BF16),
            pltpu.VMEM((3, block, team_cells), F32),
            pltpu.VMEM((rows, hid), F32),
            pltpu.VMEM((16, block), F32),
        ],
        compiler_params=params(),
        cost_estimate=cost(9e9),
        name="closure",
    )(place, w_first, wt, wo, wc, *sources)

    def first_part(lo, count, fcol, g2z):
        return pl.pallas_call(
            functools.partial(first_kernel, nz, lanes),
            grid=(count,),
            out_shape=shape((256, hid), F32),
            in_specs=[
                whole_spec((hid, 256)),
                whole_spec((hid, rows)),
                pl.BlockSpec((1, 256, team_cells), lambda s: (s + lo, 0, 0)),
                pl.BlockSpec((1, 3, block, team_cells), lambda s: (s + lo, 0, 0, 0)),
            ],
            out_specs=whole_spec((256, hid)),
            compiler_params=params(),
            cost_estimate=cost(7.6e9 * count / samples),
            name="first",
        )(w_first, w_back, fcol, g2z)

    if fast:
        core, y = slab & 1, slab >> 1

        def chip(at):
            at = at % 8
            return (0, at) if at < 4 else (1, 7 - at)

        def device(at, c):
            y, z = chip(at)
            return (2 * y + c) * n_rep + z

        def around(v, by):
            return lax.ppermute(v, team, [(device(at, c), device(at + by, c)) for at in range(8) for c in range(2)])

        def tie(*values):
            return lax.optimization_barrier(values)

        f1, b1 = around(piece, 1), around(piece, -1)
        half_one = first_part(0, samples // 2, fcol, g2z)
        f1, b1, half_one, fcol, g2z = tie(f1, b1, half_one, fcol, g2z)
        f2, b2 = around(f1, 1), around(b1, -1)
        half_two = first_part(samples // 2, samples - samples // 2, fcol, g2z)
        f2, b2, half_two = tie(f2, b2, half_two)
        f3, b3 = around(f2, 1), around(b2, -1)

        message, keep, kept = pl.pallas_call(
            split_kernel,
            out_shape=(shape((384, hid), F32), shape((128, hid), F32), shape((256, hid), F32)),
            in_specs=[SMEM] + [VMEM] * 3,
            out_specs=(VMEM,) * 3,
            compiler_params=params(),
            name="split",
        )(core[None], half_one, half_two, closure)
        got = trade(message, 4)
        message, kept = pl.pallas_call(
            merge_kernel,
            out_shape=(shape((256, hid), BF16), shape((128, hid), F32)),
            in_specs=[SMEM] + [VMEM] * 3,
            out_specs=(VMEM,) * 2,
            compiler_params=params(),
            name="merge",
        )(y[None], got, keep, kept)
        got = trade(message, 8)
        kept, *messages = pl.pallas_call(
            fan_kernel,
            out_shape=(shape((32, hid), F32),) + (shape((160, hid), BF16),) * 3,
            in_specs=[VMEM] * 3,
            out_specs=(VMEM,) * 4,
            compiler_params=params(),
            name="fan",
        )(got, message, kept)
        got = [trade(message, mask) for mask, message in zip((1, 2, 3), messages)]
        f4 = around(f3, 1)
        own, own_closure = pl.pallas_call(
            total_kernel,
            out_shape=(shape((128, hid), F32), shape((32, hid), F32)),
            in_specs=[VMEM] * 5,
            out_specs=(VMEM,) * 2,
            compiler_params=params(),
            name="total",
        )(messages[0], kept, *got)
        other = trade(own, 4)
        pieces = [piece, f1, b1, f2, b2, f3, b3, f4]
        pieces = [v[None] for v in pieces + [trade(v, 4) for v in pieces]]
        position = jnp.where(y == 0, rep, 7 - rep)
        theirs, their_z = everyone // n_rep, everyone % n_rep
        apart = (jnp.where(theirs < 2, their_z, 7 - their_z) - position) % 8
        piece_place = jnp.where(apart < 4, 2 * apart, 2 * (8 - apart) - 1)
        piece_place = jnp.where(apart == 0, 0, piece_place) + 8 * ((theirs ^ slab) & 1)
        piece_place = piece_place.astype(jnp.int32)
    else:
        raw_first = first_part(0, samples, fcol, g2z)
        core = jnp.zeros((), jnp.int32)
        if not joined:
            raw_first = lax.psum(raw_first, "rep")
            body = lax.psum(piece[:rows].astype(F32), "rep")
            extra = lax.psum(piece[rows:].astype(F32), "rep")
            squares = jnp.sum(body * body)
            high = squares.astype(BF16).astype(F32)
            extra = extra.at[8, 0].set(high).at[8, 1].set(squares - high)
            piece = jnp.concatenate([body, extra], 0).astype(BF16)
        raw_first = lax.psum(raw_first, team)
        own, other = raw_first[:128], raw_first[128:]
        pieces = [lax.all_gather(piece, team)]
        piece_place = everyone
        part = closure.reshape(samples, n_slab, planes * 16, lanes // 2)
        part = jnp.swapaxes(part, 0, 1).reshape(size, planes * 16, lanes // 2).astype(F32)
        own_closure = lax.psum_scatter(part, team, scatter_dimension=0)

    near = jnp.take(group, jnp.stack([(slab + n_slab - 1) % n_slab, (slab + 1) % n_slab]))
    halo = sources if fast else [sources[0].reshape(n_slab, samples, 16, cells)[:, sample]]
    new_fields = pl.pallas_call(
        functools.partial(step_kernel, nz),
        out_shape=shape(fields.shape, F32),
        in_specs=[SMEM] + [VMEM] * (3 + len(halo)),
        out_specs=VMEM,
        compiler_params=params(),
        name="step",
    )(near, fields, drag, own_closure, *halo)

    weight_count = w_in.size + w_mid.size + w_out.size
    grad_middle, grad_first, grad_last = pl.pallas_call(
        functools.partial(finish_kernel, len(pieces), weight_count),
        out_shape=(shape((27, hid, hid), F32), shape((9, 27, hid), F32), shape((cout, hid), F32)),
        in_specs=[SMEM] * 2 + [VMEM] * 2 + [ANY] * len(pieces),
        out_specs=(ANY, VMEM, VMEM),
        scratch_shapes=[
            pltpu.VMEM((size, rows + 16, hid), BF16),
            pltpu.VMEM((27, hid, hid), F32),
            pltpu.SemaphoreType.DMA((len(pieces),)),
            pltpu.SemaphoreType.DMA((27,)),
        ],
        compiler_params=params(),
        name="finish",
    )(piece_place, core[None], own, other, *pieces)
    return (new_fields, jnp.transpose(grad_first, (1, 0, 2)), grad_middle, grad_last.T)


def solution(mesh):
    placed = (
        P(("groups", "rep"), None, "slab", None, None),
        P(("groups", "rep"), "slab"),
        P(("groups", "rep"), None, "slab"),
        P(("groups", "rep"), "slab"),
        P(("groups", "rep"), "slab"),
        P(("groups", "rep"), "slab"),
        P(),
        P(),
        P(),
        P(("groups", "rep"), None, "slab", None, None),
    )
    return jax.shard_map(
        shards,
        mesh=mesh,
        in_specs=placed,
        out_specs=(
            P(("groups", "rep"), None, "slab", None, None),
            P("groups", None, None),
            P("groups", None, None),
            P("groups", None),
        ),
        check_vma=False,
    )
```

```python
import functools
import math

import jax
import jax.numpy as jnp
from jax import lax
from jax.experimental import pallas as pl
from jax.experimental.pallas import tpu as pltpu
from jax.sharding import PartitionSpec as P

dt_step = 0.2
viscosity = 0.05
drag_rate = 0.5
clip_rms = 0.5

F32 = jnp.float32
BF16 = jnp.bfloat16
offsets = [(x, y, z) for x in (-1, 0, 1) for y in (-1, 0, 1) for z in (-1, 0, 1)]


def dot(a, b):
    return lax.dot_general(a, b, (((1,), (0,)), ((), ())), preferred_element_type=F32)


def dot_nt(a, b):
    return lax.dot_general(a, b, (((1,), (1,)), ((), ())), preferred_element_type=F32)


def logistic(p):
    return 0.5 * jnp.tanh(0.5 * p) + 0.5


def roll_z(v, by, nz):
    return jnp.concatenate(
        [pltpu.roll(v[:, k : k + nz], by % nz, 1) for k in range(0, v.shape[1], nz)], 1
    )


def ahead_y(v, by, nz):
    if by == 0:
        return v
    cut = (by * nz) % v.shape[1]
    return jnp.concatenate([v[:, cut:], v[:, :cut]], 1)


def flat_cells(ref):
    planes, rows = ref.shape[2], ref.shape[3]
    return jnp.concatenate([ref[0, :, x, y, :] for x in range(planes) for y in range(rows)], 1)


def deposit_kernel(mass, vel, cell, listed, counts, stay, up, down):
    drops = mass.shape[1]
    slots = listed.shape[1]
    half = slots // 2
    k = lax.broadcasted_iota(jnp.int32, (1, slots), 1)
    valid = k < jnp.where(k < half, counts[0, 0], half + counts[0, 1])
    chosen = jnp.where(valid, listed[...], -1)
    member = (lax.broadcasted_iota(jnp.int32, (drops, slots), 0) == chosen).astype(F32).astype(BF16)
    row = lax.broadcasted_iota(jnp.int32, (16, slots), 0)
    column = lax.broadcasted_iota(jnp.int32, (16, slots), 1)
    which = (row == (column >= half).astype(jnp.int32)).astype(F32).astype(BF16)
    mask = dot_nt(which, member)
    goes_up, goes_down = mask[0:1], mask[1:2]
    m = mass[...]
    charges = jnp.concatenate([m] + [m * vel[i] for i in range(vel.shape[0])], 0)
    high = charges.astype(BF16).astype(F32)
    both = jnp.concatenate([high, charges - high], 0)
    rows = jnp.concatenate(
        [both * (1.0 - goes_up - goes_down), both * goes_up, both * goes_down, jnp.zeros_like(both)], 0
    ).astype(BF16)
    chunk = 256
    for start in range(0, stay.shape[1], chunk):
        here = lax.broadcasted_iota(jnp.int32, (chunk, drops), 0) + start
        onehot = (here == cell[...]).astype(F32).astype(BF16)
        got = dot_nt(rows, onehot)
        for i, out in enumerate((stay, up, down)):
            out[:, start : start + chunk] = got[8 * i : 8 * i + 4] + got[8 * i + 4 : 8 * i + 8]


def feature_kernel(stay, below, above, fields, cotangent, feats, drag):
    deposit = stay[...] + below[...] + above[...]
    state = flat_cells(fields)
    force = drag_rate * (deposit[1:4] - deposit[0:1] * state[0:3])
    drag[...] = force
    cells = state.shape[1]
    feats[...] = jnp.concatenate(
        [
            dt_step * flat_cells(cotangent),
            force[2:3],
            jnp.zeros((2, cells), F32),
            state,
            deposit[0:1],
            force[0:2],
        ],
        0,
    ).astype(BF16)


def tap_rows():
    r = lax.broadcasted_iota(jnp.int32, (288, 256), 0)
    k = lax.broadcasted_iota(jnp.int32, (288, 256), 1)
    c, t = r >> 5, r & 31
    ox = (t >= 9).astype(jnp.int32) + (t >= 18).astype(jnp.int32)
    q = t - 9 * ox
    ninth = jnp.where(q < 8, 216 + 8 * ox + q, 240 + ox)
    at = jnp.where(c < 8, 8 * t + c, ninth)
    return ((at == k) & (t < 27)).astype(F32).astype(BF16)


def weight_kernel(me, w_in, w_mid, w_out, wt, w_back, w_first, wo, wc):
    block, hid = wo.shape[0], wt.shape[1]
    row = lax.broadcasted_iota(jnp.int32, (block, hid), 0)
    column = lax.broadcasted_iota(jnp.int32, (block, hid), 1)
    chosen = (column == row + me[0] * block).astype(F32).astype(BF16)
    for t in range(27):
        wt[t * block : (t + 1) * block] = dot_nt(chosen, w_mid[t]).astype(BF16)
    w_back[...] = wt[...].astype(F32).T.astype(BF16)
    pad = jnp.zeros((5, hid), F32)
    tall = jnp.concatenate([v for c in range(9) for v in (w_in[c].astype(F32), pad)], 0)
    w_first[...] = (0.5 * dot(tall.T.astype(BF16), tap_rows())).astype(BF16)
    wide = w_out[...].astype(F32)
    wide = jnp.concatenate([wide, jnp.zeros((16 - wide.shape[0], hid), F32)], 0).astype(BF16)
    wo[...] = dot_nt(chosen, wide).astype(BF16)
    wc[...] = dot_nt(wide, chosen).astype(BF16)


def span(x, lanes, count=1):
    return slice(x * lanes, (x + count) * lanes)


def plane_taps(g2z, x, planes, nz, lanes):
    parts = []
    for ox, oy, oz in offsets:
        parts.append(ahead_y(g2z[0, oz + 1, :, span((x - ox) % planes, lanes)], -oy, nz))
    return jnp.concatenate(parts, 0)


def closure_kernel(nz, lanes, sources, place, w_first, wt, wo, wc, *refs):
    arrived, refs = refs[:sources], refs[sources:]
    piece, closure, g2z, fcol, feats, fz, eighth, ninth, hidden, sums, mid, last = refs
    s = pl.program_id(0)
    samples = pl.num_programs(0)
    slabs = place.shape[0]
    cells = hidden.shape[1]
    planes = cells // lanes
    per = planes // slabs
    block = wo.shape[0]
    group = 4

    @pl.when(s == 0)
    def _():
        mid[...] = jnp.zeros_like(mid)
        last[...] = jnp.zeros_like(last)
        at = 0
        for ref in arrived:
            feats[at : at + ref.shape[0]] = ref[...]
            at += ref.shape[0]

    sums[...] = jnp.zeros_like(sums)
    sub = lax.broadcasted_iota(jnp.int32, (8, lanes), 0)

    def spread(j):
        f = feats[place[j] + s].astype(F32)
        at = span(j, per * lanes)
        fz[0, :, at] = roll_z(f, 1, nz)
        fz[1, :, at] = f
        fz[2, :, at] = roll_z(f, -1, nz)

    for j in range(slabs):
        spread(j)

    def around(x):
        return [span((x + ox) % planes, lanes) for ox in (-1, 0, 1)]

    def ninth_rows(x):
        at = span(x, lanes)
        rows = [jnp.broadcast_to(fz[oz + 1, 5:6, at], (8, lanes)) for oz in (-1, 0, 1)]
        tile = ahead_y(rows[0], -1, nz)
        for q in range(1, 8):
            tile = jnp.where(sub == q, ahead_y(rows[q % 3], q // 3 - 1, nz), tile)
        eighth[:, at] = tile
        ninth[:, at] = ahead_y(rows[2], 1, nz)

    for x in range(planes):
        ninth_rows(x)

    def patches(x):
        near = around(x)
        pieces = [ahead_y(fz[oz + 1, 8:16, near[ox + 1]], oy, nz) for ox, oy, oz in offsets]
        pieces += [eighth[:, n] for n in near]
        tail = jnp.where(sub == 0, ninth[:, near[0]], jnp.where(sub == 1, ninth[:, near[1]], ninth[:, near[2]]))
        pieces += [jnp.where(sub < 3, tail, 0.0), jnp.zeros((8, lanes), F32)]
        fcol[0, :, near[1]] = jnp.concatenate(pieces, 0).astype(BF16)

    for x in range(planes):
        patches(x)

    def first(x):
        at = span(x, lanes)
        half = dot(w_first[...], fcol[0, :, at])
        hidden[:, at] = (half * jnp.tanh(half) + half).astype(BF16)

    for x in range(planes):
        first(x)

    def second(x):
        near = around(x)
        prod = dot(wt[...], hidden[:, near[1]])
        for ox in (-1, 0, 1):
            to = near[1 - ox]
            for oz in (-1, 0, 1):
                total = None
                for oy in (-1, 0, 1):
                    t = 9 * (ox + 1) + 3 * (oy + 1) + oz + 1
                    v = ahead_y(prod[t * block : (t + 1) * block], oy, nz)
                    total = v if total is None else total + v
                sums[oz + 1, :, to] += total

    for x in range(planes):
        second(x)

    def gradient(j):
        here = feats[place[j] + s]
        at = span(j, per * lanes)
        pre = sums[1, :, at] + roll_z(sums[0, :, at], 1, nz) + roll_z(sums[2, :, at], -1, nz)
        sig = logistic(pre)
        hid = (pre * sig).astype(BF16)
        out = dot(wc[...], hid)
        for h in range(per):
            for k in range(2):
                start = h * lanes + k * (lanes // 2)
                closure[0, j * per + h, 8 * k : 8 * k + 8] = out[0:8, start : start + lanes // 2].astype(BF16)
        grad = dot(wo[...], here) * (sig * (1.0 + pre * (1.0 - sig)))
        last[...] += dot_nt(here, hid)
        rounded = grad.astype(BF16)
        grad = rounded.astype(F32)
        g2z[0, 0, :, at] = roll_z(grad, -1, nz).astype(BF16)
        g2z[0, 1, :, at] = rounded
        g2z[0, 2, :, at] = roll_z(grad, 1, nz).astype(BF16)

    for j in range(slabs):
        gradient(j)

    @pl.when(s >= 0)
    def _():
        for x in range(0, planes, group):
            columns = [plane_taps(g2z, x + h, planes, nz, lanes) for h in range(group)]
            mid[...] += dot_nt(jnp.concatenate(columns, 1), hidden[:, span(x, lanes, group)])

    @pl.when(s == samples - 1)
    def _():
        total = mid[...]
        taps = total.shape[0]
        piece[0:taps] = total.astype(BF16)
        squares = jnp.sum(total * total, keepdims=True)
        high = squares.astype(BF16).astype(F32)
        width = total.shape[1]
        row = lax.broadcasted_iota(jnp.int32, (block, width), 0)
        column = lax.broadcasted_iota(jnp.int32, (block, width), 1)
        extra = jnp.concatenate([last[...], jnp.zeros((block, width - block), F32)], 1)
        extra = jnp.where(row < 5, extra, 0.0)
        extra = jnp.where((row == 8) & (column == 0), high, extra)
        extra = jnp.where((row == 8) & (column == 1), squares - high, extra)
        piece[taps:] = extra.astype(BF16)


def first_kernel(nz, lanes, w_first, w_back, fcol, g2z, out):
    @pl.when(pl.program_id(0) == 0)
    def _():
        out[...] = jnp.zeros_like(out)

    planes = fcol.shape[2] // lanes
    group = 2
    for x in range(0, planes, group):
        at = span(x, lanes, group)
        columns = [plane_taps(g2z, x + h, planes, nz, lanes) for h in range(group)]
        back = dot(w_back[...], jnp.concatenate(columns, 1))
        column = fcol[0, :, at]
        half = dot(w_first[...], column)
        double = 1.0 + jnp.tanh(half)
        grad = (back * (double * (0.5 + half - 0.5 * half * double))).astype(BF16)
        out[...] += dot_nt(column, grad)


def split_kernel(core, one, two, closure, message, keep, kept):
    half = keep.shape[0]
    mine = pl.multiple_of(core[0] * half, half)
    theirs = pl.multiple_of((1 - core[0]) * half, half)
    keep[...] = one[pl.ds(mine, half)] + two[pl.ds(mine, half)]
    message[0:half] = one[pl.ds(theirs, half)] + two[pl.ds(theirs, half)]
    samples, planes = closure.shape[:2]
    at = 0
    for s in range(samples):
        for y in range(planes // 4):
            for p in range(2):
                kept[at : at + 16] = closure[s, 4 * y + 2 * core[0] + p].astype(F32)
                message[half + at : half + at + 16] = closure[s, 4 * y + 2 * (1 - core[0]) + p].astype(F32)
                at += 16


def merge_kernel(bit, got, mine, kept, message, keep):
    half = 128
    message[0:half] = (mine[...] + got[0:half]).astype(BF16)
    for o in range(keep.shape[0] // 32):
        a = pl.multiple_of((2 * o + bit[0]) * 32, 32)
        b = pl.multiple_of((2 * o + 1 - bit[0]) * 32, 32)
        keep[o * 32 : o * 32 + 32] = kept[pl.ds(a, 32)] + got[pl.ds(half + a, 32)]
        message[half + o * 32 : half + o * 32 + 32] = (kept[pl.ds(b, 32)] + got[pl.ds(half + b, 32)]).astype(BF16)


def fan_kernel(got, mine, kept, keep, *messages):
    half = 128
    raw = (mine[0:half].astype(F32) + got[0:half].astype(F32)).astype(BF16)
    for o in range(4):
        rows = kept[o * 32 : o * 32 + 32] + got[half + o * 32 : half + o * 32 + 32].astype(F32)
        if o == 0:
            keep[...] = rows
        else:
            messages[o - 1][0:half] = raw
            messages[o - 1][half:] = rows.astype(BF16)


def step_kernel(nz, place, fields, drag, closure, *refs):
    step_fields(nz, place, fields, drag, closure[...], refs[:-1], refs[-1])


def total_kernel(nz, place, fields, drag, mine, kept, one, two, three, *refs):
    sources, (half, out) = refs[:-2], refs[-2:]
    pair = mine[0:128].astype(F32) + one[0:128].astype(F32)
    half[...] = pair + (two[0:128].astype(F32) + three[0:128].astype(F32))
    closure = kept[...] + (one[128:].astype(F32) + two[128:].astype(F32) + three[128:].astype(F32))
    step_fields(nz, place, fields, drag, closure, sources, out)


def step_fields(nz, place, fields, drag, closure, sources, out):
    state = flat_cells(fields)
    cells = state.shape[1]
    planes, rows = fields.shape[2], fields.shape[3]
    lanes = cells // planes
    lower, upper = (sources[0][place[i] if len(sources) == 1 else 0].astype(F32) for i in range(2))
    for g in range(1, len(sources)):
        other = sources[g][0].astype(F32)
        lower, upper = (jnp.where(place[i] == g, other, v) for i, v in enumerate((lower, upper)))
    lower, upper = lower[8:13, cells - lanes :], upper[8:13, :lanes]
    wide = jnp.concatenate([lower, state, upper], 1)
    next_x, last_x = wide[:, 2 * lanes :], wide[:, :cells]
    parts = [state[:, i * lanes : (i + 1) * lanes] for i in range(planes)]
    next_y = jnp.concatenate([ahead_y(v, 1, nz) for v in parts], 1)
    last_y = jnp.concatenate([ahead_y(v, -1, nz) for v in parts], 1)
    next_z, last_z = roll_z(state, -1, nz), roll_z(state, 1, nz)
    laplace = next_x + last_x + next_y + last_y + next_z + last_z - 6.0 * state
    advect = -0.5 * (
        state[0:1] * (next_x - last_x) + state[1:2] * (next_y - last_y) + state[2:3] * (next_z - last_z)
    )
    momentum = jnp.concatenate([drag[...], jnp.zeros((2, cells), F32)], 0)
    closed = jnp.concatenate([closure[k : k + 5] for k in range(0, closure.shape[0], 8)], 1)
    new = state + dt_step * (viscosity * laplace + advect + closed + momentum)
    for x in range(planes):
        for y in range(rows):
            at = (x * rows + y) * nz
            out[0, :, x, y, :] = new[:, at : at + nz]


def finish_kernel(count, weight_count, place, core, own, other, *refs):
    pieces, (mid_out, first_out, last_out, held, done, arrive, leave) = refs[:count], refs[count:]
    slots = held.shape[0]
    block = done.shape[1] // slots
    rows = held.shape[1] - 16
    width = done.shape[1]

    copies, at = [], 0
    for i, ref in enumerate(pieces):
        copies.append(pltpu.make_async_copy(ref, held.at[at : at + ref.shape[0]], arrive.at[i]))
        at += ref.shape[0]
    for copy in copies:
        copy.start()
    a, b = own[...], other[...]
    swapped = core[0] == 1
    raw = jnp.concatenate([jnp.where(swapped, b, a), jnp.where(swapped, a, b)], 0)
    squares = jnp.sum(raw * raw, keepdims=True)
    high = raw.astype(BF16)
    ordered = dot(tap_rows(), high) + dot(tap_rows(), (raw - high.astype(F32)).astype(BF16))
    for copy in copies:
        copy.wait()
    last = []
    for d in range(slots):
        extra = held[place[d], rows:].astype(F32)
        last.append(extra[0:5, 0:block])
        squares = squares + jnp.sum(extra[8:9, 0:2], keepdims=True)
    last = jnp.concatenate(last, 1)
    squares = squares + jnp.sum(last * last, keepdims=True)
    clip = jnp.minimum(1.0, clip_rms * math.sqrt(weight_count) / jnp.sqrt(squares + 1e-06))
    last_out[...] = last * clip
    ordered = ordered * clip
    for c in range(first_out.shape[0]):
        first_out[c] = ordered[32 * c : 32 * c + 27]

    eye = (
        lax.broadcasted_iota(jnp.int32, (width, width), 0) == lax.broadcasted_iota(jnp.int32, (width, width), 1)
    ).astype(F32).astype(BF16)

    def leaving(t):
        return pltpu.make_async_copy(done.at[t], mid_out.at[t], leave.at[t])

    def flip(i, carry):
        for k in range(3):
            t = 3 * i + k
            start = pl.multiple_of(t * block, block)
            flipped = jnp.concatenate([held[place[d], pl.ds(start, block)] for d in range(slots)], 0)
            done[t] = dot_nt(eye, flipped) * clip
            leaving(t).start()
        return carry

    lax.fori_loop(0, 9, flip, 0)
    for t in range(27):
        leaving(t).wait()


def whole_spec(shape):
    return pl.BlockSpec(shape, lambda *unused: (0,) * len(shape))


SMEM = pl.BlockSpec(memory_space=pltpu.SMEM)
VMEM = pl.BlockSpec(memory_space=pltpu.VMEM)
ANY = pl.BlockSpec(memory_space=pl.ANY)


def cost(flops):
    return pl.CostEstimate(flops=int(flops), bytes_accessed=2**22, transcendentals=0)


def params(mebibytes):
    return pltpu.CompilerParams(vmem_limit_bytes=mebibytes * 2**20)


def shards(
    fields, drop_mass, drop_vel, drop_cell, cross_list, cross_count, w_in, w_mid, w_out, cotangent
):
    shape = jax.ShapeDtypeStruct
    n_slab, n_rep = lax.axis_size("slab"), lax.axis_size("rep")
    planes, ny, nz = fields.shape[2:]
    cells = planes * ny * nz
    lanes = ny * nz
    hid, cout = w_out.shape
    joined = n_slab * n_rep * 16 <= hid
    team = ("slab", "rep") if joined else ("slab",)
    samples = n_rep if joined else 1
    size = n_slab * samples
    block = hid // size
    fast = joined and n_slab == 4 and n_rep == 4
    slab, rep = lax.axis_index("slab"), lax.axis_index("rep")
    sample = rep if joined else jnp.zeros((), jnp.int32)
    me = slab * samples + sample
    all_planes = n_slab * planes
    everyone = jnp.arange(size, dtype=jnp.int32)

    def trade(v, mask):
        return lax.ppermute(v, team, [(d, d ^ mask) for d in range(size)])

    dense = shape((4, cells), F32)
    stay, up, down = pl.pallas_call(
        deposit_kernel,
        out_shape=(dense, dense, dense),
        in_specs=[VMEM] * 4 + [SMEM],
        out_specs=(VMEM,) * 3,
        compiler_params=params(8),
        name="deposit",
    )(drop_mass, jnp.transpose(drop_vel, (1, 0, 2)), drop_cell, cross_list, cross_count)
    from_below = lax.ppermute(up, "slab", [(i, (i + 1) % n_slab) for i in range(n_slab)])
    from_above = lax.ppermute(down, "slab", [((i + 1) % n_slab, i) for i in range(n_slab)])
    own_feats, drag = pl.pallas_call(
        feature_kernel,
        out_shape=(shape((16, cells), BF16), shape((3, cells), F32)),
        in_specs=[VMEM] * 5,
        out_specs=(VMEM,) * 2,
        compiler_params=params(4),
        name="features",
    )(stay, from_below, from_above, fields, cotangent)

    rows = 27 * block
    wt, w_back, w_first, wo, wc = pl.pallas_call(
        weight_kernel,
        out_shape=(
            shape((rows, hid), BF16),
            shape((hid, rows), BF16),
            shape((hid, 256), BF16),
            shape((block, 16), BF16),
            shape((16, block), BF16),
        ),
        in_specs=[SMEM] + [VMEM] * 3,
        out_specs=(VMEM,) * 5,
        compiler_params=params(16),
        cost_estimate=cost(1.5e9),
        name="weights",
    )(me[None], jnp.transpose(w_in, (1, 0, 2)), w_mid, w_out.T)

    if fast:
        near_z = [trade(own_feats, mask) for mask in (1, 2, 3)]
        wt, w_back, w_first, wo, wc, *near_z = lax.optimization_barrier((wt, w_back, w_first, wo, wc, *near_z))
        mine = jnp.stack([own_feats] + near_z)
        across = trade(mine, 8)
        sources = [mine, across, trade(mine, 4), trade(across, 4)]
        slabs = jnp.arange(n_slab, dtype=jnp.int32)
        group = 2 * ((slabs ^ slab) & 1) + (((slabs ^ slab) >> 1) & 1)
        place = group * samples
    else:
        sources = [lax.all_gather(own_feats, team)]
        group = jnp.arange(n_slab, dtype=jnp.int32)
        place = group * samples

    near = jnp.take(group, jnp.stack([(slab + n_slab - 1) % n_slab, (slab + 1) % n_slab]))

    team_cells = all_planes * lanes
    piece, closure, g2z, fcol = pl.pallas_call(
        functools.partial(closure_kernel, nz, lanes, len(sources)),
        grid=(samples,),
        out_shape=(
            shape((rows + 16, hid), BF16),
            shape((samples, all_planes, 16, lanes // 2), BF16),
            shape((samples, 3, block, team_cells), BF16),
            shape((samples, 256, team_cells), BF16),
        ),
        in_specs=[SMEM] + [VMEM] * (4 + len(sources)),
        out_specs=(
            whole_spec((rows + 16, hid)),
            pl.BlockSpec((1, all_planes, 16, lanes // 2), lambda s: (s, 0, 0, 0)),
            pl.BlockSpec((1, 3, block, team_cells), lambda s: (s, 0, 0, 0)),
            pl.BlockSpec((1, 256, team_cells), lambda s: (s, 0, 0)),
        ),
        scratch_shapes=[
            pltpu.VMEM((size, 16, cells), BF16),
            pltpu.VMEM((3, 16, team_cells), F32),
            pltpu.VMEM((8, team_cells), F32),
            pltpu.VMEM((8, team_cells), F32),
            pltpu.VMEM((hid, team_cells), BF16),
            pltpu.VMEM((3, block, team_cells), F32),
            pltpu.VMEM((rows, hid), F32),
            pltpu.VMEM((16, block), F32),
        ],
        compiler_params=params(30 if all_planes <= 8 else 58),
        cost_estimate=cost(9e9),
        name="closure",
    )(place, w_first, wt, wo, wc, *sources)

    def first_part(lo, count, fcol, g2z):
        return pl.pallas_call(
            functools.partial(first_kernel, nz, lanes),
            grid=(count,),
            out_shape=shape((256, hid), F32),
            in_specs=[
                whole_spec((hid, 256)),
                whole_spec((hid, rows)),
                pl.BlockSpec((1, 256, team_cells), lambda s: (s + lo, 0, 0)),
                pl.BlockSpec((1, 3, block, team_cells), lambda s: (s + lo, 0, 0, 0)),
            ],
            out_specs=whole_spec((256, hid)),
            compiler_params=params(18 if all_planes <= 8 else 58),
            cost_estimate=cost(7.6e9 * count / samples),
            name="first",
        )(w_first, w_back, fcol, g2z)

    if fast:
        core, y = slab & 1, slab >> 1

        def chip(at):
            at = at % 8
            return (0, at) if at < 4 else (1, 7 - at)

        def device(at, c):
            y, z = chip(at)
            return (2 * y + c) * n_rep + z

        def around(v, by):
            return lax.ppermute(v, team, [(device(at, c), device(at + by, c)) for at in range(8) for c in range(2)])

        def tie(*values):
            return lax.optimization_barrier(values)

        position = jnp.where(y == 0, rep, 7 - rep)
        theirs, their_z = everyone // n_rep, everyone % n_rep
        apart = (jnp.where(theirs < 2, their_z, 7 - their_z) - position) % 8
        piece_place = jnp.where(apart < 4, 2 * apart, 2 * (8 - apart) - 1)
        piece_place = jnp.where(apart == 0, 0, piece_place) + 8 * ((theirs ^ slab) & 1)
        piece_place = piece_place.astype(jnp.int32)
        f1, b1 = around(piece, 1), around(piece, -1)
        half_one = first_part(0, samples // 2, fcol, g2z)
        f1, b1, half_one, fcol, g2z, piece_place, near = tie(f1, b1, half_one, fcol, g2z, piece_place, near)
        f2, b2 = around(f1, 1), around(b1, -1)
        half_two = first_part(samples // 2, samples - samples // 2, fcol, g2z)
        f2, b2, half_two = tie(f2, b2, half_two)
        f3, b3 = around(f2, 1), around(b2, -1)

        message, keep, kept = pl.pallas_call(
            split_kernel,
            out_shape=(shape((384, hid), F32), shape((128, hid), F32), shape((256, hid), F32)),
            in_specs=[SMEM] + [VMEM] * 3,
            out_specs=(VMEM,) * 3,
            compiler_params=params(4),
            name="split",
        )(core[None], half_one, half_two, closure)
        got = trade(message, 4)
        message, kept = pl.pallas_call(
            merge_kernel,
            out_shape=(shape((256, hid), BF16), shape((128, hid), F32)),
            in_specs=[SMEM] + [VMEM] * 3,
            out_specs=(VMEM,) * 2,
            compiler_params=params(4),
            name="merge",
        )(y[None], got, keep, kept)
        got, f3, b3 = tie(trade(message, 8), f3, b3)
        f4 = around(f3, 1)
        kept, *messages = pl.pallas_call(
            fan_kernel,
            out_shape=(shape((32, hid), F32),) + (shape((160, hid), BF16),) * 3,
            in_specs=[VMEM] * 3,
            out_specs=(VMEM,) * 4,
            compiler_params=params(4),
            name="fan",
        )(got, message, kept)
        got = [trade(message, mask) for mask, message in zip((1, 2, 3), messages)]
        own, new_fields = pl.pallas_call(
            functools.partial(total_kernel, nz),
            out_shape=(shape((128, hid), F32), shape(fields.shape, F32)),
            in_specs=[SMEM] + [VMEM] * (7 + len(sources)),
            out_specs=(VMEM,) * 2,
            compiler_params=params(6),
            name="total",
        )(near, fields, drag, messages[0], kept, *got, *sources)
        other = trade(own, 4)
        pieces = [piece, f1, b1, f2, b2, f3, b3, f4]
        pieces = [v[None] for v in pieces + [trade(v, 4) for v in pieces]]
    else:
        raw_first = first_part(0, samples, fcol, g2z)
        core = jnp.zeros((), jnp.int32)
        if not joined:
            raw_first = lax.psum(raw_first, "rep")
            body = lax.psum(piece[:rows].astype(F32), "rep")
            extra = lax.psum(piece[rows:].astype(F32), "rep")
            squares = jnp.sum(body * body)
            high = squares.astype(BF16).astype(F32)
            extra = extra.at[8, 0].set(high).at[8, 1].set(squares - high)
            piece = jnp.concatenate([body, extra], 0).astype(BF16)
        raw_first = lax.psum(raw_first, team)
        own, other = raw_first[:128], raw_first[128:]
        pieces = [lax.all_gather(piece, team)]
        piece_place = everyone
        part = closure.reshape(samples, n_slab, planes * 16, lanes // 2)
        part = jnp.swapaxes(part, 0, 1).reshape(size, planes * 16, lanes // 2).astype(F32)
        own_closure = lax.psum_scatter(part, team, scatter_dimension=0)
        new_fields = pl.pallas_call(
            functools.partial(step_kernel, nz),
            out_shape=shape(fields.shape, F32),
            in_specs=[SMEM] + [VMEM] * 4,
            out_specs=VMEM,
            compiler_params=params(6),
            name="step",
        )(near, fields, drag, own_closure, sources[0].reshape(n_slab, samples, 16, cells)[:, sample])

    weight_count = w_in.size + w_mid.size + w_out.size
    grad_middle, grad_first, grad_last = pl.pallas_call(
        functools.partial(finish_kernel, len(pieces), weight_count),
        out_shape=(shape((27, hid, hid), F32), shape((9, 27, hid), F32), shape((cout, hid), F32)),
        in_specs=[SMEM] * 2 + [VMEM] * 2 + [ANY] * len(pieces),
        out_specs=(ANY, VMEM, VMEM),
        scratch_shapes=[
            pltpu.VMEM((size, rows + 16, hid), BF16),
            pltpu.VMEM((27, hid, hid), F32),
            pltpu.SemaphoreType.DMA((len(pieces),)),
            pltpu.SemaphoreType.DMA((27,)),
        ],
        compiler_params=params(20),
        name="finish",
    )(piece_place, core[None], own, other, *pieces)
    return (new_fields, jnp.transpose(grad_first, (1, 0, 2)), grad_middle, grad_last.T)


def solution(mesh):
    placed = (
        P(("groups", "rep"), None, "slab", None, None),
        P(("groups", "rep"), "slab"),
        P(("groups", "rep"), None, "slab"),
        P(("groups", "rep"), "slab"),
        P(("groups", "rep"), "slab"),
        P(("groups", "rep"), "slab"),
        P(),
        P(),
        P(),
        P(("groups", "rep"), None, "slab", None, None),
    )
    return jax.shard_map(
        shards,
        mesh=mesh,
        in_specs=placed,
        out_specs=(
            P(("groups", "rep"), None, "slab", None, None),
            P("groups", None, None),
            P("groups", None, None),
            P("groups", None),
        ),
        check_vma=False,
    )
```

```python
import functools
import math

import jax
import jax.numpy as jnp
from jax import lax
from jax.experimental import pallas as pl
from jax.experimental.pallas import tpu as pltpu
from jax.sharding import PartitionSpec as P

dt_step = 0.2
viscosity = 0.05
drag_rate = 0.5
clip_rms = 0.5

F32 = jnp.float32
BF16 = jnp.bfloat16
offsets = [(x, y, z) for x in (-1, 0, 1) for y in (-1, 0, 1) for z in (-1, 0, 1)]


def dot(a, b):
    return lax.dot_general(a, b, (((1,), (0,)), ((), ())), preferred_element_type=F32)


def dot_nt(a, b):
    return lax.dot_general(a, b, (((1,), (1,)), ((), ())), preferred_element_type=F32)


def logistic(p):
    return 0.5 * jnp.tanh(0.5 * p) + 0.5


def roll_z(v, by, nz):
    return jnp.concatenate(
        [pltpu.roll(v[:, k : k + nz], by % nz, 1) for k in range(0, v.shape[1], nz)], 1
    )


def ahead_y(v, by, nz):
    if by == 0:
        return v
    cut = (by * nz) % v.shape[1]
    return jnp.concatenate([v[:, cut:], v[:, :cut]], 1)


def flat_cells(ref):
    planes, rows = ref.shape[2], ref.shape[3]
    return jnp.concatenate([ref[0, :, x, y, :] for x in range(planes) for y in range(rows)], 1)


def fetch(pairs, sems):
    copies = [pltpu.make_async_copy(src, dst, sems.at[i]) for i, (src, dst) in enumerate(pairs)]
    for copy in copies:
        copy.start()
    for copy in copies:
        copy.wait()


def deposit_kernel(mass_in, vel_in, cell_in, listed_in, fields_in, cotangent_in, counts, stay, up, down, state, last_grad, *held):
    *held, sems = held
    fetch(list(zip((mass_in, vel_in, cell_in, listed_in, fields_in, cotangent_in), held)), sems)
    mass, vel, cell, listed, fields, cotangent = held
    state[...] = flat_cells(fields)
    last_grad[...] = dt_step * flat_cells(cotangent)
    drops = mass.shape[1]
    slots = listed.shape[1]
    half = slots // 2
    k = lax.broadcasted_iota(jnp.int32, (1, slots), 1)
    valid = k < jnp.where(k < half, counts[0, 0], half + counts[0, 1])
    chosen = jnp.where(valid, listed[...], -1)
    member = (lax.broadcasted_iota(jnp.int32, (drops, slots), 0) == chosen).astype(F32).astype(BF16)
    row = lax.broadcasted_iota(jnp.int32, (16, slots), 0)
    column = lax.broadcasted_iota(jnp.int32, (16, slots), 1)
    which = (row == (column >= half).astype(jnp.int32)).astype(F32).astype(BF16)
    mask = dot_nt(which, member)
    goes_up, goes_down = mask[0:1], mask[1:2]
    m = mass[...]
    charges = jnp.concatenate([m] + [m * vel[i] for i in range(vel.shape[0])], 0)
    high = charges.astype(BF16).astype(F32)
    both = jnp.concatenate([high, charges - high], 0)
    rows = jnp.concatenate(
        [both * (1.0 - goes_up - goes_down), both * goes_up, both * goes_down, jnp.zeros_like(both)], 0
    ).astype(BF16)
    chunk = 256
    for start in range(0, stay.shape[1], chunk):
        here = lax.broadcasted_iota(jnp.int32, (chunk, drops), 0) + start
        onehot = (here == cell[...]).astype(F32).astype(BF16)
        got = dot_nt(rows, onehot)
        for i, out in enumerate((stay, up, down)):
            out[:, start : start + chunk] = got[8 * i : 8 * i + 4] + got[8 * i + 4 : 8 * i + 8]


def feature_kernel(stay, below, above, fields, last_grad, feats, drag):
    deposit = stay[...] + below[...] + above[...]
    state = fields[...]
    force = drag_rate * (deposit[1:4] - deposit[0:1] * state[0:3])
    drag[...] = force
    cells = state.shape[1]
    feats[...] = jnp.concatenate(
        [
            last_grad[...],
            force[2:3],
            jnp.zeros((2, cells), F32),
            state,
            deposit[0:1],
            force[0:2],
        ],
        0,
    ).astype(BF16)


def tap_rows():
    r = lax.broadcasted_iota(jnp.int32, (288, 256), 0)
    k = lax.broadcasted_iota(jnp.int32, (288, 256), 1)
    c, t = r >> 5, r & 31
    ox = (t >= 9).astype(jnp.int32) + (t >= 18).astype(jnp.int32)
    q = t - 9 * ox
    ninth = jnp.where(q < 8, 216 + 8 * ox + q, 240 + ox)
    at = jnp.where(c < 8, 8 * t + c, ninth)
    return ((at == k) & (t < 27)).astype(F32).astype(BF16)


def weight_kernel(me, in_hbm, mid_hbm, out_hbm, wt, w_back, w_first, wo, wc, w_in, w_mid, w_out, sems):
    parts = 9
    share = w_mid.shape[0] // parts
    copies = []
    for i in range(parts):
        at = slice(i * share, (i + 1) * share)
        copies.append(pltpu.make_async_copy(mid_hbm.at[at], w_mid.at[at], sems.at[i]))
    small = [pltpu.make_async_copy(in_hbm, w_in, sems.at[parts]), pltpu.make_async_copy(out_hbm, w_out, sems.at[parts + 1])]
    for copy in small + copies:
        copy.start()
    for copy in small:
        copy.wait()
    block, hid = wo.shape[0], wt.shape[1]
    row = lax.broadcasted_iota(jnp.int32, (block, hid), 0)
    column = lax.broadcasted_iota(jnp.int32, (block, hid), 1)
    chosen = (column == row + me[0] * block).astype(F32).astype(BF16)
    pad = jnp.zeros((5, hid), F32)
    tall = jnp.concatenate([v for c in range(9) for v in (w_in[c].astype(F32), pad)], 0)
    w_first[...] = (0.5 * dot(tall.T.astype(BF16), tap_rows())).astype(BF16)
    wide = w_out[...].astype(F32)
    wide = jnp.concatenate([wide, jnp.zeros((16 - wide.shape[0], hid), F32)], 0).astype(BF16)
    wo[...] = dot_nt(chosen, wide).astype(BF16)
    wc[...] = dot_nt(wide, chosen).astype(BF16)
    for i, copy in enumerate(copies):
        copy.wait()
        for t in range(i * share, (i + 1) * share):
            wt[t * block : (t + 1) * block] = dot_nt(chosen, w_mid[t]).astype(BF16)
    w_back[...] = wt[...].astype(F32).T.astype(BF16)


def span(x, lanes, count=1):
    return slice(x * lanes, (x + count) * lanes)


def plane_taps(g2z, x, planes, nz, lanes):
    parts = []
    for ox, oy, oz in offsets:
        parts.append(ahead_y(g2z[0, oz + 1, :, span((x - ox) % planes, lanes)], -oy, nz))
    return jnp.concatenate(parts, 0)


def closure_kernel(nz, lanes, sources, place, w_first, wt, wo, wc, *refs):
    arrived, refs = refs[:sources], refs[sources:]
    piece, closure, g2z, fcol, feats, fz, eighth, ninth, hidden, sums, mid, last = refs
    s = pl.program_id(0)
    samples = pl.num_programs(0)
    slabs = place.shape[0]
    cells = hidden.shape[1]
    planes = cells // lanes
    per = planes // slabs
    block = wo.shape[0]
    group = 4

    @pl.when(s == 0)
    def _():
        mid[...] = jnp.zeros_like(mid)
        last[...] = jnp.zeros_like(last)
        at = 0
        for ref in arrived:
            feats[at : at + ref.shape[0]] = ref[...]
            at += ref.shape[0]

    sums[...] = jnp.zeros_like(sums)
    sub = lax.broadcasted_iota(jnp.int32, (8, lanes), 0)

    def spread(j):
        f = feats[place[j] + s].astype(F32)
        at = span(j, per * lanes)
        fz[0, :, at] = roll_z(f, 1, nz)
        fz[1, :, at] = f
        fz[2, :, at] = roll_z(f, -1, nz)

    for j in range(slabs):
        spread(j)

    def around(x):
        return [span((x + ox) % planes, lanes) for ox in (-1, 0, 1)]

    def ninth_rows(x):
        at = span(x, lanes)
        rows = [jnp.broadcast_to(fz[oz + 1, 5:6, at], (8, lanes)) for oz in (-1, 0, 1)]
        tile = ahead_y(rows[0], -1, nz)
        for q in range(1, 8):
            tile = jnp.where(sub == q, ahead_y(rows[q % 3], q // 3 - 1, nz), tile)
        eighth[:, at] = tile
        ninth[:, at] = ahead_y(rows[2], 1, nz)

    for x in range(planes):
        ninth_rows(x)

    def patches(x):
        near = around(x)
        pieces = [ahead_y(fz[oz + 1, 8:16, near[ox + 1]], oy, nz) for ox, oy, oz in offsets]
        pieces += [eighth[:, n] for n in near]
        tail = jnp.where(sub == 0, ninth[:, near[0]], jnp.where(sub == 1, ninth[:, near[1]], ninth[:, near[2]]))
        pieces += [jnp.where(sub < 3, tail, 0.0), jnp.zeros((8, lanes), F32)]
        fcol[0, :, near[1]] = jnp.concatenate(pieces, 0).astype(BF16)

    for x in range(planes):
        patches(x)

    def first(x):
        at = span(x, lanes)
        half = dot(w_first[...], fcol[0, :, at])
        hidden[:, at] = (half * jnp.tanh(half) + half).astype(BF16)

    for x in range(planes):
        first(x)

    def second(x):
        near = around(x)
        prod = dot(wt[...], hidden[:, near[1]])
        for ox in (-1, 0, 1):
            to = near[1 - ox]
            for oz in (-1, 0, 1):
                total = None
                for oy in (-1, 0, 1):
                    t = 9 * (ox + 1) + 3 * (oy + 1) + oz + 1
                    v = ahead_y(prod[t * block : (t + 1) * block], oy, nz)
                    total = v if total is None else total + v
                sums[oz + 1, :, to] += total

    for x in range(planes):
        second(x)

    def gradient(j):
        here = feats[place[j] + s]
        at = span(j, per * lanes)
        pre = sums[1, :, at] + roll_z(sums[0, :, at], 1, nz) + roll_z(sums[2, :, at], -1, nz)
        sig = logistic(pre)
        hid = (pre * sig).astype(BF16)
        out = dot(wc[...], hid)
        for h in range(per):
            for k in range(2):
                start = h * lanes + k * (lanes // 2)
                closure[0, j * per + h, 8 * k : 8 * k + 8] = out[0:8, start : start + lanes // 2].astype(BF16)
        grad = dot(wo[...], here) * (sig * (1.0 + pre * (1.0 - sig)))
        last[...] += dot_nt(here, hid)
        rounded = grad.astype(BF16)
        grad = rounded.astype(F32)
        g2z[0, 0, :, at] = roll_z(grad, -1, nz).astype(BF16)
        g2z[0, 1, :, at] = rounded
        g2z[0, 2, :, at] = roll_z(grad, 1, nz).astype(BF16)

    for j in range(slabs):
        gradient(j)

    @pl.when(s >= 0)
    def _():
        for x in range(0, planes, group):
            columns = [plane_taps(g2z, x + h, planes, nz, lanes) for h in range(group)]
            mid[...] += dot_nt(jnp.concatenate(columns, 1), hidden[:, span(x, lanes, group)])

    @pl.when(s == samples - 1)
    def _():
        total = mid[...]
        taps = total.shape[0]
        piece[0:taps] = total.astype(BF16)
        squares = jnp.sum(total * total, keepdims=True)
        high = squares.astype(BF16).astype(F32)
        width = total.shape[1]
        row = lax.broadcasted_iota(jnp.int32, (block, width), 0)
        column = lax.broadcasted_iota(jnp.int32, (block, width), 1)
        extra = jnp.concatenate([last[...], jnp.zeros((block, width - block), F32)], 1)
        extra = jnp.where(row < 5, extra, 0.0)
        extra = jnp.where((row == 8) & (column == 0), high, extra)
        extra = jnp.where((row == 8) & (column == 1), squares - high, extra)
        piece[taps:] = extra.astype(BF16)


def first_kernel(nz, lanes, w_first, w_back, fcol, g2z, out):
    @pl.when(pl.program_id(0) == 0)
    def _():
        out[...] = jnp.zeros_like(out)

    planes = fcol.shape[2] // lanes
    group = 2
    for x in range(0, planes, group):
        at = span(x, lanes, group)
        columns = [plane_taps(g2z, x + h, planes, nz, lanes) for h in range(group)]
        back = dot(w_back[...], jnp.concatenate(columns, 1))
        column = fcol[0, :, at]
        half = dot(w_first[...], column)
        double = 1.0 + jnp.tanh(half)
        grad = (back * (double * (0.5 + half - 0.5 * half * double))).astype(BF16)
        out[...] += dot_nt(column, grad)


def split_kernel(core, one, two, closure, message, keep, kept):
    half = keep.shape[0]
    mine = pl.multiple_of(core[0] * half, half)
    theirs = pl.multiple_of((1 - core[0]) * half, half)
    keep[...] = one[pl.ds(mine, half)] + two[pl.ds(mine, half)]
    message[0:half] = one[pl.ds(theirs, half)] + two[pl.ds(theirs, half)]
    samples, planes = closure.shape[:2]
    at = 0
    for s in range(samples):
        for y in range(planes // 4):
            for p in range(2):
                kept[at : at + 16] = closure[s, 4 * y + 2 * core[0] + p].astype(F32)
                message[half + at : half + at + 16] = closure[s, 4 * y + 2 * (1 - core[0]) + p].astype(F32)
                at += 16


def merge_kernel(bit, got, mine, kept, message, keep):
    half = 128
    message[0:half] = (mine[...] + got[0:half]).astype(BF16)
    for o in range(keep.shape[0] // 32):
        a = pl.multiple_of((2 * o + bit[0]) * 32, 32)
        b = pl.multiple_of((2 * o + 1 - bit[0]) * 32, 32)
        keep[o * 32 : o * 32 + 32] = kept[pl.ds(a, 32)] + got[pl.ds(half + a, 32)]
        message[half + o * 32 : half + o * 32 + 32] = (kept[pl.ds(b, 32)] + got[pl.ds(half + b, 32)]).astype(BF16)


def fan_kernel(got, mine, kept, keep, *messages):
    half = 128
    raw = (mine[0:half].astype(F32) + got[0:half].astype(F32)).astype(BF16)
    for o in range(4):
        rows = kept[o * 32 : o * 32 + 32] + got[half + o * 32 : half + o * 32 + 32].astype(F32)
        if o == 0:
            keep[...] = rows
        else:
            messages[o - 1][0:half] = raw
            messages[o - 1][half:] = rows.astype(BF16)


def step_kernel(nz, place, fields, drag, closure, *refs):
    step_fields(nz, place, fields, drag, closure[...], refs[:-1], refs[-1])


def total_kernel(nz, place, fields, drag, mine, kept, one, two, three, *refs):
    sources, (half, out) = refs[:-2], refs[-2:]
    pair = mine[0:128].astype(F32) + one[0:128].astype(F32)
    half[...] = pair + (two[0:128].astype(F32) + three[0:128].astype(F32))
    closure = kept[...] + (one[128:].astype(F32) + two[128:].astype(F32) + three[128:].astype(F32))
    step_fields(nz, place, fields, drag, closure, sources, out)


def step_fields(nz, place, fields, drag, closure, sources, out):
    state = fields[...]
    cells = state.shape[1]
    planes, rows = out.shape[2], out.shape[3]
    lanes = cells // planes
    lower, upper = (sources[0][place[i] if len(sources) == 1 else 0].astype(F32) for i in range(2))
    for g in range(1, len(sources)):
        other = sources[g][0].astype(F32)
        lower, upper = (jnp.where(place[i] == g, other, v) for i, v in enumerate((lower, upper)))
    lower, upper = lower[8:13, cells - lanes :], upper[8:13, :lanes]
    wide = jnp.concatenate([lower, state, upper], 1)
    next_x, last_x = wide[:, 2 * lanes :], wide[:, :cells]
    parts = [state[:, i * lanes : (i + 1) * lanes] for i in range(planes)]
    next_y = jnp.concatenate([ahead_y(v, 1, nz) for v in parts], 1)
    last_y = jnp.concatenate([ahead_y(v, -1, nz) for v in parts], 1)
    next_z, last_z = roll_z(state, -1, nz), roll_z(state, 1, nz)
    laplace = next_x + last_x + next_y + last_y + next_z + last_z - 6.0 * state
    advect = -0.5 * (
        state[0:1] * (next_x - last_x) + state[1:2] * (next_y - last_y) + state[2:3] * (next_z - last_z)
    )
    momentum = jnp.concatenate([drag[...], jnp.zeros((2, cells), F32)], 0)
    closed = jnp.concatenate([closure[k : k + 5] for k in range(0, closure.shape[0], 8)], 1)
    new = state + dt_step * (viscosity * laplace + advect + closed + momentum)
    for x in range(planes):
        for y in range(rows):
            at = (x * rows + y) * nz
            out[0, :, x, y, :] = new[:, at : at + nz]


def finish_kernel(count, weight_count, place, core, own, other, *refs):
    pieces, (mid_out, first_out, last_out, held, done, leave) = refs[:count], refs[count:]
    slots = held.shape[0]
    block = done.shape[1] // slots
    rows = held.shape[1] - 16
    width = done.shape[1]

    at = 0
    for ref in pieces:
        held[at : at + ref.shape[0]] = ref[...]
        at += ref.shape[0]
    a, b = own[...], other[...]
    swapped = core[0] == 1
    raw = jnp.concatenate([jnp.where(swapped, b, a), jnp.where(swapped, a, b)], 0)
    squares = jnp.sum(raw * raw, keepdims=True)
    high = raw.astype(BF16)
    ordered = dot(tap_rows(), high) + dot(tap_rows(), (raw - high.astype(F32)).astype(BF16))
    last = []
    for d in range(slots):
        extra = held[place[d], rows:].astype(F32)
        last.append(extra[0:5, 0:block])
        squares = squares + jnp.sum(extra[8:9, 0:2], keepdims=True)
    last = jnp.concatenate(last, 1)
    squares = squares + jnp.sum(last * last, keepdims=True)
    clip = jnp.minimum(1.0, clip_rms * math.sqrt(weight_count) / jnp.sqrt(squares + 1e-06))
    last_out[...] = last * clip
    ordered = ordered * clip
    for c in range(first_out.shape[0]):
        first_out[c] = ordered[32 * c : 32 * c + 27]

    eye = (
        lax.broadcasted_iota(jnp.int32, (width, width), 0) == lax.broadcasted_iota(jnp.int32, (width, width), 1)
    ).astype(F32).astype(BF16)

    def leaving(t):
        return pltpu.make_async_copy(done.at[t], mid_out.at[t], leave.at[t])

    def flip(i, carry):
        for k in range(3):
            t = 3 * i + k
            start = pl.multiple_of(t * block, block)
            flipped = jnp.concatenate([held[place[d], pl.ds(start, block)] for d in range(slots)], 0)
            done[t] = dot_nt(eye, flipped) * clip
            leaving(t).start()
        return carry

    lax.fori_loop(0, 9, flip, 0, unroll=3)
    for t in range(27):
        leaving(t).wait()


def whole_spec(shape):
    return pl.BlockSpec(shape, lambda *unused: (0,) * len(shape))


SMEM = pl.BlockSpec(memory_space=pltpu.SMEM)
VMEM = pl.BlockSpec(memory_space=pltpu.VMEM)
ANY = pl.BlockSpec(memory_space=pl.ANY)
HBM = pl.BlockSpec(memory_space=pltpu.HBM)


def cost(flops):
    return pl.CostEstimate(flops=int(flops), bytes_accessed=2**22, transcendentals=0)


def params(mebibytes):
    return pltpu.CompilerParams(vmem_limit_bytes=mebibytes * 2**20)


def shards(
    fields, drop_mass, drop_vel, drop_cell, cross_list, cross_count, w_in, w_mid, w_out, cotangent
):
    shape = jax.ShapeDtypeStruct
    n_slab, n_rep = lax.axis_size("slab"), lax.axis_size("rep")
    planes, ny, nz = fields.shape[2:]
    cells = planes * ny * nz
    lanes = ny * nz
    hid, cout = w_out.shape
    joined = n_slab * n_rep * 16 <= hid
    team = ("slab", "rep") if joined else ("slab",)
    samples = n_rep if joined else 1
    size = n_slab * samples
    block = hid // size
    fast = joined and n_slab == 4 and n_rep == 4
    slab, rep = lax.axis_index("slab"), lax.axis_index("rep")
    sample = rep if joined else jnp.zeros((), jnp.int32)
    me = slab * samples + sample
    all_planes = n_slab * planes
    everyone = jnp.arange(size, dtype=jnp.int32)

    def trade(v, mask):
        return lax.ppermute(v, team, [(d, d ^ mask) for d in range(size)])

    dense = shape((4, cells), F32)
    flows = (drop_mass, jnp.transpose(drop_vel, (1, 0, 2)), drop_cell, cross_list, fields, cotangent)
    stay, up, down, state, last_grad = pl.pallas_call(
        deposit_kernel,
        out_shape=(dense, dense, dense, shape((5, cells), F32), shape((5, cells), F32)),
        in_specs=[HBM] * 6 + [SMEM],
        out_specs=(VMEM,) * 5,
        scratch_shapes=[pltpu.VMEM(v.shape, v.dtype) for v in flows] + [pltpu.SemaphoreType.DMA((6,))],
        compiler_params=params(8),
        name="deposit",
    )(*flows, cross_count)
    from_below = lax.ppermute(up, "slab", [(i, (i + 1) % n_slab) for i in range(n_slab)])
    from_above = lax.ppermute(down, "slab", [((i + 1) % n_slab, i) for i in range(n_slab)])
    own_feats, drag = pl.pallas_call(
        feature_kernel,
        out_shape=(shape((16, cells), BF16), shape((3, cells), F32)),
        in_specs=[VMEM] * 5,
        out_specs=(VMEM,) * 2,
        compiler_params=params(4),
        name="features",
    )(stay, from_below, from_above, state, last_grad)

    rows = 27 * block
    wt, w_back, w_first, wo, wc = pl.pallas_call(
        weight_kernel,
        out_shape=(
            shape((rows, hid), BF16),
            shape((hid, rows), BF16),
            shape((hid, 256), BF16),
            shape((block, 16), BF16),
            shape((16, block), BF16),
        ),
        in_specs=[SMEM] + [HBM] * 3,
        out_specs=(VMEM,) * 5,
        scratch_shapes=[
            pltpu.VMEM((9, 27, hid), BF16),
            pltpu.VMEM(w_mid.shape, BF16),
            pltpu.VMEM((cout, hid), BF16),
            pltpu.SemaphoreType.DMA((11,)),
        ],
        compiler_params=params(16),
        cost_estimate=cost(1.5e9),
        name="weights",
    )(me[None], jnp.transpose(w_in, (1, 0, 2)), w_mid, w_out.T)

    if fast:
        far, middle, close = (trade(own_feats, mask) for mask in (3, 2, 1))
        near_z = [close, middle, far]
        wt, w_back, w_first, wo, wc, *near_z = lax.optimization_barrier((wt, w_back, w_first, wo, wc, *near_z))
        mine = jnp.stack([own_feats] + near_z)
        across = trade(mine, 8)
        sources = [mine, across, trade(mine, 4), trade(across, 4)]
        slabs = jnp.arange(n_slab, dtype=jnp.int32)
        group = 2 * ((slabs ^ slab) & 1) + (((slabs ^ slab) >> 1) & 1)
        place = group * samples
    else:
        sources = [lax.all_gather(own_feats, team)]
        group = jnp.arange(n_slab, dtype=jnp.int32)
        place = group * samples

    near = jnp.take(group, jnp.stack([(slab + n_slab - 1) % n_slab, (slab + 1) % n_slab]))

    team_cells = all_planes * lanes
    piece, closure, g2z, fcol = pl.pallas_call(
        functools.partial(closure_kernel, nz, lanes, len(sources)),
        grid=(samples,),
        out_shape=(
            shape((rows + 16, hid), BF16),
            shape((samples, all_planes, 16, lanes // 2), BF16),
            shape((samples, 3, block, team_cells), BF16),
            shape((samples, 256, team_cells), BF16),
        ),
        in_specs=[SMEM] + [VMEM] * (4 + len(sources)),
        out_specs=(
            whole_spec((rows + 16, hid)),
            pl.BlockSpec((1, all_planes, 16, lanes // 2), lambda s: (s, 0, 0, 0)),
            pl.BlockSpec((1, 3, block, team_cells), lambda s: (s, 0, 0, 0)),
            pl.BlockSpec((1, 256, team_cells), lambda s: (s, 0, 0)),
        ),
        scratch_shapes=[
            pltpu.VMEM((size, 16, cells), BF16),
            pltpu.VMEM((3, 16, team_cells), F32),
            pltpu.VMEM((8, team_cells), F32),
            pltpu.VMEM((8, team_cells), F32),
            pltpu.VMEM((hid, team_cells), BF16),
            pltpu.VMEM((3, block, team_cells), F32),
            pltpu.VMEM((rows, hid), F32),
            pltpu.VMEM((16, block), F32),
        ],
        compiler_params=params(30 if all_planes <= 8 else 58),
        cost_estimate=cost(9e9),
        name="closure",
    )(place, w_first, wt, wo, wc, *sources)

    def first_part(lo, count, fcol, g2z):
        return pl.pallas_call(
            functools.partial(first_kernel, nz, lanes),
            grid=(count,),
            out_shape=shape((256, hid), F32),
            in_specs=[
                whole_spec((hid, 256)),
                whole_spec((hid, rows)),
                pl.BlockSpec((1, 256, team_cells), lambda s: (s + lo, 0, 0)),
                pl.BlockSpec((1, 3, block, team_cells), lambda s: (s + lo, 0, 0, 0)),
            ],
            out_specs=whole_spec((256, hid)),
            compiler_params=params(18 if all_planes <= 8 else 58),
            cost_estimate=cost(7.6e9 * count / samples),
            name="first",
        )(w_first, w_back, fcol, g2z)

    if fast:
        core, y = slab & 1, slab >> 1

        def chip(at):
            at = at % 8
            return (0, at) if at < 4 else (1, 7 - at)

        def device(at, c):
            y, z = chip(at)
            return (2 * y + c) * n_rep + z

        def around(v, by):
            return lax.ppermute(v, team, [(device(at, c), device(at + by, c)) for at in range(8) for c in range(2)])

        def tie(*values):
            return lax.optimization_barrier(values)

        position = jnp.where(y == 0, rep, 7 - rep)
        theirs, their_z = everyone // n_rep, everyone % n_rep
        apart = (jnp.where(theirs < 2, their_z, 7 - their_z) - position) % 8
        piece_place = jnp.where(apart < 4, 2 * apart, 2 * (8 - apart) - 1)
        piece_place = jnp.where(apart == 0, 0, piece_place) + 8 * ((theirs ^ slab) & 1)
        piece_place = piece_place.astype(jnp.int32)
        f1, b1 = around(piece, 1), around(piece, -1)
        half_one = first_part(0, samples // 2, fcol, g2z)
        f1, b1, half_one, fcol, g2z, piece_place, near = tie(f1, b1, half_one, fcol, g2z, piece_place, near)
        f2, b2 = around(f1, 1), around(b1, -1)
        half_two = first_part(samples // 2, samples - samples // 2, fcol, g2z)
        f2, b2, half_two = tie(f2, b2, half_two)
        f3, b3 = around(f2, 1), around(b2, -1)

        message, keep, kept = pl.pallas_call(
            split_kernel,
            out_shape=(shape((384, hid), F32), shape((128, hid), F32), shape((256, hid), F32)),
            in_specs=[SMEM] + [VMEM] * 3,
            out_specs=(VMEM,) * 3,
            compiler_params=params(4),
            name="split",
        )(core[None], half_one, half_two, closure)
        got = trade(message, 4)
        message, kept = pl.pallas_call(
            merge_kernel,
            out_shape=(shape((256, hid), BF16), shape((128, hid), F32)),
            in_specs=[SMEM] + [VMEM] * 3,
            out_specs=(VMEM,) * 2,
            compiler_params=params(4),
            name="merge",
        )(y[None], got, keep, kept)
        got, f3, b3 = tie(trade(message, 8), f3, b3)
        f4 = around(f3, 1)
        kept, *messages = pl.pallas_call(
            fan_kernel,
            out_shape=(shape((32, hid), F32),) + (shape((160, hid), BF16),) * 3,
            in_specs=[VMEM] * 3,
            out_specs=(VMEM,) * 4,
            compiler_params=params(4),
            name="fan",
        )(got, message, kept)
        got = [trade(message, mask) for mask, message in zip((1, 2, 3), messages)]
        own, new_fields = pl.pallas_call(
            functools.partial(total_kernel, nz),
            out_shape=(shape((128, hid), F32), shape(fields.shape, F32)),
            in_specs=[SMEM] + [VMEM] * (7 + len(sources)),
            out_specs=(VMEM,) * 2,
            compiler_params=params(6),
            name="total",
        )(near, state, drag, messages[0], kept, *got, *sources)
        other = trade(own, 4)
        pieces = [piece, f1, b1, f2, b2, f3, b3, f4]
        pieces = [v[None] for v in pieces + [trade(v, 4) for v in pieces]]
    else:
        raw_first = first_part(0, samples, fcol, g2z)
        core = jnp.zeros((), jnp.int32)
        if not joined:
            raw_first = lax.psum(raw_first, "rep")
            body = lax.psum(piece[:rows].astype(F32), "rep")
            extra = lax.psum(piece[rows:].astype(F32), "rep")
            squares = jnp.sum(body * body)
            high = squares.astype(BF16).astype(F32)
            extra = extra.at[8, 0].set(high).at[8, 1].set(squares - high)
            piece = jnp.concatenate([body, extra], 0).astype(BF16)
        raw_first = lax.psum(raw_first, team)
        own, other = raw_first[:128], raw_first[128:]
        pieces = [lax.all_gather(piece, team)]
        piece_place = everyone
        part = closure.reshape(samples, n_slab, planes * 16, lanes // 2)
        part = jnp.swapaxes(part, 0, 1).reshape(size, planes * 16, lanes // 2).astype(F32)
        own_closure = lax.psum_scatter(part, team, scatter_dimension=0)
        new_fields = pl.pallas_call(
            functools.partial(step_kernel, nz),
            out_shape=shape(fields.shape, F32),
            in_specs=[SMEM] + [VMEM] * 4,
            out_specs=VMEM,
            compiler_params=params(6),
            name="step",
        )(near, state, drag, own_closure, sources[0].reshape(n_slab, samples, 16, cells)[:, sample])

    weight_count = w_in.size + w_mid.size + w_out.size
    grad_middle, grad_first, grad_last = pl.pallas_call(
        functools.partial(finish_kernel, len(pieces), weight_count),
        out_shape=(shape((27, hid, hid), F32), shape((9, 27, hid), F32), shape((cout, hid), F32)),
        in_specs=[SMEM] * 2 + [VMEM] * (2 + len(pieces)),
        out_specs=(ANY, VMEM, VMEM),
        scratch_shapes=[
            pltpu.VMEM((size, rows + 16, hid), BF16),
            pltpu.VMEM((27, hid, hid), F32),
            pltpu.SemaphoreType.DMA((27,)),
        ],
        compiler_params=params(24),
        name="finish",
    )(piece_place, core[None], own, other, *pieces)
    return (new_fields, jnp.transpose(grad_first, (1, 0, 2)), grad_middle, grad_last.T)


def solution(mesh):
    placed = (
        P(("groups", "rep"), None, "slab", None, None),
        P(("groups", "rep"), "slab"),
        P(("groups", "rep"), None, "slab"),
        P(("groups", "rep"), "slab"),
        P(("groups", "rep"), "slab"),
        P(("groups", "rep"), "slab"),
        P(),
        P(),
        P(),
        P(("groups", "rep"), None, "slab", None, None),
    )
    return jax.shard_map(
        shards,
        mesh=mesh,
        in_specs=placed,
        out_specs=(
            P(("groups", "rep"), None, "slab", None, None),
            P("groups", None, None),
            P("groups", None, None),
            P("groups", None),
        ),
        check_vma=False,
    )
```

```python
import functools
import math

import jax
import jax.numpy as jnp
from jax import lax
from jax.experimental import pallas as pl
from jax.experimental.pallas import tpu as pltpu
from jax.sharding import PartitionSpec as P

dt_step = 0.2
viscosity = 0.05
drag_rate = 0.5
clip_rms = 0.5

F32 = jnp.float32
BF16 = jnp.bfloat16
offsets = [(x, y, z) for x in (-1, 0, 1) for y in (-1, 0, 1) for z in (-1, 0, 1)]


def dot(a, b):
    return lax.dot_general(a, b, (((1,), (0,)), ((), ())), preferred_element_type=F32)


def dot_nt(a, b):
    return lax.dot_general(a, b, (((1,), (1,)), ((), ())), preferred_element_type=F32)


def logistic(p):
    return 0.5 * jnp.tanh(0.5 * p) + 0.5


def roll_z(v, by, nz):
    return jnp.concatenate(
        [pltpu.roll(v[:, k : k + nz], by % nz, 1) for k in range(0, v.shape[1], nz)], 1
    )


def ahead_y(v, by, nz):
    if by == 0:
        return v
    cut = (by * nz) % v.shape[1]
    return jnp.concatenate([v[:, cut:], v[:, :cut]], 1)


def flat_cells(ref):
    planes, rows = ref.shape[2], ref.shape[3]
    return jnp.concatenate([ref[0, :, x, y, :] for x in range(planes) for y in range(rows)], 1)


def fetch(pairs, sems):
    copies = [pltpu.make_async_copy(src, dst, sems.at[i]) for i, (src, dst) in enumerate(pairs)]
    for copy in copies:
        copy.start()
    for copy in copies:
        copy.wait()


def deposit_kernel(mass_in, vel_in, cell_in, listed_in, fields_in, cotangent_in, counts, stay, up, down, *held):
    *held, sems = held
    fetch(list(zip((mass_in, vel_in, cell_in, listed_in, fields_in, cotangent_in), held)), sems)
    mass, vel, cell, listed, fields, cotangent = held
    stay[4:9] = flat_cells(fields)
    stay[9:14] = dt_step * flat_cells(cotangent)
    stay[14:] = jnp.zeros((2, stay.shape[1]), F32)
    drops = mass.shape[1]
    slots = listed.shape[1]
    half = slots // 2
    k = lax.broadcasted_iota(jnp.int32, (1, slots), 1)
    valid = k < jnp.where(k < half, counts[0, 0], half + counts[0, 1])
    chosen = jnp.where(valid, listed[...], -1)
    member = (lax.broadcasted_iota(jnp.int32, (drops, slots), 0) == chosen).astype(F32).astype(BF16)
    row = lax.broadcasted_iota(jnp.int32, (16, slots), 0)
    column = lax.broadcasted_iota(jnp.int32, (16, slots), 1)
    which = (row == (column >= half).astype(jnp.int32)).astype(F32).astype(BF16)
    mask = dot_nt(which, member)
    goes_up, goes_down = mask[0:1], mask[1:2]
    m = mass[...]
    charges = jnp.concatenate([m] + [m * vel[i] for i in range(vel.shape[0])], 0)
    high = charges.astype(BF16).astype(F32)
    both = jnp.concatenate([high, charges - high], 0)
    rows = jnp.concatenate(
        [both * (1.0 - goes_up - goes_down), both * goes_up, both * goes_down, jnp.zeros_like(both)], 0
    ).astype(BF16)
    chunk = 256
    for start in range(0, stay.shape[1], chunk):
        here = lax.broadcasted_iota(jnp.int32, (chunk, drops), 0) + start
        onehot = (here == cell[...]).astype(F32).astype(BF16)
        got = dot_nt(rows, onehot)
        for i, out in enumerate((stay, up, down)):
            out[0:4, start : start + chunk] = got[8 * i : 8 * i + 4] + got[8 * i + 4 : 8 * i + 8]


def feature_kernel(stay, below, above, feats, own):
    deposit = stay[0:4] + below[...] + above[...]
    state = stay[4:9]
    force = drag_rate * (deposit[1:4] - deposit[0:1] * state[0:3])
    own[...] = jnp.concatenate([state, force], 0)
    cells = state.shape[1]
    feats[...] = jnp.concatenate(
        [
            stay[9:14],
            force[2:3],
            jnp.zeros((2, cells), F32),
            state,
            deposit[0:1],
            force[0:2],
        ],
        0,
    ).astype(BF16)


def tap_rows():
    r = lax.broadcasted_iota(jnp.int32, (288, 256), 0)
    k = lax.broadcasted_iota(jnp.int32, (288, 256), 1)
    c, t = r >> 5, r & 31
    ox = (t >= 9).astype(jnp.int32) + (t >= 18).astype(jnp.int32)
    q = t - 9 * ox
    ninth = jnp.where(q < 8, 216 + 8 * ox + q, 240 + ox)
    at = jnp.where(c < 8, 8 * t + c, ninth)
    return ((at == k) & (t < 27)).astype(F32).astype(BF16)


def weight_kernel(me, in_hbm, mid_hbm, out_hbm, packed, w_back, w_in, w_mid, w_out, sems):
    parts = 9
    share = w_mid.shape[0] // parts
    copies = []
    for i in range(parts):
        at = slice(i * share, (i + 1) * share)
        copies.append(pltpu.make_async_copy(mid_hbm.at[at], w_mid.at[at], sems.at[i]))
    small = [pltpu.make_async_copy(in_hbm, w_in, sems.at[parts]), pltpu.make_async_copy(out_hbm, w_out, sems.at[parts + 1])]
    for copy in small + copies:
        copy.start()
    for copy in small:
        copy.wait()
    hid, rows = w_back.shape
    block = rows // 27
    row = lax.broadcasted_iota(jnp.int32, (block, hid), 0)
    column = lax.broadcasted_iota(jnp.int32, (block, hid), 1)
    chosen = (column == row + me[0] * block).astype(F32).astype(BF16)
    pad = jnp.zeros((5, hid), F32)
    tall = jnp.concatenate([v for c in range(9) for v in (w_in[c].astype(F32), pad)], 0)
    packed[rows : rows + hid] = (0.5 * dot(tall.T.astype(BF16), tap_rows())).astype(BF16)
    wide = w_out[...].astype(F32)
    wide = jnp.concatenate([wide, jnp.zeros((16 - wide.shape[0], hid), F32)], 0).astype(BF16)
    both = jnp.concatenate([dot_nt(chosen, wide), dot_nt(wide, chosen)], 0)
    packed[rows + hid :] = jnp.concatenate([both, jnp.zeros((32, hid - 16), F32)], 1).astype(BF16)
    for i, copy in enumerate(copies):
        copy.wait()
        for t in range(i * share, (i + 1) * share):
            packed[t * block : (t + 1) * block] = dot_nt(chosen, w_mid[t]).astype(BF16)
    w_back[...] = packed[0:rows].astype(F32).T.astype(BF16)


def span(x, lanes, count=1):
    return slice(x * lanes, (x + count) * lanes)


def plane_taps(g2z, x, planes, nz, lanes):
    parts = []
    for ox, oy, oz in offsets:
        parts.append(ahead_y(g2z[0, oz + 1, :, span((x - ox) % planes, lanes)], -oy, nz))
    return jnp.concatenate(parts, 0)


def closure_kernel(nz, lanes, sources, place, packed, *refs):
    arrived, refs = refs[:sources], refs[sources:]
    piece, closure, g2z, fcol, feats, fz, eighth, ninth, hidden, sums, mid, last = refs
    s = pl.program_id(0)
    samples = pl.num_programs(0)
    slabs = place.shape[0]
    cells = hidden.shape[1]
    planes = cells // lanes
    per = planes // slabs
    rows, hid = mid.shape
    block = last.shape[1]
    group = 4
    wt, w_first = packed.at[0:rows], packed.at[rows : rows + hid]
    wo = packed[rows + hid : rows + hid + 16, 0:16]
    wc = packed[rows + hid + 16 :, 0:16]

    @pl.when(s == 0)
    def _():
        mid[...] = jnp.zeros_like(mid)
        last[...] = jnp.zeros_like(last)
        at = 0
        for ref in arrived:
            feats[at : at + ref.shape[0]] = ref[...]
            at += ref.shape[0]

    sums[...] = jnp.zeros_like(sums)
    sub = lax.broadcasted_iota(jnp.int32, (8, lanes), 0)

    def spread(j):
        f = feats[place[j] + s].astype(F32)
        at = span(j, per * lanes)
        fz[0, :, at] = roll_z(f, 1, nz)
        fz[1, :, at] = f
        fz[2, :, at] = roll_z(f, -1, nz)

    for j in range(slabs):
        spread(j)

    def around(x):
        return [span((x + ox) % planes, lanes) for ox in (-1, 0, 1)]

    def ninth_rows(x):
        at = span(x, lanes)
        rows = [jnp.broadcast_to(fz[oz + 1, 5:6, at], (8, lanes)) for oz in (-1, 0, 1)]
        tile = ahead_y(rows[0], -1, nz)
        for q in range(1, 8):
            tile = jnp.where(sub == q, ahead_y(rows[q % 3], q // 3 - 1, nz), tile)
        eighth[:, at] = tile
        ninth[:, at] = ahead_y(rows[2], 1, nz)

    for x in range(planes):
        ninth_rows(x)

    def patches(x):
        near = around(x)
        pieces = [ahead_y(fz[oz + 1, 8:16, near[ox + 1]], oy, nz) for ox, oy, oz in offsets]
        pieces += [eighth[:, n] for n in near]
        tail = jnp.where(sub == 0, ninth[:, near[0]], jnp.where(sub == 1, ninth[:, near[1]], ninth[:, near[2]]))
        pieces += [jnp.where(sub < 3, tail, 0.0), jnp.zeros((8, lanes), F32)]
        fcol[0, :, near[1]] = jnp.concatenate(pieces, 0).astype(BF16)

    for x in range(planes):
        patches(x)

    def first(x):
        at = span(x, lanes)
        half = dot(w_first[...], fcol[0, :, at])
        hidden[:, at] = (half * jnp.tanh(half) + half).astype(BF16)

    for x in range(planes):
        first(x)

    def second(x):
        near = around(x)
        prod = dot(wt[...], hidden[:, near[1]])
        for ox in (-1, 0, 1):
            to = near[1 - ox]
            for oz in (-1, 0, 1):
                total = None
                for oy in (-1, 0, 1):
                    t = 9 * (ox + 1) + 3 * (oy + 1) + oz + 1
                    v = ahead_y(prod[t * block : (t + 1) * block], oy, nz)
                    total = v if total is None else total + v
                sums[oz + 1, :, to] += total

    for x in range(planes):
        second(x)

    def gradient(j):
        here = feats[place[j] + s]
        at = span(j, per * lanes)
        pre = sums[1, :, at] + roll_z(sums[0, :, at], 1, nz) + roll_z(sums[2, :, at], -1, nz)
        sig = logistic(pre)
        active = (pre * sig).astype(BF16)
        out = dot(wc, active)
        for h in range(per):
            for k in range(2):
                start = h * lanes + k * (lanes // 2)
                closure[0, j * per + h, 8 * k : 8 * k + 8] = out[0:8, start : start + lanes // 2].astype(BF16)
        grad = dot(wo, here) * (sig * (1.0 + pre * (1.0 - sig)))
        last[...] += dot_nt(here, active)
        rounded = grad.astype(BF16)
        grad = rounded.astype(F32)
        g2z[0, 0, :, at] = roll_z(grad, -1, nz).astype(BF16)
        g2z[0, 1, :, at] = rounded
        g2z[0, 2, :, at] = roll_z(grad, 1, nz).astype(BF16)

    for j in range(slabs):
        gradient(j)

    @pl.when(s >= 0)
    def _():
        for x in range(0, planes, group):
            columns = [plane_taps(g2z, x + h, planes, nz, lanes) for h in range(group)]
            mid[...] += dot_nt(jnp.concatenate(columns, 1), hidden[:, span(x, lanes, group)])

    @pl.when(s == samples - 1)
    def _():
        total = mid[...]
        taps = total.shape[0]
        piece[0:taps] = total.astype(BF16)
        squares = jnp.sum(total * total, keepdims=True)
        high = squares.astype(BF16).astype(F32)
        width = total.shape[1]
        row = lax.broadcasted_iota(jnp.int32, (block, width), 0)
        column = lax.broadcasted_iota(jnp.int32, (block, width), 1)
        extra = jnp.concatenate([last[...], jnp.zeros((block, width - block), F32)], 1)
        extra = jnp.where(row < 5, extra, 0.0)
        extra = jnp.where((row == 8) & (column == 0), high, extra)
        extra = jnp.where((row == 8) & (column == 1), squares - high, extra)
        piece[taps:] = extra.astype(BF16)


def first_kernel(nz, lanes, packed, w_back, fcol, g2z, out):
    @pl.when(pl.program_id(0) == 0)
    def _():
        out[...] = jnp.zeros_like(out)

    planes = fcol.shape[2] // lanes
    group = 2
    hid, rows = w_back.shape
    w_first = packed.at[rows : rows + hid]
    for x in range(0, planes, group):
        at = span(x, lanes, group)
        columns = [plane_taps(g2z, x + h, planes, nz, lanes) for h in range(group)]
        back = dot(w_back[...], jnp.concatenate(columns, 1))
        column = fcol[0, :, at]
        half = dot(w_first[...], column)
        double = 1.0 + jnp.tanh(half)
        grad = (back * (double * (0.5 + half - 0.5 * half * double))).astype(BF16)
        out[...] += dot_nt(column, grad)


def split_kernel(core, one, two, closure, message, keep, kept):
    half = keep.shape[0]
    mine = pl.multiple_of(core[0] * half, half)
    theirs = pl.multiple_of((1 - core[0]) * half, half)
    keep[...] = one[pl.ds(mine, half)] + two[pl.ds(mine, half)]
    message[0:half] = one[pl.ds(theirs, half)] + two[pl.ds(theirs, half)]
    samples, planes = closure.shape[:2]
    at = 0
    for s in range(samples):
        for y in range(planes // 4):
            for p in range(2):
                kept[at : at + 16] = closure[s, 4 * y + 2 * core[0] + p].astype(F32)
                message[half + at : half + at + 16] = closure[s, 4 * y + 2 * (1 - core[0]) + p].astype(F32)
                at += 16


def merge_kernel(bit, got, mine, kept, message, keep):
    half = 128
    message[0:half] = (mine[...] + got[0:half]).astype(BF16)
    for o in range(keep.shape[0] // 32):
        a = pl.multiple_of((2 * o + bit[0]) * 32, 32)
        b = pl.multiple_of((2 * o + 1 - bit[0]) * 32, 32)
        keep[o * 32 : o * 32 + 32] = kept[pl.ds(a, 32)] + got[pl.ds(half + a, 32)]
        message[half + o * 32 : half + o * 32 + 32] = (kept[pl.ds(b, 32)] + got[pl.ds(half + b, 32)]).astype(BF16)


def fan_kernel(got, mine, kept, keep, *messages):
    half = 128
    raw = (mine[0:half].astype(F32) + got[0:half].astype(F32)).astype(BF16)
    for o in range(4):
        rows = kept[o * 32 : o * 32 + 32] + got[half + o * 32 : half + o * 32 + 32].astype(F32)
        if o == 0:
            keep[...] = rows
        else:
            messages[o - 1][0:half] = raw
            messages[o - 1][half:] = rows.astype(BF16)


def step_kernel(nz, place, own, closure, *refs):
    step_fields(nz, place, own, closure[...], refs[:-1], refs[-1])


def total_kernel(nz, place, own, mine, kept, one, two, three, *refs):
    sources, (half, out) = refs[:-2], refs[-2:]
    pair = mine[0:128].astype(F32) + one[0:128].astype(F32)
    half[...] = pair + (two[0:128].astype(F32) + three[0:128].astype(F32))
    closure = kept[...] + (one[128:].astype(F32) + two[128:].astype(F32) + three[128:].astype(F32))
    step_fields(nz, place, own, closure, sources, out)


def step_fields(nz, place, own, closure, sources, out):
    state = own[0:5]
    cells = state.shape[1]
    planes, rows = out.shape[2], out.shape[3]
    lanes = cells // planes
    lower, upper = (sources[0][place[i] if len(sources) == 1 else 0].astype(F32) for i in range(2))
    for g in range(1, len(sources)):
        other = sources[g][0].astype(F32)
        lower, upper = (jnp.where(place[i] == g, other, v) for i, v in enumerate((lower, upper)))
    lower, upper = lower[8:13, cells - lanes :], upper[8:13, :lanes]
    wide = jnp.concatenate([lower, state, upper], 1)
    next_x, last_x = wide[:, 2 * lanes :], wide[:, :cells]
    parts = [state[:, i * lanes : (i + 1) * lanes] for i in range(planes)]
    next_y = jnp.concatenate([ahead_y(v, 1, nz) for v in parts], 1)
    last_y = jnp.concatenate([ahead_y(v, -1, nz) for v in parts], 1)
    next_z, last_z = roll_z(state, -1, nz), roll_z(state, 1, nz)
    laplace = next_x + last_x + next_y + last_y + next_z + last_z - 6.0 * state
    advect = -0.5 * (
        state[0:1] * (next_x - last_x) + state[1:2] * (next_y - last_y) + state[2:3] * (next_z - last_z)
    )
    momentum = jnp.concatenate([own[5:8], jnp.zeros((2, cells), F32)], 0)
    closed = jnp.concatenate([closure[k : k + 5] for k in range(0, closure.shape[0], 8)], 1)
    new = state + dt_step * (viscosity * laplace + advect + closed + momentum)
    for x in range(planes):
        for y in range(rows):
            at = (x * rows + y) * nz
            out[0, :, x, y, :] = new[:, at : at + nz]


def finish_kernel(count, weight_count, place, core, own, other, *refs):
    pieces, (mid_out, first_out, last_out, held, done, leave) = refs[:count], refs[count:]
    slots = held.shape[0]
    block = done.shape[1] // slots
    rows = held.shape[1] - 16
    width = done.shape[1]

    at = 0
    for ref in pieces:
        held[at : at + ref.shape[0]] = ref[...]
        at += ref.shape[0]
    a, b = own[...], other[...]
    swapped = core[0] == 1
    raw = jnp.concatenate([jnp.where(swapped, b, a), jnp.where(swapped, a, b)], 0)
    squares = jnp.sum(raw * raw, keepdims=True)
    high = raw.astype(BF16)
    ordered = dot(tap_rows(), high) + dot(tap_rows(), (raw - high.astype(F32)).astype(BF16))
    last = []
    for d in range(slots):
        extra = held[place[d], rows:].astype(F32)
        last.append(extra[0:5, 0:block])
        squares = squares + jnp.sum(extra[8:9, 0:2], keepdims=True)
    last = jnp.concatenate(last, 1)
    squares = squares + jnp.sum(last * last, keepdims=True)
    clip = jnp.minimum(1.0, clip_rms * math.sqrt(weight_count) / jnp.sqrt(squares + 1e-06))
    last_out[...] = last * clip
    ordered = ordered * clip
    for c in range(first_out.shape[0]):
        first_out[c] = ordered[32 * c : 32 * c + 27]

    eye = (
        lax.broadcasted_iota(jnp.int32, (width, width), 0) == lax.broadcasted_iota(jnp.int32, (width, width), 1)
    ).astype(F32).astype(BF16)

    def leaving(t):
        return pltpu.make_async_copy(done.at[t], mid_out.at[t], leave.at[t])

    def flip(i, carry):
        for k in range(3):
            t = 3 * i + k
            start = pl.multiple_of(t * block, block)
            flipped = jnp.concatenate([held[place[d], pl.ds(start, block)] for d in range(slots)], 0)
            done[t] = dot_nt(eye, flipped) * clip
            leaving(t).start()
        return carry

    lax.fori_loop(0, 9, flip, 0, unroll=3)
    for t in range(27):
        leaving(t).wait()


def whole_spec(shape):
    return pl.BlockSpec(shape, lambda *unused: (0,) * len(shape))


SMEM = pl.BlockSpec(memory_space=pltpu.SMEM)
VMEM = pl.BlockSpec(memory_space=pltpu.VMEM)
ANY = pl.BlockSpec(memory_space=pl.ANY)
HBM = pl.BlockSpec(memory_space=pltpu.HBM)


def cost(flops):
    return pl.CostEstimate(flops=int(flops), bytes_accessed=2**22, transcendentals=0)


def params(mebibytes):
    return pltpu.CompilerParams(vmem_limit_bytes=mebibytes * 2**20)


def shards(
    fields, drop_mass, drop_vel, drop_cell, cross_list, cross_count, w_in, w_mid, w_out, cotangent
):
    shape = jax.ShapeDtypeStruct
    n_slab, n_rep = lax.axis_size("slab"), lax.axis_size("rep")
    planes, ny, nz = fields.shape[2:]
    cells = planes * ny * nz
    lanes = ny * nz
    hid, cout = w_out.shape
    joined = n_slab * n_rep * 16 <= hid
    team = ("slab", "rep") if joined else ("slab",)
    samples = n_rep if joined else 1
    size = n_slab * samples
    block = hid // size
    fast = joined and n_slab == 4 and n_rep == 4
    slab, rep = lax.axis_index("slab"), lax.axis_index("rep")
    sample = rep if joined else jnp.zeros((), jnp.int32)
    me = slab * samples + sample
    all_planes = n_slab * planes
    everyone = jnp.arange(size, dtype=jnp.int32)

    def trade(v, mask):
        return lax.ppermute(v, team, [(d, d ^ mask) for d in range(size)])

    dense = shape((4, cells), F32)
    flows = (drop_mass, jnp.transpose(drop_vel, (1, 0, 2)), drop_cell, cross_list, fields, cotangent)
    stay, up, down = pl.pallas_call(
        deposit_kernel,
        out_shape=(shape((16, cells), F32), dense, dense),
        in_specs=[HBM] * 6 + [SMEM],
        out_specs=(VMEM,) * 3,
        scratch_shapes=[pltpu.VMEM(v.shape, v.dtype) for v in flows] + [pltpu.SemaphoreType.DMA((6,))],
        compiler_params=params(60),
        name="deposit",
    )(*flows, cross_count)
    from_below = lax.ppermute(up, "slab", [(i, (i + 1) % n_slab) for i in range(n_slab)])
    from_above = lax.ppermute(down, "slab", [((i + 1) % n_slab, i) for i in range(n_slab)])
    own_feats, own_state = pl.pallas_call(
        feature_kernel,
        out_shape=(shape((16, cells), BF16), shape((8, cells), F32)),
        in_specs=[VMEM] * 3,
        out_specs=(VMEM,) * 2,
        compiler_params=params(4),
        name="features",
    )(stay, from_below, from_above)

    rows = 27 * block
    packed, w_back = pl.pallas_call(
        weight_kernel,
        out_shape=(shape((rows + hid + 32, hid), BF16), shape((hid, rows), BF16)),
        in_specs=[SMEM] + [HBM] * 3,
        out_specs=(VMEM,) * 2,
        scratch_shapes=[
            pltpu.VMEM((9, 27, hid), BF16),
            pltpu.VMEM(w_mid.shape, BF16),
            pltpu.VMEM((cout, hid), BF16),
            pltpu.SemaphoreType.DMA((11,)),
        ],
        compiler_params=params(60),
        cost_estimate=cost(1.5e9),
        name="weights",
    )(me[None], jnp.transpose(w_in, (1, 0, 2)), w_mid, w_out.T)

    if fast:
        far, middle, close = (trade(own_feats, mask) for mask in (3, 2, 1))
        near_z = [close, middle, far]
        packed, w_back, *near_z = lax.optimization_barrier((packed, w_back, *near_z))
        mine = jnp.stack([own_feats] + near_z)
        across = trade(mine, 8)
        sources = [mine, across, trade(mine, 4), trade(across, 4)]
        slabs = jnp.arange(n_slab, dtype=jnp.int32)
        group = 2 * ((slabs ^ slab) & 1) + (((slabs ^ slab) >> 1) & 1)
        place = group * samples
    else:
        sources = [lax.all_gather(own_feats, team)]
        group = jnp.arange(n_slab, dtype=jnp.int32)
        place = group * samples

    near = jnp.take(group, jnp.stack([(slab + n_slab - 1) % n_slab, (slab + 1) % n_slab]))

    team_cells = all_planes * lanes
    piece, closure, g2z, fcol = pl.pallas_call(
        functools.partial(closure_kernel, nz, lanes, len(sources)),
        grid=(samples,),
        out_shape=(
            shape((rows + 16, hid), BF16),
            shape((samples, all_planes, 16, lanes // 2), BF16),
            shape((samples, 3, block, team_cells), BF16),
            shape((samples, 256, team_cells), BF16),
        ),
        in_specs=[SMEM] + [VMEM] * (1 + len(sources)),
        out_specs=(
            whole_spec((rows + 16, hid)),
            pl.BlockSpec((1, all_planes, 16, lanes // 2), lambda s: (s, 0, 0, 0)),
            pl.BlockSpec((1, 3, block, team_cells), lambda s: (s, 0, 0, 0)),
            pl.BlockSpec((1, 256, team_cells), lambda s: (s, 0, 0)),
        ),
        scratch_shapes=[
            pltpu.VMEM((size, 16, cells), BF16),
            pltpu.VMEM((3, 16, team_cells), F32),
            pltpu.VMEM((8, team_cells), F32),
            pltpu.VMEM((8, team_cells), F32),
            pltpu.VMEM((hid, team_cells), BF16),
            pltpu.VMEM((3, block, team_cells), F32),
            pltpu.VMEM((rows, hid), F32),
            pltpu.VMEM((16, block), F32),
        ],
        compiler_params=params(30 if all_planes <= 8 else 58),
        cost_estimate=cost(9e9),
        name="closure",
    )(place, packed, *sources)

    def first_part(lo, count, fcol, g2z):
        return pl.pallas_call(
            functools.partial(first_kernel, nz, lanes),
            grid=(count,),
            out_shape=shape((256, hid), F32),
            in_specs=[
                whole_spec(packed.shape),
                whole_spec((hid, rows)),
                pl.BlockSpec((1, 256, team_cells), lambda s: (s + lo, 0, 0)),
                pl.BlockSpec((1, 3, block, team_cells), lambda s: (s + lo, 0, 0, 0)),
            ],
            out_specs=whole_spec((256, hid)),
            compiler_params=params(18 if all_planes <= 8 else 58),
            cost_estimate=cost(7.6e9 * count / samples),
            name="first",
        )(packed, w_back, fcol, g2z)

    if fast:
        core, y = slab & 1, slab >> 1

        def chip(at):
            at = at % 8
            return (0, at) if at < 4 else (1, 7 - at)

        def device(at, c):
            y, z = chip(at)
            return (2 * y + c) * n_rep + z

        def around(v, by):
            return lax.ppermute(v, team, [(device(at, c), device(at + by, c)) for at in range(8) for c in range(2)])

        def tie(*values):
            return lax.optimization_barrier(values)

        position = jnp.where(y == 0, rep, 7 - rep)
        theirs, their_z = everyone // n_rep, everyone % n_rep
        apart = (jnp.where(theirs < 2, their_z, 7 - their_z) - position) % 8
        piece_place = jnp.where(apart < 4, 2 * apart, 2 * (8 - apart) - 1)
        piece_place = jnp.where(apart == 0, 0, piece_place) + 8 * ((theirs ^ slab) & 1)
        piece_place = piece_place.astype(jnp.int32)
        f1, b1 = around(piece, 1), around(piece, -1)
        half_one = first_part(0, samples // 2, fcol, g2z)
        f1, b1, half_one, fcol, g2z, piece_place, near = tie(f1, b1, half_one, fcol, g2z, piece_place, near)
        f2, b2 = around(f1, 1), around(b1, -1)
        half_two = first_part(samples // 2, samples - samples // 2, fcol, g2z)
        f2, b2, half_two = tie(f2, b2, half_two)
        f3, b3 = around(f2, 1), around(b2, -1)

        message, keep, kept = pl.pallas_call(
            split_kernel,
            out_shape=(shape((384, hid), F32), shape((128, hid), F32), shape((256, hid), F32)),
            in_specs=[SMEM] + [VMEM] * 3,
            out_specs=(VMEM,) * 3,
            compiler_params=params(4),
            name="split",
        )(core[None], half_one, half_two, closure)
        got = trade(message, 4)
        message, kept = pl.pallas_call(
            merge_kernel,
            out_shape=(shape((256, hid), BF16), shape((128, hid), F32)),
            in_specs=[SMEM] + [VMEM] * 3,
            out_specs=(VMEM,) * 2,
            compiler_params=params(4),
            name="merge",
        )(y[None], got, keep, kept)
        got, f3, b3 = tie(trade(message, 8), f3, b3)
        f4 = around(f3, 1)
        kept, *messages = pl.pallas_call(
            fan_kernel,
            out_shape=(shape((32, hid), F32),) + (shape((160, hid), BF16),) * 3,
            in_specs=[VMEM] * 3,
            out_specs=(VMEM,) * 4,
            compiler_params=params(4),
            name="fan",
        )(got, message, kept)
        got = [trade(message, mask) for mask, message in zip((1, 2, 3), messages)]
        own, new_fields = pl.pallas_call(
            functools.partial(total_kernel, nz),
            out_shape=(shape((128, hid), F32), shape(fields.shape, F32)),
            in_specs=[SMEM] + [VMEM] * (6 + len(sources)),
            out_specs=(VMEM,) * 2,
            compiler_params=params(6),
            name="total",
        )(near, own_state, messages[0], kept, *got, *sources)
        other = trade(own, 4)
        pieces = [piece, f1, b1, f2, b2, f3, b3, f4]
        pieces = [v[None] for v in pieces + [trade(v, 4) for v in pieces]]
    else:
        raw_first = first_part(0, samples, fcol, g2z)
        core = jnp.zeros((), jnp.int32)
        if not joined:
            raw_first = lax.psum(raw_first, "rep")
            body = lax.psum(piece[:rows].astype(F32), "rep")
            extra = lax.psum(piece[rows:].astype(F32), "rep")
            squares = jnp.sum(body * body)
            high = squares.astype(BF16).astype(F32)
            extra = extra.at[8, 0].set(high).at[8, 1].set(squares - high)
            piece = jnp.concatenate([body, extra], 0).astype(BF16)
        raw_first = lax.psum(raw_first, team)
        own, other = raw_first[:128], raw_first[128:]
        pieces = [lax.all_gather(piece, team)]
        piece_place = everyone
        part = closure.reshape(samples, n_slab, planes * 16, lanes // 2)
        part = jnp.swapaxes(part, 0, 1).reshape(size, planes * 16, lanes // 2).astype(F32)
        own_closure = lax.psum_scatter(part, team, scatter_dimension=0)
        new_fields = pl.pallas_call(
            functools.partial(step_kernel, nz),
            out_shape=shape(fields.shape, F32),
            in_specs=[SMEM] + [VMEM] * 3,
            out_specs=VMEM,
            compiler_params=params(6),
            name="step",
        )(near, own_state, own_closure, sources[0].reshape(n_slab, samples, 16, cells)[:, sample])

    weight_count = w_in.size + w_mid.size + w_out.size
    grad_middle, grad_first, grad_last = pl.pallas_call(
        functools.partial(finish_kernel, len(pieces), weight_count),
        out_shape=(shape((27, hid, hid), F32), shape((9, 27, hid), F32), shape((cout, hid), F32)),
        in_specs=[SMEM] * 2 + [VMEM] * (2 + len(pieces)),
        out_specs=(ANY, VMEM, VMEM),
        scratch_shapes=[
            pltpu.VMEM((size, rows + 16, hid), BF16),
            pltpu.VMEM((27, hid, hid), F32),
            pltpu.SemaphoreType.DMA((27,)),
        ],
        compiler_params=params(24),
        name="finish",
    )(piece_place, core[None], own, other, *pieces)
    return (new_fields, jnp.transpose(grad_first, (1, 0, 2)), grad_middle, grad_last.T)


def solution(mesh):
    placed = (
        P(("groups", "rep"), None, "slab", None, None),
        P(("groups", "rep"), "slab"),
        P(("groups", "rep"), None, "slab"),
        P(("groups", "rep"), "slab"),
        P(("groups", "rep"), "slab"),
        P(("groups", "rep"), "slab"),
        P(),
        P(),
        P(),
        P(("groups", "rep"), None, "slab", None, None),
    )
    return jax.shard_map(
        shards,
        mesh=mesh,
        in_specs=placed,
        out_specs=(
            P(("groups", "rep"), None, "slab", None, None),
            P("groups", None, None),
            P("groups", None, None),
            P("groups", None),
        ),
        check_vma=False,
    )
```

```python
import functools
import math

import jax
import jax.numpy as jnp
from jax import lax
from jax.experimental import pallas as pl
from jax.experimental.pallas import tpu as pltpu
from jax.sharding import PartitionSpec as P

dt_step = 0.2
viscosity = 0.05
drag_rate = 0.5
clip_rms = 0.5

F32 = jnp.float32
BF16 = jnp.bfloat16
offsets = [(x, y, z) for x in (-1, 0, 1) for y in (-1, 0, 1) for z in (-1, 0, 1)]


def dot(a, b):
    return lax.dot_general(a, b, (((1,), (0,)), ((), ())), preferred_element_type=F32)


def dot_nt(a, b):
    return lax.dot_general(a, b, (((1,), (1,)), ((), ())), preferred_element_type=F32)


def logistic(p):
    return 0.5 * jnp.tanh(0.5 * p) + 0.5


def roll_z(v, by, nz):
    return jnp.concatenate(
        [pltpu.roll(v[:, k : k + nz], by % nz, 1) for k in range(0, v.shape[1], nz)], 1
    )


def ahead_y(v, by, nz):
    if by == 0:
        return v
    cut = (by * nz) % v.shape[1]
    return jnp.concatenate([v[:, cut:], v[:, :cut]], 1)


def flat_cells(ref):
    planes, rows = ref.shape[2], ref.shape[3]
    return jnp.concatenate([ref[0, :, x, y, :] for x in range(planes) for y in range(rows)], 1)


def fetch(pairs, sems):
    copies = [pltpu.make_async_copy(src, dst, sems.at[i]) for i, (src, dst) in enumerate(pairs)]
    for copy in copies:
        copy.start()
    for copy in copies:
        copy.wait()


def deposit_kernel(mass_in, vel_in, cell_in, listed_in, fields_in, cotangent_in, counts, stay, up, down, *held):
    *held, sems = held
    fetch(list(zip((mass_in, vel_in, cell_in, listed_in, fields_in, cotangent_in), held)), sems)
    mass, vel, cell, listed, fields, cotangent = held
    stay[4:9] = flat_cells(fields)
    stay[9:14] = dt_step * flat_cells(cotangent)
    stay[14:] = jnp.zeros((2, stay.shape[1]), F32)
    drops = mass.shape[1]
    slots = listed.shape[1]
    half = slots // 2
    k = lax.broadcasted_iota(jnp.int32, (1, slots), 1)
    valid = k < jnp.where(k < half, counts[0, 0], half + counts[0, 1])
    chosen = jnp.where(valid, listed[...], -1)
    member = (lax.broadcasted_iota(jnp.int32, (drops, slots), 0) == chosen).astype(F32).astype(BF16)
    row = lax.broadcasted_iota(jnp.int32, (16, slots), 0)
    column = lax.broadcasted_iota(jnp.int32, (16, slots), 1)
    which = (row == (column >= half).astype(jnp.int32)).astype(F32).astype(BF16)
    mask = dot_nt(which, member)
    goes_up, goes_down = mask[0:1], mask[1:2]
    m = mass[...]
    charges = jnp.concatenate([m] + [m * vel[i] for i in range(vel.shape[0])], 0)
    high = charges.astype(BF16).astype(F32)
    both = jnp.concatenate([high, charges - high], 0)
    rows = jnp.concatenate(
        [both * (1.0 - goes_up - goes_down), both * goes_up, both * goes_down, jnp.zeros_like(both)], 0
    ).astype(BF16)
    chunk = 256
    for start in range(0, stay.shape[1], chunk):
        here = lax.broadcasted_iota(jnp.int32, (chunk, drops), 0) + start
        onehot = (here == cell[...]).astype(F32).astype(BF16)
        got = dot_nt(rows, onehot)
        for i, out in enumerate((stay, up, down)):
            out[0:4, start : start + chunk] = got[8 * i : 8 * i + 4] + got[8 * i + 4 : 8 * i + 8]


def feature_kernel(stay, below, above, feats, own):
    deposit = stay[0:4] + below[...] + above[...]
    state = stay[4:9]
    force = drag_rate * (deposit[1:4] - deposit[0:1] * state[0:3])
    own[...] = jnp.concatenate([state, force], 0)
    cells = state.shape[1]
    feats[...] = jnp.concatenate(
        [
            stay[9:14],
            force[2:3],
            jnp.zeros((2, cells), F32),
            state,
            deposit[0:1],
            force[0:2],
        ],
        0,
    ).astype(BF16)


def tap_rows():
    r = lax.broadcasted_iota(jnp.int32, (288, 256), 0)
    k = lax.broadcasted_iota(jnp.int32, (288, 256), 1)
    c, t = r >> 5, r & 31
    ox = (t >= 9).astype(jnp.int32) + (t >= 18).astype(jnp.int32)
    q = t - 9 * ox
    ninth = jnp.where(q < 8, 216 + 8 * ox + q, 240 + ox)
    at = jnp.where(c < 8, 8 * t + c, ninth)
    return ((at == k) & (t < 27)).astype(F32).astype(BF16)


def weight_kernel(me, w_in, w_mid, w_out, packed, w_back):
    hid, rows = w_back.shape
    block = rows // 27
    row = lax.broadcasted_iota(jnp.int32, (block, hid), 0)
    column = lax.broadcasted_iota(jnp.int32, (block, hid), 1)
    chosen = (column == row + me[0] * block).astype(F32).astype(BF16)
    pad = jnp.zeros((5, hid), F32)
    tall = jnp.concatenate([v for c in range(9) for v in (w_in[c].astype(F32), pad)], 0)
    packed[rows : rows + hid] = (0.5 * dot(tall.T.astype(BF16), tap_rows())).astype(BF16)
    wide = w_out[...].astype(F32)
    wide = jnp.concatenate([wide, jnp.zeros((16 - wide.shape[0], hid), F32)], 0).astype(BF16)
    both = jnp.concatenate([dot_nt(chosen, wide), dot_nt(wide, chosen)], 0)
    packed[rows + hid :] = jnp.concatenate([both, jnp.zeros((32, hid - 16), F32)], 1).astype(BF16)
    for t in range(27):
        packed[t * block : (t + 1) * block] = dot_nt(chosen, w_mid[t]).astype(BF16)
    w_back[...] = packed[0:rows].astype(F32).T.astype(BF16)


def span(x, lanes, count=1):
    return slice(x * lanes, (x + count) * lanes)


def plane_taps(g2z, x, planes, nz, lanes):
    parts = []
    for ox, oy, oz in offsets:
        parts.append(ahead_y(g2z[0, oz + 1, :, span((x - ox) % planes, lanes)], -oy, nz))
    return jnp.concatenate(parts, 0)


def closure_kernel(nz, lanes, sources, place, packed, *refs):
    arrived, refs = refs[:sources], refs[sources:]
    piece, closure, g2z, fcol, feats, fz, eighth, ninth, hidden, sums, mid, last = refs
    s = pl.program_id(0)
    samples = pl.num_programs(0)
    slabs = place.shape[0]
    cells = hidden.shape[1]
    planes = cells // lanes
    per = planes // slabs
    rows, hid = mid.shape
    block = last.shape[1]
    group = 4
    wt, w_first = packed.at[0:rows], packed.at[rows : rows + hid]
    wo = packed[rows + hid : rows + hid + 16, 0:16]
    wc = packed[rows + hid + 16 :, 0:16]

    @pl.when(s == 0)
    def _():
        mid[...] = jnp.zeros_like(mid)
        last[...] = jnp.zeros_like(last)
        at = 0
        for ref in arrived:
            feats[at : at + ref.shape[0]] = ref[...]
            at += ref.shape[0]

    sums[...] = jnp.zeros_like(sums)
    sub = lax.broadcasted_iota(jnp.int32, (8, lanes), 0)

    def spread(j):
        f = feats[place[j] + s].astype(F32)
        at = span(j, per * lanes)
        fz[0, :, at] = roll_z(f, 1, nz)
        fz[1, :, at] = f
        fz[2, :, at] = roll_z(f, -1, nz)

    for j in range(slabs):
        spread(j)

    def around(x):
        return [span((x + ox) % planes, lanes) for ox in (-1, 0, 1)]

    def ninth_rows(x):
        at = span(x, lanes)
        rows = [jnp.broadcast_to(fz[oz + 1, 5:6, at], (8, lanes)) for oz in (-1, 0, 1)]
        tile = ahead_y(rows[0], -1, nz)
        for q in range(1, 8):
            tile = jnp.where(sub == q, ahead_y(rows[q % 3], q // 3 - 1, nz), tile)
        eighth[:, at] = tile
        ninth[:, at] = ahead_y(rows[2], 1, nz)

    for x in range(planes):
        ninth_rows(x)

    def patches(x):
        near = around(x)
        pieces = [ahead_y(fz[oz + 1, 8:16, near[ox + 1]], oy, nz) for ox, oy, oz in offsets]
        pieces += [eighth[:, n] for n in near]
        tail = jnp.where(sub == 0, ninth[:, near[0]], jnp.where(sub == 1, ninth[:, near[1]], ninth[:, near[2]]))
        pieces += [jnp.where(sub < 3, tail, 0.0), jnp.zeros((8, lanes), F32)]
        fcol[0, :, near[1]] = jnp.concatenate(pieces, 0).astype(BF16)

    for x in range(planes):
        patches(x)

    def first(x):
        at = span(x, lanes)
        half = dot(w_first[...], fcol[0, :, at])
        hidden[:, at] = (half * jnp.tanh(half) + half).astype(BF16)

    for x in range(planes):
        first(x)

    def second(x):
        near = around(x)
        prod = dot(wt[...], hidden[:, near[1]])
        for ox in (-1, 0, 1):
            to = near[1 - ox]
            for oz in (-1, 0, 1):
                total = None
                for oy in (-1, 0, 1):
                    t = 9 * (ox + 1) + 3 * (oy + 1) + oz + 1
                    v = ahead_y(prod[t * block : (t + 1) * block], oy, nz)
                    total = v if total is None else total + v
                sums[oz + 1, :, to] += total

    for x in range(planes):
        second(x)

    def gradient(j):
        here = feats[place[j] + s]
        at = span(j, per * lanes)
        pre = sums[1, :, at] + roll_z(sums[0, :, at], 1, nz) + roll_z(sums[2, :, at], -1, nz)
        sig = logistic(pre)
        active = (pre * sig).astype(BF16)
        out = dot(wc, active)
        for h in range(per):
            for k in range(2):
                start = h * lanes + k * (lanes // 2)
                closure[0, j * per + h, 8 * k : 8 * k + 8] = out[0:8, start : start + lanes // 2].astype(BF16)
        grad = dot(wo, here) * (sig * (1.0 + pre * (1.0 - sig)))
        last[...] += dot_nt(here, active)
        rounded = grad.astype(BF16)
        grad = rounded.astype(F32)
        g2z[0, 0, :, at] = roll_z(grad, -1, nz).astype(BF16)
        g2z[0, 1, :, at] = rounded
        g2z[0, 2, :, at] = roll_z(grad, 1, nz).astype(BF16)

    for j in range(slabs):
        gradient(j)

    @pl.when(s >= 0)
    def _():
        for x in range(0, planes, group):
            columns = [plane_taps(g2z, x + h, planes, nz, lanes) for h in range(group)]
            mid[...] += dot_nt(jnp.concatenate(columns, 1), hidden[:, span(x, lanes, group)])

    @pl.when(s == samples - 1)
    def _():
        total = mid[...]
        taps = total.shape[0]
        piece[0:taps] = total.astype(BF16)
        squares = jnp.sum(total * total, keepdims=True)
        high = squares.astype(BF16).astype(F32)
        width = total.shape[1]
        row = lax.broadcasted_iota(jnp.int32, (block, width), 0)
        column = lax.broadcasted_iota(jnp.int32, (block, width), 1)
        extra = jnp.concatenate([last[...], jnp.zeros((block, width - block), F32)], 1)
        extra = jnp.where(row < 5, extra, 0.0)
        extra = jnp.where((row == 8) & (column == 0), high, extra)
        extra = jnp.where((row == 8) & (column == 1), squares - high, extra)
        piece[taps:] = extra.astype(BF16)


def first_kernel(nz, lanes, packed, w_back, fcol, g2z, out):
    @pl.when(pl.program_id(0) == 0)
    def _():
        out[...] = jnp.zeros_like(out)

    planes = fcol.shape[2] // lanes
    group = 2
    hid, rows = w_back.shape
    w_first = packed.at[rows : rows + hid]
    for x in range(0, planes, group):
        at = span(x, lanes, group)
        columns = [plane_taps(g2z, x + h, planes, nz, lanes) for h in range(group)]
        back = dot(w_back[...], jnp.concatenate(columns, 1))
        column = fcol[0, :, at]
        half = dot(w_first[...], column)
        double = 1.0 + jnp.tanh(half)
        grad = (back * (double * (0.5 + half - 0.5 * half * double))).astype(BF16)
        out[...] += dot_nt(column, grad)


def split_kernel(core, one, two, closure, message, keep, kept):
    half = keep.shape[0]
    mine = pl.multiple_of(core[0] * half, half)
    theirs = pl.multiple_of((1 - core[0]) * half, half)
    keep[...] = one[pl.ds(mine, half)] + two[pl.ds(mine, half)]
    message[0:half] = one[pl.ds(theirs, half)] + two[pl.ds(theirs, half)]
    samples, planes = closure.shape[:2]
    at = 0
    for s in range(samples):
        for y in range(planes // 4):
            for p in range(2):
                kept[at : at + 16] = closure[s, 4 * y + 2 * core[0] + p].astype(F32)
                message[half + at : half + at + 16] = closure[s, 4 * y + 2 * (1 - core[0]) + p].astype(F32)
                at += 16


def merge_kernel(bit, got, mine, kept, message, keep):
    half = 128
    message[0:half] = (mine[...] + got[0:half]).astype(BF16)
    for o in range(keep.shape[0] // 32):
        a = pl.multiple_of((2 * o + bit[0]) * 32, 32)
        b = pl.multiple_of((2 * o + 1 - bit[0]) * 32, 32)
        keep[o * 32 : o * 32 + 32] = kept[pl.ds(a, 32)] + got[pl.ds(half + a, 32)]
        message[half + o * 32 : half + o * 32 + 32] = (kept[pl.ds(b, 32)] + got[pl.ds(half + b, 32)]).astype(BF16)


def fan_kernel(got, mine, kept, keep, *messages):
    half = 128
    raw = (mine[0:half].astype(F32) + got[0:half].astype(F32)).astype(BF16)
    for o in range(4):
        rows = kept[o * 32 : o * 32 + 32] + got[half + o * 32 : half + o * 32 + 32].astype(F32)
        if o == 0:
            keep[...] = rows
        else:
            messages[o - 1][0:half] = raw
            messages[o - 1][half:] = rows.astype(BF16)


def step_kernel(nz, place, own, closure, *refs):
    step_fields(nz, place, own, closure[...], refs[:-1], refs[-1])


def total_kernel(mine, kept, one, two, three, half, closure):
    pair = mine[0:128].astype(F32) + one[0:128].astype(F32)
    half[...] = pair + (two[0:128].astype(F32) + three[0:128].astype(F32))
    closure[...] = kept[...] + (one[128:].astype(F32) + two[128:].astype(F32) + three[128:].astype(F32))


def step_fields(nz, place, own, closure, sources, out):
    state = own[0:5]
    cells = state.shape[1]
    planes, rows = out.shape[2], out.shape[3]
    lanes = cells // planes
    lower, upper = (sources[0][place[i] if len(sources) == 1 else 0].astype(F32) for i in range(2))
    for g in range(1, len(sources)):
        other = sources[g][0].astype(F32)
        lower, upper = (jnp.where(place[i] == g, other, v) for i, v in enumerate((lower, upper)))
    lower, upper = lower[8:13, cells - lanes :], upper[8:13, :lanes]
    wide = jnp.concatenate([lower, state, upper], 1)
    next_x, last_x = wide[:, 2 * lanes :], wide[:, :cells]
    parts = [state[:, i * lanes : (i + 1) * lanes] for i in range(planes)]
    next_y = jnp.concatenate([ahead_y(v, 1, nz) for v in parts], 1)
    last_y = jnp.concatenate([ahead_y(v, -1, nz) for v in parts], 1)
    next_z, last_z = roll_z(state, -1, nz), roll_z(state, 1, nz)
    laplace = next_x + last_x + next_y + last_y + next_z + last_z - 6.0 * state
    advect = -0.5 * (
        state[0:1] * (next_x - last_x) + state[1:2] * (next_y - last_y) + state[2:3] * (next_z - last_z)
    )
    momentum = jnp.concatenate([own[5:8], jnp.zeros((2, cells), F32)], 0)
    closed = jnp.concatenate([closure[k : k + 5] for k in range(0, closure.shape[0], 8)], 1)
    new = state + dt_step * (viscosity * laplace + advect + closed + momentum)
    for x in range(planes):
        for y in range(rows):
            at = (x * rows + y) * nz
            out[0, :, x, y, :] = new[:, at : at + nz]


def finish_kernel(count, weight_count, place, core, own, other, *refs):
    pieces, (mid_out, first_out, last_out, held, done, leave) = refs[:count], refs[count:]
    slots = held.shape[0]
    block = done.shape[1] // slots
    rows = held.shape[1] - 16
    width = done.shape[1]

    at = 0
    for ref in pieces:
        held[at : at + ref.shape[0]] = ref[...]
        at += ref.shape[0]
    a, b = own[...], other[...]
    swapped = core[0] == 1
    raw = jnp.concatenate([jnp.where(swapped, b, a), jnp.where(swapped, a, b)], 0)
    squares = jnp.sum(raw * raw, keepdims=True)
    high = raw.astype(BF16)
    ordered = dot(tap_rows(), high) + dot(tap_rows(), (raw - high.astype(F32)).astype(BF16))
    last = []
    for d in range(slots):
        extra = held[place[d], rows:].astype(F32)
        last.append(extra[0:5, 0:block])
        squares = squares + jnp.sum(extra[8:9, 0:2], keepdims=True)
    last = jnp.concatenate(last, 1)
    squares = squares + jnp.sum(last * last, keepdims=True)
    clip = jnp.minimum(1.0, clip_rms * math.sqrt(weight_count) / jnp.sqrt(squares + 1e-06))
    last_out[...] = last * clip
    ordered = ordered * clip
    for c in range(first_out.shape[0]):
        first_out[c] = ordered[32 * c : 32 * c + 27]

    eye = (
        lax.broadcasted_iota(jnp.int32, (width, width), 0) == lax.broadcasted_iota(jnp.int32, (width, width), 1)
    ).astype(F32).astype(BF16)

    def leaving(t):
        return pltpu.make_async_copy(done.at[t], mid_out.at[t], leave.at[t])

    def flip(i, carry):
        for k in range(3):
            t = 3 * i + k
            start = pl.multiple_of(t * block, block)
            flipped = jnp.concatenate([held[place[d], pl.ds(start, block)] for d in range(slots)], 0)
            done[t] = dot_nt(eye, flipped) * clip
            leaving(t).start()
        return carry

    lax.fori_loop(0, 9, flip, 0, unroll=3)
    for t in range(27):
        leaving(t).wait()


def whole_spec(shape):
    return pl.BlockSpec(shape, lambda *unused: (0,) * len(shape))


SMEM = pl.BlockSpec(memory_space=pltpu.SMEM)
VMEM = pl.BlockSpec(memory_space=pltpu.VMEM)
ANY = pl.BlockSpec(memory_space=pl.ANY)
HBM = pl.BlockSpec(memory_space=pltpu.HBM)


def cost(flops):
    return pl.CostEstimate(flops=int(flops), bytes_accessed=2**22, transcendentals=0)


def params(mebibytes):
    return pltpu.CompilerParams(vmem_limit_bytes=mebibytes * 2**20)


def shards(
    fields, drop_mass, drop_vel, drop_cell, cross_list, cross_count, w_in, w_mid, w_out, cotangent
):
    shape = jax.ShapeDtypeStruct
    n_slab, n_rep = lax.axis_size("slab"), lax.axis_size("rep")
    planes, ny, nz = fields.shape[2:]
    cells = planes * ny * nz
    lanes = ny * nz
    hid, cout = w_out.shape
    joined = n_slab * n_rep * 16 <= hid
    team = ("slab", "rep") if joined else ("slab",)
    samples = n_rep if joined else 1
    size = n_slab * samples
    block = hid // size
    fast = joined and n_slab == 4 and n_rep == 4
    slab, rep = lax.axis_index("slab"), lax.axis_index("rep")
    sample = rep if joined else jnp.zeros((), jnp.int32)
    me = slab * samples + sample
    all_planes = n_slab * planes
    everyone = jnp.arange(size, dtype=jnp.int32)

    def trade(v, mask):
        return lax.ppermute(v, team, [(d, d ^ mask) for d in range(size)])

    dense = shape((4, cells), F32)
    flows = (drop_mass, jnp.transpose(drop_vel, (1, 0, 2)), drop_cell, cross_list, fields, cotangent)
    stay, up, down = pl.pallas_call(
        deposit_kernel,
        out_shape=(shape((16, cells), F32), dense, dense),
        in_specs=[HBM] * 6 + [SMEM],
        out_specs=(VMEM,) * 3,
        scratch_shapes=[pltpu.VMEM(v.shape, v.dtype) for v in flows] + [pltpu.SemaphoreType.DMA((6,))],
        compiler_params=params(60),
        name="deposit",
    )(*flows, cross_count)
    from_below = lax.ppermute(up, "slab", [(i, (i + 1) % n_slab) for i in range(n_slab)])
    from_above = lax.ppermute(down, "slab", [((i + 1) % n_slab, i) for i in range(n_slab)])
    own_feats, own_state = pl.pallas_call(
        feature_kernel,
        out_shape=(shape((16, cells), BF16), shape((8, cells), F32)),
        in_specs=[VMEM] * 3,
        out_specs=(VMEM,) * 2,
        compiler_params=params(4),
        name="features",
    )(stay, from_below, from_above)

    rows = 27 * block
    own_feats, late_me, late_in, late_mid, late_out = lax.optimization_barrier((own_feats, me, w_in, w_mid, w_out))
    packed, w_back = pl.pallas_call(
        weight_kernel,
        out_shape=(shape((rows + hid + 32, hid), BF16), shape((hid, rows), BF16)),
        in_specs=[SMEM] + [VMEM] * 3,
        out_specs=(VMEM,) * 2,
        compiler_params=params(16),
        cost_estimate=cost(1.5e9),
        name="weights",
    )(late_me[None], jnp.transpose(late_in, (1, 0, 2)), late_mid, late_out.T)

    if fast:
        far, middle, close = (trade(own_feats, mask) for mask in (3, 2, 1))
        near_z = [close, middle, far]
        packed, w_back, *near_z = lax.optimization_barrier((packed, w_back, *near_z))
        mine = jnp.stack([own_feats] + near_z)
        across = trade(mine, 8)
        sources = [mine, across, trade(mine, 4), trade(across, 4)]

        def held_at(slabs):
            return 2 * ((slabs ^ slab) & 1) + (((slabs ^ slab) >> 1) & 1)
    else:
        sources = [lax.all_gather(own_feats, team)]

        def held_at(slabs):
            return slabs

    place = held_at(jnp.arange(n_slab, dtype=jnp.int32)) * samples
    near = held_at((slab + jnp.array([n_slab - 1, 1], jnp.int32)) % n_slab)

    team_cells = all_planes * lanes
    piece, closure, g2z, fcol = pl.pallas_call(
        functools.partial(closure_kernel, nz, lanes, len(sources)),
        grid=(samples,),
        out_shape=(
            shape((rows + 16, hid), BF16),
            shape((samples, all_planes, 16, lanes // 2), BF16),
            shape((samples, 3, block, team_cells), BF16),
            shape((samples, 256, team_cells), BF16),
        ),
        in_specs=[SMEM] + [VMEM] * (1 + len(sources)),
        out_specs=(
            whole_spec((rows + 16, hid)),
            pl.BlockSpec((1, all_planes, 16, lanes // 2), lambda s: (s, 0, 0, 0)),
            pl.BlockSpec((1, 3, block, team_cells), lambda s: (s, 0, 0, 0)),
            pl.BlockSpec((1, 256, team_cells), lambda s: (s, 0, 0)),
        ),
        scratch_shapes=[
            pltpu.VMEM((size, 16, cells), BF16),
            pltpu.VMEM((3, 16, team_cells), F32),
            pltpu.VMEM((8, team_cells), F32),
            pltpu.VMEM((8, team_cells), F32),
            pltpu.VMEM((hid, team_cells), BF16),
            pltpu.VMEM((3, block, team_cells), F32),
            pltpu.VMEM((rows, hid), F32),
            pltpu.VMEM((16, block), F32),
        ],
        compiler_params=params(30 if all_planes <= 8 else 58),
        cost_estimate=cost(9e9),
        name="closure",
    )(place, packed, *sources)

    def first_part(lo, count, fcol, g2z):
        return pl.pallas_call(
            functools.partial(first_kernel, nz, lanes),
            grid=(count,),
            out_shape=shape((256, hid), F32),
            in_specs=[
                whole_spec(packed.shape),
                whole_spec((hid, rows)),
                pl.BlockSpec((1, 256, team_cells), lambda s: (s + lo, 0, 0)),
                pl.BlockSpec((1, 3, block, team_cells), lambda s: (s + lo, 0, 0, 0)),
            ],
            out_specs=whole_spec((256, hid)),
            compiler_params=params(18 if all_planes <= 8 else 58),
            cost_estimate=cost(7.6e9 * count / samples),
            name="first",
        )(packed, w_back, fcol, g2z)

    if fast:
        core, y = slab & 1, slab >> 1

        def chip(at):
            at = at % 8
            return (0, at) if at < 4 else (1, 7 - at)

        def device(at, c):
            y, z = chip(at)
            return (2 * y + c) * n_rep + z

        def around(v, by):
            return lax.ppermute(v, team, [(device(at, c), device(at + by, c)) for at in range(8) for c in range(2)])

        def tie(*values):
            return lax.optimization_barrier(values)

        position = jnp.where(y == 0, rep, 7 - rep)
        theirs, their_z = everyone // n_rep, everyone % n_rep
        apart = (jnp.where(theirs < 2, their_z, 7 - their_z) - position) % 8
        piece_place = jnp.where(apart < 4, 2 * apart, 2 * (8 - apart) - 1)
        piece_place = jnp.where(apart == 0, 0, piece_place) + 8 * ((theirs ^ slab) & 1)
        piece_place = piece_place.astype(jnp.int32)
        f1, b1 = around(piece, 1), around(piece, -1)
        half_one = first_part(0, samples // 2, fcol, g2z)
        f1, b1, half_one, fcol, g2z, piece_place, near = tie(f1, b1, half_one, fcol, g2z, piece_place, near)
        f2, b2 = around(f1, 1), around(b1, -1)
        half_two = first_part(samples // 2, samples - samples // 2, fcol, g2z)
        f2, b2, half_two = tie(f2, b2, half_two)
        f3, b3 = around(f2, 1), around(b2, -1)

        message, keep, kept = pl.pallas_call(
            split_kernel,
            out_shape=(shape((384, hid), F32), shape((128, hid), F32), shape((256, hid), F32)),
            in_specs=[SMEM] + [VMEM] * 3,
            out_specs=(VMEM,) * 3,
            compiler_params=params(4),
            name="split",
        )(core[None], half_one, half_two, closure)
        got = trade(message, 4)
        message, kept = pl.pallas_call(
            merge_kernel,
            out_shape=(shape((256, hid), BF16), shape((128, hid), F32)),
            in_specs=[SMEM] + [VMEM] * 3,
            out_specs=(VMEM,) * 2,
            compiler_params=params(4),
            name="merge",
        )(y[None], got, keep, kept)
        got = trade(message, 8)
        f4 = around(f3, 1)
        kept, *messages = pl.pallas_call(
            fan_kernel,
            out_shape=(shape((32, hid), F32),) + (shape((160, hid), BF16),) * 3,
            in_specs=[VMEM] * 3,
            out_specs=(VMEM,) * 4,
            compiler_params=params(4),
            name="fan",
        )(got, message, kept)
        got = [trade(message, mask) for mask, message in zip((1, 2, 3), messages)]
        own, own_closure = pl.pallas_call(
            total_kernel,
            out_shape=(shape((128, hid), F32), shape((32, hid), F32)),
            in_specs=[VMEM] * 5,
            out_specs=(VMEM,) * 2,
            compiler_params=params(4),
            name="total",
        )(messages[0], kept, *got)
        other = trade(own, 4)
        halo = sources
        pieces = [piece, f1, b1, f2, b2, f3, b3, f4]
        pieces = [v[None] for v in pieces + [trade(v, 4) for v in pieces]]
    else:
        raw_first = first_part(0, samples, fcol, g2z)
        core = jnp.zeros((), jnp.int32)
        if not joined:
            raw_first = lax.psum(raw_first, "rep")
            body = lax.psum(piece[:rows].astype(F32), "rep")
            extra = lax.psum(piece[rows:].astype(F32), "rep")
            squares = jnp.sum(body * body)
            high = squares.astype(BF16).astype(F32)
            extra = extra.at[8, 0].set(high).at[8, 1].set(squares - high)
            piece = jnp.concatenate([body, extra], 0).astype(BF16)
        raw_first = lax.psum(raw_first, team)
        own, other = raw_first[:128], raw_first[128:]
        pieces = [lax.all_gather(piece, team)]
        piece_place = everyone
        part = closure.reshape(samples, n_slab, planes * 16, lanes // 2)
        part = jnp.swapaxes(part, 0, 1).reshape(size, planes * 16, lanes // 2).astype(F32)
        own_closure = lax.psum_scatter(part, team, scatter_dimension=0)
        halo = [sources[0].reshape(n_slab, samples, 16, cells)[:, sample]]
    new_fields = pl.pallas_call(
        functools.partial(step_kernel, nz),
        out_shape=shape(fields.shape, F32),
        in_specs=[SMEM] + [VMEM] * (2 + len(halo)),
        out_specs=VMEM,
        compiler_params=params(6),
        name="step",
    )(near, own_state, own_closure, *halo)

    weight_count = w_in.size + w_mid.size + w_out.size
    grad_middle, grad_first, grad_last = pl.pallas_call(
        functools.partial(finish_kernel, len(pieces), weight_count),
        out_shape=(shape((27, hid, hid), F32), shape((9, 27, hid), F32), shape((cout, hid), F32)),
        in_specs=[SMEM] * 2 + [VMEM] * (2 + len(pieces)),
        out_specs=(ANY, VMEM, VMEM),
        scratch_shapes=[
            pltpu.VMEM((size, rows + 16, hid), BF16),
            pltpu.VMEM((27, hid, hid), F32),
            pltpu.SemaphoreType.DMA((27,)),
        ],
        compiler_params=params(24),
        name="finish",
    )(piece_place, core[None], own, other, *pieces)
    return (new_fields, jnp.transpose(grad_first, (1, 0, 2)), grad_middle, grad_last.T)


def solution(mesh):
    placed = (
        P(("groups", "rep"), None, "slab", None, None),
        P(("groups", "rep"), "slab"),
        P(("groups", "rep"), None, "slab"),
        P(("groups", "rep"), "slab"),
        P(("groups", "rep"), "slab"),
        P(("groups", "rep"), "slab"),
        P(),
        P(),
        P(),
        P(("groups", "rep"), None, "slab", None, None),
    )
    return jax.shard_map(
        shards,
        mesh=mesh,
        in_specs=placed,
        out_specs=(
            P(("groups", "rep"), None, "slab", None, None),
            P("groups", None, None),
            P("groups", None, None),
            P("groups", None),
        ),
        check_vma=False,
    )
```

```python
import functools
import math

import jax
import jax.numpy as jnp
from jax import lax
from jax.experimental import pallas as pl
from jax.experimental.pallas import tpu as pltpu
from jax.sharding import PartitionSpec as P

dt_step = 0.2
viscosity = 0.05
drag_rate = 0.5
clip_rms = 0.5

F32 = jnp.float32
BF16 = jnp.bfloat16
offsets = [(x, y, z) for x in (-1, 0, 1) for y in (-1, 0, 1) for z in (-1, 0, 1)]


def dot(a, b):
    return lax.dot_general(a, b, (((1,), (0,)), ((), ())), preferred_element_type=F32)


def dot_nt(a, b):
    return lax.dot_general(a, b, (((1,), (1,)), ((), ())), preferred_element_type=F32)


def logistic(p):
    return 0.5 * jnp.tanh(0.5 * p) + 0.5


def roll_z(v, by, nz):
    return jnp.concatenate(
        [pltpu.roll(v[:, k : k + nz], by % nz, 1) for k in range(0, v.shape[1], nz)], 1
    )


def ahead_y(v, by, nz):
    if by == 0:
        return v
    cut = (by * nz) % v.shape[1]
    return jnp.concatenate([v[:, cut:], v[:, :cut]], 1)


def flat_cells(ref):
    planes, rows = ref.shape[2], ref.shape[3]
    return jnp.concatenate([ref[0, :, x, y, :] for x in range(planes) for y in range(rows)], 1)


def deposit_kernel(mass_in, vel_in, cell_in, listed_in, fields_in, cotangent_in, counts, stay, up, down, *held):
    *held, sems = held
    sources = (mass_in, vel_in, cell_in, listed_in, fields_in, cotangent_in)
    copies = [pltpu.make_async_copy(src, dst, sems.at[i]) for i, (src, dst) in enumerate(zip(sources, held))]
    for copy in copies:
        copy.start()
    mass, vel, cell, listed, fields, cotangent = held
    for copy in copies[:4]:
        copy.wait()
    drops = mass.shape[1]
    slots = listed.shape[1]
    half = slots // 2
    k = lax.broadcasted_iota(jnp.int32, (1, slots), 1)
    valid = k < jnp.where(k < half, counts[0, 0], half + counts[0, 1])
    chosen = jnp.where(valid, listed[...], -1)
    member = (lax.broadcasted_iota(jnp.int32, (drops, slots), 0) == chosen).astype(F32).astype(BF16)
    row = lax.broadcasted_iota(jnp.int32, (16, slots), 0)
    column = lax.broadcasted_iota(jnp.int32, (16, slots), 1)
    which = (row == (column >= half).astype(jnp.int32)).astype(F32).astype(BF16)
    mask = dot_nt(which, member)
    goes_up, goes_down = mask[0:1], mask[1:2]
    m = mass[...]
    charges = jnp.concatenate([m] + [m * vel[i] for i in range(vel.shape[0])], 0)
    high = charges.astype(BF16).astype(F32)
    both = jnp.concatenate([high, charges - high], 0)
    rows = jnp.concatenate(
        [both * (1.0 - goes_up - goes_down), both * goes_up, both * goes_down, jnp.zeros_like(both)], 0
    ).astype(BF16)
    chunk = 256
    for start in range(0, stay.shape[1], chunk):
        here = lax.broadcasted_iota(jnp.int32, (chunk, drops), 0) + start
        onehot = (here == cell[...]).astype(F32).astype(BF16)
        got = dot_nt(rows, onehot)
        for i, out in enumerate((stay, up, down)):
            out[0:4, start : start + chunk] = got[8 * i : 8 * i + 4] + got[8 * i + 4 : 8 * i + 8]
    for copy in copies[4:]:
        copy.wait()
    stay[4:9] = flat_cells(fields)
    stay[9:14] = dt_step * flat_cells(cotangent)
    stay[14:] = jnp.zeros((2, stay.shape[1]), F32)


def hold_kernel(values, out):
    out[...] = values[...]


def feature_kernel(stay, below, above, feats, own):
    deposit = stay[0:4] + below[...] + above[...]
    state = stay[4:9]
    force = drag_rate * (deposit[1:4] - deposit[0:1] * state[0:3])
    own[...] = jnp.concatenate([state, force], 0)
    cells = state.shape[1]
    feats[...] = jnp.concatenate(
        [
            stay[9:14],
            force[2:3],
            jnp.zeros((2, cells), F32),
            state,
            deposit[0:1],
            force[0:2],
        ],
        0,
    ).astype(BF16)


def tap_rows():
    r = lax.broadcasted_iota(jnp.int32, (288, 256), 0)
    k = lax.broadcasted_iota(jnp.int32, (288, 256), 1)
    c, t = r >> 5, r & 31
    ox = (t >= 9).astype(jnp.int32) + (t >= 18).astype(jnp.int32)
    q = t - 9 * ox
    ninth = jnp.where(q < 8, 216 + 8 * ox + q, 240 + ox)
    at = jnp.where(c < 8, 8 * t + c, ninth)
    return ((at == k) & (t < 27)).astype(F32).astype(BF16)


def chosen_columns(me, block, hid):
    row = lax.broadcasted_iota(jnp.int32, (block, hid), 0)
    column = lax.broadcasted_iota(jnp.int32, (block, hid), 1)
    return (column == row + me[0] * block).astype(F32).astype(BF16)


def outer_weight_kernel(me, w_in, w_out, packed):
    hid = packed.shape[1]
    pad = jnp.zeros((5, hid), F32)
    tall = jnp.concatenate([v for c in range(9) for v in (w_in[c].astype(F32), pad)], 0)
    packed[0:hid] = (0.5 * dot(tall.T.astype(BF16), tap_rows())).astype(BF16)
    wide = w_out[...].astype(F32)
    wide = jnp.concatenate([wide, jnp.zeros((16 - wide.shape[0], hid), F32)], 0).astype(BF16)
    chosen = chosen_columns(me, 16, hid)
    both = jnp.concatenate([dot_nt(chosen, wide), dot_nt(wide, chosen)], 0)
    packed[hid:] = jnp.concatenate([both, jnp.zeros((32, hid - 16), F32)], 1).astype(BF16)


def middle_weight_kernel(me, w_mid, wt, w_back):
    rows, hid = wt.shape
    block = rows // 27
    chosen = chosen_columns(me, block, hid)
    for t in range(27):
        wt[t * block : (t + 1) * block] = dot_nt(chosen, w_mid[t]).astype(BF16)
    w_back[...] = wt[...].astype(F32).T.astype(BF16)


def span(x, lanes, count=1):
    return slice(x * lanes, (x + count) * lanes)


def plane_taps(g2z, x, planes, nz, lanes):
    parts = []
    for ox, oy, oz in offsets:
        parts.append(ahead_y(g2z[0, oz + 1, :, span((x - ox) % planes, lanes)], -oy, nz))
    return jnp.concatenate(parts, 0)


def closure_kernel(nz, lanes, sources, place, wt, packed, *refs):
    arrived, refs = refs[:sources], refs[sources:]
    piece, closure, g2z, fcol, feats, fz, eighth, ninth, hidden, sums, mid, last = refs
    s = pl.program_id(0)
    samples = pl.num_programs(0)
    slabs = place.shape[0]
    cells = hidden.shape[1]
    planes = cells // lanes
    per = planes // slabs
    block = last.shape[1]
    group = 4
    hid = mid.shape[1]
    w_first = packed.at[0:hid]
    wo = packed[hid : hid + 16, 0:16]
    wc = packed[hid + 16 :, 0:16]

    @pl.when(s == 0)
    def _():
        mid[...] = jnp.zeros_like(mid)
        last[...] = jnp.zeros_like(last)
        at = 0
        for ref in arrived:
            feats[at : at + ref.shape[0]] = ref[...]
            at += ref.shape[0]

    sums[...] = jnp.zeros_like(sums)
    sub = lax.broadcasted_iota(jnp.int32, (8, lanes), 0)

    def spread(j):
        f = feats[place[j] + s].astype(F32)
        at = span(j, per * lanes)
        fz[0, :, at] = roll_z(f, 1, nz)
        fz[1, :, at] = f
        fz[2, :, at] = roll_z(f, -1, nz)

    for j in range(slabs):
        spread(j)

    def around(x):
        return [span((x + ox) % planes, lanes) for ox in (-1, 0, 1)]

    def ninth_rows(x):
        at = span(x, lanes)
        rows = [jnp.broadcast_to(fz[oz + 1, 5:6, at], (8, lanes)) for oz in (-1, 0, 1)]
        tile = ahead_y(rows[0], -1, nz)
        for q in range(1, 8):
            tile = jnp.where(sub == q, ahead_y(rows[q % 3], q // 3 - 1, nz), tile)
        eighth[:, at] = tile
        ninth[:, at] = ahead_y(rows[2], 1, nz)

    for x in range(planes):
        ninth_rows(x)

    def patches(x):
        near = around(x)
        pieces = [ahead_y(fz[oz + 1, 8:16, near[ox + 1]], oy, nz) for ox, oy, oz in offsets]
        pieces += [eighth[:, n] for n in near]
        tail = jnp.where(sub == 0, ninth[:, near[0]], jnp.where(sub == 1, ninth[:, near[1]], ninth[:, near[2]]))
        pieces += [jnp.where(sub < 3, tail, 0.0), jnp.zeros((8, lanes), F32)]
        fcol[0, :, near[1]] = jnp.concatenate(pieces, 0).astype(BF16)

    for x in range(planes):
        patches(x)

    def first(x):
        at = span(x, lanes)
        half = dot(w_first[...], fcol[0, :, at])
        hidden[:, at] = (half * jnp.tanh(half) + half).astype(BF16)

    for x in range(planes):
        first(x)

    def second(x):
        near = around(x)
        prod = dot(wt[...], hidden[:, near[1]])
        for ox in (-1, 0, 1):
            to = near[1 - ox]
            for oz in (-1, 0, 1):
                total = None
                for oy in (-1, 0, 1):
                    t = 9 * (ox + 1) + 3 * (oy + 1) + oz + 1
                    v = ahead_y(prod[t * block : (t + 1) * block], oy, nz)
                    total = v if total is None else total + v
                sums[oz + 1, :, to] += total

    for x in range(planes):
        second(x)

    def gradient(j):
        here = feats[place[j] + s]
        at = span(j, per * lanes)
        pre = sums[1, :, at] + roll_z(sums[0, :, at], 1, nz) + roll_z(sums[2, :, at], -1, nz)
        sig = logistic(pre)
        active = (pre * sig).astype(BF16)
        out = dot(wc, active)
        for h in range(per):
            for k in range(2):
                start = h * lanes + k * (lanes // 2)
                closure[0, j * per + h, 8 * k : 8 * k + 8] = out[0:8, start : start + lanes // 2].astype(BF16)
        grad = dot(wo, here) * (sig * (1.0 + pre * (1.0 - sig)))
        last[...] += dot_nt(here, active)
        rounded = grad.astype(BF16)
        grad = rounded.astype(F32)
        g2z[0, 0, :, at] = roll_z(grad, -1, nz).astype(BF16)
        g2z[0, 1, :, at] = rounded
        g2z[0, 2, :, at] = roll_z(grad, 1, nz).astype(BF16)

    for j in range(slabs):
        gradient(j)

    @pl.when(s >= 0)
    def _():
        for x in range(0, planes, group):
            columns = [plane_taps(g2z, x + h, planes, nz, lanes) for h in range(group)]
            mid[...] += dot_nt(jnp.concatenate(columns, 1), hidden[:, span(x, lanes, group)])

    @pl.when(s == samples - 1)
    def _():
        total = mid[...]
        taps = total.shape[0]
        piece[0:taps] = total.astype(BF16)
        squares = jnp.sum(total * total, keepdims=True)
        high = squares.astype(BF16).astype(F32)
        width = total.shape[1]
        row = lax.broadcasted_iota(jnp.int32, (block, width), 0)
        column = lax.broadcasted_iota(jnp.int32, (block, width), 1)
        extra = jnp.concatenate([last[...], jnp.zeros((block, width - block), F32)], 1)
        extra = jnp.where(row < 5, extra, 0.0)
        extra = jnp.where((row == 8) & (column == 0), high, extra)
        extra = jnp.where((row == 8) & (column == 1), squares - high, extra)
        piece[taps:] = extra.astype(BF16)


def first_kernel(nz, lanes, packed, w_back, fcol, g2z, out):
    @pl.when(pl.program_id(0) == 0)
    def _():
        out[...] = jnp.zeros_like(out)

    planes = fcol.shape[2] // lanes
    group = 2
    w_first = packed.at[0 : w_back.shape[0]]
    for x in range(0, planes, group):
        at = span(x, lanes, group)
        columns = [plane_taps(g2z, x + h, planes, nz, lanes) for h in range(group)]
        back = dot(w_back[...], jnp.concatenate(columns, 1))
        column = fcol[0, :, at]
        half = dot(w_first[...], column)
        double = 1.0 + jnp.tanh(half)
        grad = (back * (double * (0.5 + half - 0.5 * half * double))).astype(BF16)
        out[...] += dot_nt(column, grad)


def split_kernel(core, one, two, closure, message, keep, kept):
    half = keep.shape[0]
    mine = pl.multiple_of(core[0] * half, half)
    theirs = pl.multiple_of((1 - core[0]) * half, half)
    keep[...] = one[pl.ds(mine, half)] + two[pl.ds(mine, half)]
    message[0:half] = one[pl.ds(theirs, half)] + two[pl.ds(theirs, half)]
    samples, planes = closure.shape[:2]
    at = 0
    for s in range(samples):
        for y in range(planes // 4):
            for p in range(2):
                kept[at : at + 16] = closure[s, 4 * y + 2 * core[0] + p].astype(F32)
                message[half + at : half + at + 16] = closure[s, 4 * y + 2 * (1 - core[0]) + p].astype(F32)
                at += 16


def merge_kernel(bit, got, mine, kept, message, keep):
    half = 128
    message[0:half] = (mine[...] + got[0:half]).astype(BF16)
    for o in range(keep.shape[0] // 32):
        a = pl.multiple_of((2 * o + bit[0]) * 32, 32)
        b = pl.multiple_of((2 * o + 1 - bit[0]) * 32, 32)
        keep[o * 32 : o * 32 + 32] = kept[pl.ds(a, 32)] + got[pl.ds(half + a, 32)]
        message[half + o * 32 : half + o * 32 + 32] = (kept[pl.ds(b, 32)] + got[pl.ds(half + b, 32)]).astype(BF16)


def fan_kernel(got, mine, kept, keep, *messages):
    half = 128
    raw = (mine[0:half].astype(F32) + got[0:half].astype(F32)).astype(BF16)
    for o in range(4):
        rows = kept[o * 32 : o * 32 + 32] + got[half + o * 32 : half + o * 32 + 32].astype(F32)
        if o == 0:
            keep[...] = rows
        else:
            messages[o - 1][0:half] = raw
            messages[o - 1][half:] = rows.astype(BF16)


def step_kernel(nz, place, own, closure, *refs):
    step_fields(nz, place, own, closure[...], refs[:-1], refs[-1])


def total_kernel(mine, kept, one, two, three, half, closure):
    pair = mine[0:128].astype(F32) + one[0:128].astype(F32)
    half[...] = pair + (two[0:128].astype(F32) + three[0:128].astype(F32))
    closure[...] = kept[...] + (one[128:].astype(F32) + two[128:].astype(F32) + three[128:].astype(F32))


def step_fields(nz, place, own, closure, sources, out):
    state = own[0:5]
    cells = state.shape[1]
    planes, rows = out.shape[2], out.shape[3]
    lanes = cells // planes
    lower, upper = (sources[0][place[i] if len(sources) == 1 else 0].astype(F32) for i in range(2))
    for g in range(1, len(sources)):
        other = sources[g][0].astype(F32)
        lower, upper = (jnp.where(place[i] == g, other, v) for i, v in enumerate((lower, upper)))
    lower, upper = lower[8:13, cells - lanes :], upper[8:13, :lanes]
    wide = jnp.concatenate([lower, state, upper], 1)
    next_x, last_x = wide[:, 2 * lanes :], wide[:, :cells]
    parts = [state[:, i * lanes : (i + 1) * lanes] for i in range(planes)]
    next_y = jnp.concatenate([ahead_y(v, 1, nz) for v in parts], 1)
    last_y = jnp.concatenate([ahead_y(v, -1, nz) for v in parts], 1)
    next_z, last_z = roll_z(state, -1, nz), roll_z(state, 1, nz)
    laplace = next_x + last_x + next_y + last_y + next_z + last_z - 6.0 * state
    advect = -0.5 * (
        state[0:1] * (next_x - last_x) + state[1:2] * (next_y - last_y) + state[2:3] * (next_z - last_z)
    )
    momentum = jnp.concatenate([own[5:8], jnp.zeros((2, cells), F32)], 0)
    closed = jnp.concatenate([closure[k : k + 5] for k in range(0, closure.shape[0], 8)], 1)
    new = state + dt_step * (viscosity * laplace + advect + closed + momentum)
    for x in range(planes):
        for y in range(rows):
            at = (x * rows + y) * nz
            out[0, :, x, y, :] = new[:, at : at + nz]


def finish_kernel(count, weight_count, place, core, own, other, *refs):
    pieces, (mid_out, first_out, last_out, held, done, leave) = refs[:count], refs[count:]
    slots = held.shape[0]
    block = done.shape[1] // slots
    rows = held.shape[1] - 16
    width = done.shape[1]

    at = 0
    for ref in pieces:
        held[at : at + ref.shape[0]] = ref[...]
        at += ref.shape[0]
    a, b = own[...], other[...]
    swapped = core[0] == 1
    raw = jnp.concatenate([jnp.where(swapped, b, a), jnp.where(swapped, a, b)], 0)
    squares = jnp.sum(raw * raw, keepdims=True)
    high = raw.astype(BF16)
    ordered = dot(tap_rows(), high) + dot(tap_rows(), (raw - high.astype(F32)).astype(BF16))
    last = []
    for d in range(slots):
        extra = held[place[d], rows:].astype(F32)
        last.append(extra[0:5, 0:block])
        squares = squares + jnp.sum(extra[8:9, 0:2], keepdims=True)
    last = jnp.concatenate(last, 1)
    squares = squares + jnp.sum(last * last, keepdims=True)
    clip = jnp.minimum(1.0, clip_rms * math.sqrt(weight_count) / jnp.sqrt(squares + 1e-06))
    last_out[...] = last * clip
    ordered = ordered * clip
    for c in range(first_out.shape[0]):
        first_out[c] = ordered[32 * c : 32 * c + 27]

    eye = (
        lax.broadcasted_iota(jnp.int32, (width, width), 0) == lax.broadcasted_iota(jnp.int32, (width, width), 1)
    ).astype(F32).astype(BF16)

    def leaving(t):
        return pltpu.make_async_copy(done.at[t], mid_out.at[t], leave.at[t])

    def flip(i, carry):
        for k in range(3):
            t = 3 * i + k
            start = pl.multiple_of(t * block, block)
            flipped = jnp.concatenate([held[place[d], pl.ds(start, block)] for d in range(slots)], 0)
            done[t] = dot_nt(eye, flipped) * clip
            leaving(t).start()
        return carry

    lax.fori_loop(0, 9, flip, 0, unroll=3)
    for t in range(27):
        leaving(t).wait()


def whole_spec(shape):
    return pl.BlockSpec(shape, lambda *unused: (0,) * len(shape))


SMEM = pl.BlockSpec(memory_space=pltpu.SMEM)
VMEM = pl.BlockSpec(memory_space=pltpu.VMEM)
ANY = pl.BlockSpec(memory_space=pl.ANY)
HBM = pl.BlockSpec(memory_space=pltpu.HBM)


def cost(flops):
    return pl.CostEstimate(flops=int(flops), bytes_accessed=2**22, transcendentals=0)


def params(mebibytes):
    return pltpu.CompilerParams(vmem_limit_bytes=mebibytes * 2**20)


def shards(
    fields, drop_mass, drop_vel, drop_cell, cross_list, cross_count, w_in, w_mid, w_out, cotangent
):
    shape = jax.ShapeDtypeStruct
    n_slab, n_rep = lax.axis_size("slab"), lax.axis_size("rep")
    planes, ny, nz = fields.shape[2:]
    cells = planes * ny * nz
    lanes = ny * nz
    hid, cout = w_out.shape
    joined = n_slab * n_rep * 16 <= hid
    team = ("slab", "rep") if joined else ("slab",)
    samples = n_rep if joined else 1
    size = n_slab * samples
    block = hid // size
    fast = joined and n_slab == 4 and n_rep == 4
    slab, rep = lax.axis_index("slab"), lax.axis_index("rep")
    sample = rep if joined else jnp.zeros((), jnp.int32)
    me = slab * samples + sample
    all_planes = n_slab * planes
    everyone = jnp.arange(size, dtype=jnp.int32)

    def trade(v, mask):
        return lax.ppermute(v, team, [(d, d ^ mask) for d in range(size)])

    dense = shape((4, cells), F32)
    flows = (drop_mass, jnp.transpose(drop_vel, (1, 0, 2)), drop_cell, cross_list, fields, cotangent)
    stay, up, down = pl.pallas_call(
        deposit_kernel,
        out_shape=(shape((16, cells), F32), dense, dense),
        in_specs=[HBM] * 6 + [SMEM],
        out_specs=(VMEM,) * 3,
        scratch_shapes=[pltpu.VMEM(v.shape, v.dtype) for v in flows] + [pltpu.SemaphoreType.DMA((6,))],
        compiler_params=params(60),
        name="deposit",
    )(*flows, cross_count)
    stay = pl.pallas_call(
        hold_kernel,
        out_shape=shape(stay.shape, F32),
        in_specs=[VMEM],
        out_specs=VMEM,
        compiler_params=params(4),
        name="hold",
    )(stay)
    from_below = lax.ppermute(up, "slab", [(i, (i + 1) % n_slab) for i in range(n_slab)])
    from_above = lax.ppermute(down, "slab", [((i + 1) % n_slab, i) for i in range(n_slab)])
    own_feats, own_state = pl.pallas_call(
        feature_kernel,
        out_shape=(shape((16, cells), BF16), shape((8, cells), F32)),
        in_specs=[VMEM] * 3,
        out_specs=(VMEM,) * 2,
        compiler_params=params(4),
        name="features",
    )(stay, from_below, from_above)

    rows = 27 * block
    own_feats, late_me, late_in, late_out = lax.optimization_barrier((own_feats, me, w_in, w_out))
    packed = pl.pallas_call(
        outer_weight_kernel,
        out_shape=shape((hid + 32, hid), BF16),
        in_specs=[SMEM] + [VMEM] * 2,
        out_specs=VMEM,
        compiler_params=params(8),
        name="outer_weights",
    )(late_me[None], jnp.transpose(late_in, (1, 0, 2)), late_out.T)

    if fast:
        far, middle, close = (trade(own_feats, mask) for mask in (3, 2, 1))
        near_z = [close, middle, far]
        packed, *near_z = lax.optimization_barrier((packed, *near_z))
        mine = jnp.stack([own_feats] + near_z)
        mine, late_me, late_mid = lax.optimization_barrier((mine, me, w_mid))
        across = trade(mine, 8)

        def held_at(slabs):
            return 2 * ((slabs ^ slab) & 1) + (((slabs ^ slab) >> 1) & 1)
    else:
        sources = [lax.all_gather(own_feats, team)]
        late_me, late_mid = me, w_mid

        def held_at(slabs):
            return slabs

    wt, w_back = pl.pallas_call(
        middle_weight_kernel,
        out_shape=(shape((rows, hid), BF16), shape((hid, rows), BF16)),
        in_specs=[SMEM, VMEM],
        out_specs=(VMEM,) * 2,
        compiler_params=params(16),
        cost_estimate=cost(1.5e9),
        name="middle_weights",
    )(late_me[None], late_mid)
    if fast:
        across, wt, w_back = lax.optimization_barrier((across, wt, w_back))
        sources = [mine, across, trade(mine, 4), trade(across, 4)]
    place = held_at(jnp.arange(n_slab, dtype=jnp.int32)) * samples
    near = held_at((slab + jnp.array([n_slab - 1, 1], jnp.int32)) % n_slab)

    team_cells = all_planes * lanes
    piece, closure, g2z, fcol = pl.pallas_call(
        functools.partial(closure_kernel, nz, lanes, len(sources)),
        grid=(samples,),
        out_shape=(
            shape((rows + 16, hid), BF16),
            shape((samples, all_planes, 16, lanes // 2), BF16),
            shape((samples, 3, block, team_cells), BF16),
            shape((samples, 256, team_cells), BF16),
        ),
        in_specs=[SMEM] + [VMEM] * (2 + len(sources)),
        out_specs=(
            whole_spec((rows + 16, hid)),
            pl.BlockSpec((1, all_planes, 16, lanes // 2), lambda s: (s, 0, 0, 0)),
            pl.BlockSpec((1, 3, block, team_cells), lambda s: (s, 0, 0, 0)),
            pl.BlockSpec((1, 256, team_cells), lambda s: (s, 0, 0)),
        ),
        scratch_shapes=[
            pltpu.VMEM((size, 16, cells), BF16),
            pltpu.VMEM((3, 16, team_cells), F32),
            pltpu.VMEM((8, team_cells), F32),
            pltpu.VMEM((8, team_cells), F32),
            pltpu.VMEM((hid, team_cells), BF16),
            pltpu.VMEM((3, block, team_cells), F32),
            pltpu.VMEM((rows, hid), F32),
            pltpu.VMEM((16, block), F32),
        ],
        compiler_params=params(30 if all_planes <= 8 else 58),
        cost_estimate=cost(9e9),
        name="closure",
    )(place, wt, packed, *sources)

    def first_part(lo, count, fcol, g2z):
        return pl.pallas_call(
            functools.partial(first_kernel, nz, lanes),
            grid=(count,),
            out_shape=shape((256, hid), F32),
            in_specs=[
                whole_spec(packed.shape),
                whole_spec((hid, rows)),
                pl.BlockSpec((1, 256, team_cells), lambda s: (s + lo, 0, 0)),
                pl.BlockSpec((1, 3, block, team_cells), lambda s: (s + lo, 0, 0, 0)),
            ],
            out_specs=whole_spec((256, hid)),
            compiler_params=params(18 if all_planes <= 8 else 58),
            cost_estimate=cost(7.6e9 * count / samples),
            name="first",
        )(packed, w_back, fcol, g2z)

    if fast:
        core, y = slab & 1, slab >> 1

        def chip(at):
            at = at % 8
            return (0, at) if at < 4 else (1, 7 - at)

        def device(at, c):
            y, z = chip(at)
            return (2 * y + c) * n_rep + z

        def around(v, by):
            return lax.ppermute(v, team, [(device(at, c), device(at + by, c)) for at in range(8) for c in range(2)])

        def tie(*values):
            return lax.optimization_barrier(values)

        position = jnp.where(y == 0, rep, 7 - rep)
        theirs, their_z = everyone // n_rep, everyone % n_rep
        apart = (jnp.where(theirs < 2, their_z, 7 - their_z) - position) % 8
        piece_place = jnp.where(apart < 4, 2 * apart, 2 * (8 - apart) - 1)
        piece_place = jnp.where(apart == 0, 0, piece_place) + 8 * ((theirs ^ slab) & 1)
        piece_place = piece_place.astype(jnp.int32)
        f1, b1 = around(piece, 1), around(piece, -1)
        half_one = first_part(0, samples // 2, fcol, g2z)
        f1, b1, half_one, fcol, g2z, piece_place, near = tie(f1, b1, half_one, fcol, g2z, piece_place, near)
        f2, b2 = around(f1, 1), around(b1, -1)
        half_two = first_part(samples // 2, samples - samples // 2, fcol, g2z)
        f2, b2, half_two = tie(f2, b2, half_two)
        f3, b3 = around(f2, 1), around(b2, -1)

        message, keep, kept = pl.pallas_call(
            split_kernel,
            out_shape=(shape((384, hid), F32), shape((128, hid), F32), shape((256, hid), F32)),
            in_specs=[SMEM] + [VMEM] * 3,
            out_specs=(VMEM,) * 3,
            compiler_params=params(4),
            name="split",
        )(core[None], half_one, half_two, closure)
        got = trade(message, 4)
        message, kept = pl.pallas_call(
            merge_kernel,
            out_shape=(shape((256, hid), BF16), shape((128, hid), F32)),
            in_specs=[SMEM] + [VMEM] * 3,
            out_specs=(VMEM,) * 2,
            compiler_params=params(4),
            name="merge",
        )(y[None], got, keep, kept)
        got = trade(message, 8)
        f4 = around(f3, 1)
        kept, *messages = pl.pallas_call(
            fan_kernel,
            out_shape=(shape((32, hid), F32),) + (shape((160, hid), BF16),) * 3,
            in_specs=[VMEM] * 3,
            out_specs=(VMEM,) * 4,
            compiler_params=params(4),
            name="fan",
        )(got, message, kept)
        got = [trade(message, mask) for mask, message in zip((1, 2, 3), messages)]
        own, own_closure = pl.pallas_call(
            total_kernel,
            out_shape=(shape((128, hid), F32), shape((32, hid), F32)),
            in_specs=[VMEM] * 5,
            out_specs=(VMEM,) * 2,
            compiler_params=params(4),
            name="total",
        )(messages[0], kept, *got)
        other = trade(own, 4)
        halo = sources
        pieces = [piece, f1, b1, f2, b2, f3, b3, f4]
        pieces = [v[None] for v in pieces + [trade(v, 4) for v in pieces]]
    else:
        raw_first = first_part(0, samples, fcol, g2z)
        core = jnp.zeros((), jnp.int32)
        if not joined:
            raw_first = lax.psum(raw_first, "rep")
            body = lax.psum(piece[:rows].astype(F32), "rep")
            extra = lax.psum(piece[rows:].astype(F32), "rep")
            squares = jnp.sum(body * body)
            high = squares.astype(BF16).astype(F32)
            extra = extra.at[8, 0].set(high).at[8, 1].set(squares - high)
            piece = jnp.concatenate([body, extra], 0).astype(BF16)
        raw_first = lax.psum(raw_first, team)
        own, other = raw_first[:128], raw_first[128:]
        pieces = [lax.all_gather(piece, team)]
        piece_place = everyone
        part = closure.reshape(samples, n_slab, planes * 16, lanes // 2)
        part = jnp.swapaxes(part, 0, 1).reshape(size, planes * 16, lanes // 2).astype(F32)
        own_closure = lax.psum_scatter(part, team, scatter_dimension=0)
        halo = [sources[0].reshape(n_slab, samples, 16, cells)[:, sample]]
    new_fields = pl.pallas_call(
        functools.partial(step_kernel, nz),
        out_shape=shape(fields.shape, F32),
        in_specs=[SMEM] + [VMEM] * (2 + len(halo)),
        out_specs=VMEM,
        compiler_params=params(6),
        name="step",
    )(near, own_state, own_closure, *halo)

    weight_count = w_in.size + w_mid.size + w_out.size
    grad_middle, grad_first, grad_last = pl.pallas_call(
        functools.partial(finish_kernel, len(pieces), weight_count),
        out_shape=(shape((27, hid, hid), F32), shape((9, 27, hid), F32), shape((cout, hid), F32)),
        in_specs=[SMEM] * 2 + [VMEM] * (2 + len(pieces)),
        out_specs=(ANY, VMEM, VMEM),
        scratch_shapes=[
            pltpu.VMEM((size, rows + 16, hid), BF16),
            pltpu.VMEM((27, hid, hid), F32),
            pltpu.SemaphoreType.DMA((27,)),
        ],
        compiler_params=params(24),
        name="finish",
    )(piece_place, core[None], own, other, *pieces)
    return (new_fields, jnp.transpose(grad_first, (1, 0, 2)), grad_middle, grad_last.T)


def solution(mesh):
    placed = (
        P(("groups", "rep"), None, "slab", None, None),
        P(("groups", "rep"), "slab"),
        P(("groups", "rep"), None, "slab"),
        P(("groups", "rep"), "slab"),
        P(("groups", "rep"), "slab"),
        P(("groups", "rep"), "slab"),
        P(),
        P(),
        P(),
        P(("groups", "rep"), None, "slab", None, None),
    )
    return jax.shard_map(
        shards,
        mesh=mesh,
        in_specs=placed,
        out_specs=(
            P(("groups", "rep"), None, "slab", None, None),
            P("groups", None, None),
            P("groups", None, None),
            P("groups", None),
        ),
        check_vma=False,
    )
```

```python
import functools
import math

import jax
import jax.numpy as jnp
from jax import lax
from jax.experimental import pallas as pl
from jax.experimental.pallas import tpu as pltpu
from jax.sharding import PartitionSpec as P

dt_step = 0.2
viscosity = 0.05
drag_rate = 0.5
clip_rms = 0.5

F32 = jnp.float32
BF16 = jnp.bfloat16
offsets = [(x, y, z) for x in (-1, 0, 1) for y in (-1, 0, 1) for z in (-1, 0, 1)]


def dot(a, b):
    return lax.dot_general(a, b, (((1,), (0,)), ((), ())), preferred_element_type=F32)


def dot_nt(a, b):
    return lax.dot_general(a, b, (((1,), (1,)), ((), ())), preferred_element_type=F32)


def logistic(p):
    return 0.5 * jnp.tanh(0.5 * p) + 0.5


def roll_z(v, by, nz):
    return jnp.concatenate(
        [pltpu.roll(v[:, k : k + nz], by % nz, 1) for k in range(0, v.shape[1], nz)], 1
    )


def ahead_y(v, by, nz):
    if by == 0:
        return v
    cut = (by * nz) % v.shape[1]
    return jnp.concatenate([v[:, cut:], v[:, :cut]], 1)


def flat_cells(ref):
    planes, rows = ref.shape[2], ref.shape[3]
    return jnp.concatenate([ref[0, :, x, y, :] for x in range(planes) for y in range(rows)], 1)


def deposit_kernel(mass_in, vel_in, cell_in, listed_in, fields_in, cotangent_in, counts, stay, up, down, *held):
    *held, sems = held
    sources = (mass_in, vel_in, cell_in, listed_in, fields_in, cotangent_in)
    copies = [pltpu.make_async_copy(src, dst, sems.at[i]) for i, (src, dst) in enumerate(zip(sources, held))]
    for copy in copies:
        copy.start()
    mass, vel, cell, listed, fields, cotangent = held
    for copy in copies[:4]:
        copy.wait()
    drops = mass.shape[1]
    slots = listed.shape[1]
    half = slots // 2
    k = lax.broadcasted_iota(jnp.int32, (1, slots), 1)
    valid = k < jnp.where(k < half, counts[0, 0], half + counts[0, 1])
    chosen = jnp.where(valid, listed[...], -1)
    member = (lax.broadcasted_iota(jnp.int32, (drops, slots), 0) == chosen).astype(F32).astype(BF16)
    row = lax.broadcasted_iota(jnp.int32, (16, slots), 0)
    column = lax.broadcasted_iota(jnp.int32, (16, slots), 1)
    which = (row == (column >= half).astype(jnp.int32)).astype(F32).astype(BF16)
    mask = dot_nt(which, member)
    goes_up, goes_down = mask[0:1], mask[1:2]
    m = mass[...]
    charges = jnp.concatenate([m] + [m * vel[i] for i in range(vel.shape[0])], 0)
    high = charges.astype(BF16).astype(F32)
    both = jnp.concatenate([high, charges - high], 0)
    rows = jnp.concatenate(
        [both * (1.0 - goes_up - goes_down), both * goes_up, both * goes_down, jnp.zeros_like(both)], 0
    ).astype(BF16)
    chunk = 256
    for start in range(0, stay.shape[1], chunk):
        here = lax.broadcasted_iota(jnp.int32, (chunk, drops), 0) + start
        onehot = (here == cell[...]).astype(F32).astype(BF16)
        got = dot_nt(rows, onehot)
        for i, out in enumerate((stay, up, down)):
            out[0:4, start : start + chunk] = got[8 * i : 8 * i + 4] + got[8 * i + 4 : 8 * i + 8]
    for copy in copies[4:]:
        copy.wait()
    stay[4:9] = flat_cells(fields)
    stay[9:14] = dt_step * flat_cells(cotangent)
    stay[14:] = jnp.zeros((2, stay.shape[1]), F32)


def hold_kernel(values, out):
    out[...] = values[...]


def feature_kernel(stay, below, above, feats, own):
    deposit = stay[0:4] + below[...] + above[...]
    state = stay[4:9]
    force = drag_rate * (deposit[1:4] - deposit[0:1] * state[0:3])
    own[...] = jnp.concatenate([state, force], 0)
    cells = state.shape[1]
    feats[...] = jnp.concatenate(
        [
            stay[9:14],
            force[2:3],
            jnp.zeros((2, cells), F32),
            state,
            deposit[0:1],
            force[0:2],
        ],
        0,
    ).astype(BF16)


def tap_rows():
    r = lax.broadcasted_iota(jnp.int32, (288, 256), 0)
    k = lax.broadcasted_iota(jnp.int32, (288, 256), 1)
    c, t = r >> 5, r & 31
    ox = (t >= 9).astype(jnp.int32) + (t >= 18).astype(jnp.int32)
    q = t - 9 * ox
    ninth = jnp.where(q < 8, 216 + 8 * ox + q, 240 + ox)
    at = jnp.where(c < 8, 8 * t + c, ninth)
    return ((at == k) & (t < 27)).astype(F32).astype(BF16)


def chosen_columns(me, block, hid):
    row = lax.broadcasted_iota(jnp.int32, (block, hid), 0)
    column = lax.broadcasted_iota(jnp.int32, (block, hid), 1)
    return (column == row + me[0] * block).astype(F32).astype(BF16)


def outer_weight_kernel(me, w_in, w_out, packed):
    hid = packed.shape[1]
    pad = jnp.zeros((5, hid), F32)
    tall = jnp.concatenate([v for c in range(9) for v in (w_in[c].astype(F32), pad)], 0)
    packed[0:hid] = (0.5 * dot(tall.T.astype(BF16), tap_rows())).astype(BF16)
    wide = w_out[...].astype(F32)
    wide = jnp.concatenate([wide, jnp.zeros((16 - wide.shape[0], hid), F32)], 0).astype(BF16)
    chosen = chosen_columns(me, 16, hid)
    both = jnp.concatenate([dot_nt(chosen, wide), dot_nt(wide, chosen)], 0)
    packed[hid:] = jnp.concatenate([both, jnp.zeros((32, hid - 16), F32)], 1).astype(BF16)


def middle_weight_kernel(me, w_mid, wt, w_back):
    rows, hid = wt.shape
    block = rows // 27
    chosen = chosen_columns(me, block, hid)
    for t in range(27):
        wt[t * block : (t + 1) * block] = dot_nt(chosen, w_mid[t]).astype(BF16)
    w_back[...] = wt[...].astype(F32).T.astype(BF16)


def span(x, lanes, count=1):
    return slice(x * lanes, (x + count) * lanes)


def plane_taps(g2z, s, x, planes, nz, lanes):
    parts = []
    for ox, oy, oz in offsets:
        parts.append(ahead_y(g2z[s, oz + 1, :, span((x - ox) % planes, lanes)], -oy, nz))
    return jnp.concatenate(parts, 0)


def closure_kernel(nz, lanes, sources, place, wt, packed, *refs):
    arrived, refs = refs[:sources], refs[sources:]
    piece, closure, g2z, fcol, feats, fz, eighth, ninth, hidden, sums, mid, last = refs
    s = pl.program_id(0)
    samples = pl.num_programs(0)
    slabs = place.shape[0]
    cells = hidden.shape[1]
    planes = cells // lanes
    per = planes // slabs
    block = last.shape[1]
    group = 4
    hid = mid.shape[1]
    w_first = packed.at[0:hid]
    wo = packed[hid : hid + 16, 0:16]
    wc = packed[hid + 16 :, 0:16]

    @pl.when(s == 0)
    def _():
        mid[...] = jnp.zeros_like(mid)
        last[...] = jnp.zeros_like(last)
        at = 0
        for ref in arrived:
            feats[at : at + ref.shape[0]] = ref[...]
            at += ref.shape[0]

    sums[...] = jnp.zeros_like(sums)
    sub = lax.broadcasted_iota(jnp.int32, (8, lanes), 0)

    def spread(j):
        f = feats[place[j] + s].astype(F32)
        at = span(j, per * lanes)
        fz[0, :, at] = roll_z(f, 1, nz)
        fz[1, :, at] = f
        fz[2, :, at] = roll_z(f, -1, nz)

    for j in range(slabs):
        spread(j)

    def around(x):
        return [span((x + ox) % planes, lanes) for ox in (-1, 0, 1)]

    def ninth_rows(x):
        at = span(x, lanes)
        rows = [jnp.broadcast_to(fz[oz + 1, 5:6, at], (8, lanes)) for oz in (-1, 0, 1)]
        tile = ahead_y(rows[0], -1, nz)
        for q in range(1, 8):
            tile = jnp.where(sub == q, ahead_y(rows[q % 3], q // 3 - 1, nz), tile)
        eighth[:, at] = tile
        ninth[:, at] = ahead_y(rows[2], 1, nz)

    for x in range(planes):
        ninth_rows(x)

    def patches(x):
        near = around(x)
        pieces = [ahead_y(fz[oz + 1, 8:16, near[ox + 1]], oy, nz) for ox, oy, oz in offsets]
        pieces += [eighth[:, n] for n in near]
        tail = jnp.where(sub == 0, ninth[:, near[0]], jnp.where(sub == 1, ninth[:, near[1]], ninth[:, near[2]]))
        pieces += [jnp.where(sub < 3, tail, 0.0), jnp.zeros((8, lanes), F32)]
        fcol[s, :, near[1]] = jnp.concatenate(pieces, 0).astype(BF16)

    for x in range(planes):
        patches(x)

    def first(x):
        at = span(x, lanes)
        half = dot(w_first[...], fcol[s, :, at])
        hidden[:, at] = (half * jnp.tanh(half) + half).astype(BF16)

    for x in range(planes):
        first(x)

    def second(x):
        near = around(x)
        prod = dot(wt[...], hidden[:, near[1]])
        for ox in (-1, 0, 1):
            to = near[1 - ox]
            for oz in (-1, 0, 1):
                total = None
                for oy in (-1, 0, 1):
                    t = 9 * (ox + 1) + 3 * (oy + 1) + oz + 1
                    v = ahead_y(prod[t * block : (t + 1) * block], oy, nz)
                    total = v if total is None else total + v
                sums[oz + 1, :, to] += total

    for x in range(planes):
        second(x)

    def gradient(j):
        here = feats[place[j] + s]
        at = span(j, per * lanes)
        pre = sums[1, :, at] + roll_z(sums[0, :, at], 1, nz) + roll_z(sums[2, :, at], -1, nz)
        sig = logistic(pre)
        active = (pre * sig).astype(BF16)
        out = dot(wc, active)
        for h in range(per):
            left, right = h * lanes, h * lanes + lanes // 2
            both = [out[0:8, left:right], out[0:8, right : right + lanes // 2]]
            closure[s, j * per + h] = jnp.concatenate(both, 0).astype(BF16)
        grad = dot(wo, here) * (sig * (1.0 + pre * (1.0 - sig)))
        last[...] += dot_nt(here, active)
        rounded = grad.astype(BF16)
        grad = rounded.astype(F32)
        g2z[s, 0, :, at] = roll_z(grad, -1, nz).astype(BF16)
        g2z[s, 1, :, at] = rounded
        g2z[s, 2, :, at] = roll_z(grad, 1, nz).astype(BF16)

    for j in range(slabs):
        gradient(j)

    @pl.when(s >= 0)
    def _():
        for x in range(0, planes, group):
            columns = [plane_taps(g2z, s, x + h, planes, nz, lanes) for h in range(group)]
            mid[...] += dot_nt(jnp.concatenate(columns, 1), hidden[:, span(x, lanes, group)])

    @pl.when(s == samples - 1)
    def _():
        total = mid[...]
        taps = total.shape[0]
        piece[0:taps] = total.astype(BF16)
        squares = jnp.sum(total * total, keepdims=True)
        high = squares.astype(BF16).astype(F32)
        width = total.shape[1]
        row = lax.broadcasted_iota(jnp.int32, (block, width), 0)
        column = lax.broadcasted_iota(jnp.int32, (block, width), 1)
        extra = jnp.concatenate([last[...], jnp.zeros((block, width - block), F32)], 1)
        extra = jnp.where(row < 5, extra, 0.0)
        extra = jnp.where((row == 8) & (column == 0), high, extra)
        extra = jnp.where((row == 8) & (column == 1), squares - high, extra)
        piece[taps:] = extra.astype(BF16)


def first_kernel(nz, lanes, lo, packed, w_back, fcol, g2z, out):
    s = lo + pl.program_id(0)

    @pl.when(pl.program_id(0) == 0)
    def _():
        out[...] = jnp.zeros_like(out)

    planes = fcol.shape[2] // lanes
    group = 2
    w_first = packed.at[0 : w_back.shape[0]]
    for x in range(0, planes, group):
        at = span(x, lanes, group)
        columns = [plane_taps(g2z, s, x + h, planes, nz, lanes) for h in range(group)]
        back = dot(w_back[...], jnp.concatenate(columns, 1))
        column = fcol[s, :, at]
        half = dot(w_first[...], column)
        double = 1.0 + jnp.tanh(half)
        grad = (back * (double * (0.5 + half - 0.5 * half * double))).astype(BF16)
        out[...] += dot_nt(column, grad)


def split_kernel(core, one, two, closure, message, keep, kept):
    half = keep.shape[0]
    mine = pl.multiple_of(core[0] * half, half)
    theirs = pl.multiple_of((1 - core[0]) * half, half)
    keep[...] = one[pl.ds(mine, half)] + two[pl.ds(mine, half)]
    message[0:half] = one[pl.ds(theirs, half)] + two[pl.ds(theirs, half)]
    samples, planes = closure.shape[:2]
    at = 0
    for s in range(samples):
        for y in range(planes // 4):
            for p in range(2):
                kept[at : at + 16] = closure[s, 4 * y + 2 * core[0] + p].astype(F32)
                message[half + at : half + at + 16] = closure[s, 4 * y + 2 * (1 - core[0]) + p].astype(F32)
                at += 16


def merge_kernel(bit, got, mine, kept, message, keep):
    half = 128
    message[0:half] = (mine[...] + got[0:half]).astype(BF16)
    for o in range(keep.shape[0] // 32):
        a = pl.multiple_of((2 * o + bit[0]) * 32, 32)
        b = pl.multiple_of((2 * o + 1 - bit[0]) * 32, 32)
        keep[o * 32 : o * 32 + 32] = kept[pl.ds(a, 32)] + got[pl.ds(half + a, 32)]
        message[half + o * 32 : half + o * 32 + 32] = (kept[pl.ds(b, 32)] + got[pl.ds(half + b, 32)]).astype(BF16)


def fan_kernel(got, mine, kept, keep, *messages):
    half = 128
    raw = (mine[0:half].astype(F32) + got[0:half].astype(F32)).astype(BF16)
    for o in range(4):
        rows = kept[o * 32 : o * 32 + 32] + got[half + o * 32 : half + o * 32 + 32].astype(F32)
        if o == 0:
            keep[...] = rows
        else:
            messages[o - 1][0:half] = raw
            messages[o - 1][half:] = rows.astype(BF16)


def step_kernel(nz, place, own, closure, *refs):
    step_fields(nz, place, own, closure[...], refs[:-1], refs[-1])


def total_kernel(mine, kept, one, two, three, half, closure):
    pair = mine[0:128].astype(F32) + one[0:128].astype(F32)
    half[...] = pair + (two[0:128].astype(F32) + three[0:128].astype(F32))
    closure[...] = kept[...] + (one[128:].astype(F32) + two[128:].astype(F32) + three[128:].astype(F32))


def step_fields(nz, place, own, closure, sources, out):
    state = own[0:5]
    cells = state.shape[1]
    planes, rows = out.shape[2], out.shape[3]
    lanes = cells // planes
    lower, upper = (sources[0][place[i] if len(sources) == 1 else 0].astype(F32) for i in range(2))
    for g in range(1, len(sources)):
        other = sources[g][0].astype(F32)
        lower, upper = (jnp.where(place[i] == g, other, v) for i, v in enumerate((lower, upper)))
    lower, upper = lower[8:13, cells - lanes :], upper[8:13, :lanes]
    wide = jnp.concatenate([lower, state, upper], 1)
    next_x, last_x = wide[:, 2 * lanes :], wide[:, :cells]
    parts = [state[:, i * lanes : (i + 1) * lanes] for i in range(planes)]
    next_y = jnp.concatenate([ahead_y(v, 1, nz) for v in parts], 1)
    last_y = jnp.concatenate([ahead_y(v, -1, nz) for v in parts], 1)
    next_z, last_z = roll_z(state, -1, nz), roll_z(state, 1, nz)
    laplace = next_x + last_x + next_y + last_y + next_z + last_z - 6.0 * state
    advect = -0.5 * (
        state[0:1] * (next_x - last_x) + state[1:2] * (next_y - last_y) + state[2:3] * (next_z - last_z)
    )
    momentum = jnp.concatenate([own[5:8], jnp.zeros((2, cells), F32)], 0)
    closed = jnp.concatenate([closure[k : k + 5] for k in range(0, closure.shape[0], 8)], 1)
    new = state + dt_step * (viscosity * laplace + advect + closed + momentum)
    for x in range(planes):
        for y in range(rows):
            at = (x * rows + y) * nz
            out[0, :, x, y, :] = new[:, at : at + nz]


def finish_kernel(count, weight_count, place, core, own, other, *refs):
    pieces, (mid_out, first_out, last_out, held, done, leave) = refs[:count], refs[count:]
    slots = held.shape[0]
    block = done.shape[1] // slots
    rows = held.shape[1] - 16
    width = done.shape[1]

    at = 0
    for ref in pieces:
        held[at : at + ref.shape[0]] = ref[...]
        at += ref.shape[0]
    a, b = own[...], other[...]
    swapped = core[0] == 1
    raw = jnp.concatenate([jnp.where(swapped, b, a), jnp.where(swapped, a, b)], 0)
    squares = jnp.sum(raw * raw, keepdims=True)
    high = raw.astype(BF16)
    ordered = dot(tap_rows(), high) + dot(tap_rows(), (raw - high.astype(F32)).astype(BF16))
    last = []
    for d in range(slots):
        extra = held[place[d], rows:].astype(F32)
        last.append(extra[0:5, 0:block])
        squares = squares + jnp.sum(extra[8:9, 0:2], keepdims=True)
    last = jnp.concatenate(last, 1)
    squares = squares + jnp.sum(last * last, keepdims=True)
    clip = jnp.minimum(1.0, clip_rms * math.sqrt(weight_count) / jnp.sqrt(squares + 1e-06))
    last_out[...] = last * clip
    ordered = ordered * clip
    for c in range(first_out.shape[0]):
        first_out[c] = ordered[32 * c : 32 * c + 27]

    eye = (
        lax.broadcasted_iota(jnp.int32, (width, width), 0) == lax.broadcasted_iota(jnp.int32, (width, width), 1)
    ).astype(F32).astype(BF16)

    def leaving(t):
        return pltpu.make_async_copy(done.at[t], mid_out.at[t], leave.at[t])

    def flip(i, carry):
        for k in range(3):
            t = 3 * i + k
            start = pl.multiple_of(t * block, block)
            flipped = jnp.concatenate([held[place[d], pl.ds(start, block)] for d in range(slots)], 0)
            done[t] = dot_nt(eye, flipped) * clip
            leaving(t).start()
        return carry

    lax.fori_loop(0, 9, flip, 0, unroll=3)
    for t in range(27):
        leaving(t).wait()


def whole_spec(shape):
    return pl.BlockSpec(shape, lambda *unused: (0,) * len(shape))


SMEM = pl.BlockSpec(memory_space=pltpu.SMEM)
VMEM = pl.BlockSpec(memory_space=pltpu.VMEM)
ANY = pl.BlockSpec(memory_space=pl.ANY)
HBM = pl.BlockSpec(memory_space=pltpu.HBM)


def cost(flops):
    return pl.CostEstimate(flops=int(flops), bytes_accessed=2**22, transcendentals=0)


def params(mebibytes):
    return pltpu.CompilerParams(vmem_limit_bytes=mebibytes * 2**20)


def shards(
    fields, drop_mass, drop_vel, drop_cell, cross_list, cross_count, w_in, w_mid, w_out, cotangent
):
    shape = jax.ShapeDtypeStruct
    n_slab, n_rep = lax.axis_size("slab"), lax.axis_size("rep")
    planes, ny, nz = fields.shape[2:]
    cells = planes * ny * nz
    lanes = ny * nz
    hid, cout = w_out.shape
    joined = n_slab * n_rep * 16 <= hid
    team = ("slab", "rep") if joined else ("slab",)
    samples = n_rep if joined else 1
    size = n_slab * samples
    block = hid // size
    fast = joined and n_slab == 4 and n_rep == 4
    slab, rep = lax.axis_index("slab"), lax.axis_index("rep")
    sample = rep if joined else jnp.zeros((), jnp.int32)
    me = slab * samples + sample
    all_planes = n_slab * planes
    everyone = jnp.arange(size, dtype=jnp.int32)

    def trade(v, mask):
        return lax.ppermute(v, team, [(d, d ^ mask) for d in range(size)])

    dense = shape((4, cells), F32)
    flows = (drop_mass, jnp.transpose(drop_vel, (1, 0, 2)), drop_cell, cross_list, fields, cotangent)
    stay, up, down = pl.pallas_call(
        deposit_kernel,
        out_shape=(shape((16, cells), F32), dense, dense),
        in_specs=[HBM] * 6 + [SMEM],
        out_specs=(VMEM,) * 3,
        scratch_shapes=[pltpu.VMEM(v.shape, v.dtype) for v in flows] + [pltpu.SemaphoreType.DMA((6,))],
        compiler_params=params(60),
        name="deposit",
    )(*flows, cross_count)
    stay = pl.pallas_call(
        hold_kernel,
        out_shape=shape(stay.shape, F32),
        in_specs=[VMEM],
        out_specs=VMEM,
        compiler_params=params(4),
        name="hold",
    )(stay)
    from_below = lax.ppermute(up, "slab", [(i, (i + 1) % n_slab) for i in range(n_slab)])
    from_above = lax.ppermute(down, "slab", [((i + 1) % n_slab, i) for i in range(n_slab)])
    own_feats, own_state = pl.pallas_call(
        feature_kernel,
        out_shape=(shape((16, cells), BF16), shape((8, cells), F32)),
        in_specs=[VMEM] * 3,
        out_specs=(VMEM,) * 2,
        compiler_params=params(4),
        name="features",
    )(stay, from_below, from_above)

    rows = 27 * block
    own_feats, late_me, late_in, late_out = lax.optimization_barrier((own_feats, me, w_in, w_out))
    packed = pl.pallas_call(
        outer_weight_kernel,
        out_shape=shape((hid + 32, hid), BF16),
        in_specs=[SMEM] + [VMEM] * 2,
        out_specs=VMEM,
        compiler_params=params(8),
        name="outer_weights",
    )(late_me[None], jnp.transpose(late_in, (1, 0, 2)), late_out.T)

    if fast:
        far, middle, close = (trade(own_feats, mask) for mask in (3, 2, 1))
        near_z = [close, middle, far]
        packed, *near_z = lax.optimization_barrier((packed, *near_z))
        mine = jnp.stack([own_feats] + near_z)
        mine, late_me, late_mid = lax.optimization_barrier((mine, me, w_mid))
        across = trade(mine, 8)

        def held_at(slabs):
            return 2 * ((slabs ^ slab) & 1) + (((slabs ^ slab) >> 1) & 1)
    else:
        sources = [lax.all_gather(own_feats, team)]
        late_me, late_mid = me, w_mid

        def held_at(slabs):
            return slabs

    wt, w_back = pl.pallas_call(
        middle_weight_kernel,
        out_shape=(shape((rows, hid), BF16), shape((hid, rows), BF16)),
        in_specs=[SMEM, VMEM],
        out_specs=(VMEM,) * 2,
        compiler_params=params(16),
        cost_estimate=cost(1.5e9),
        name="middle_weights",
    )(late_me[None], late_mid)
    if fast:
        across, wt, w_back = lax.optimization_barrier((across, wt, w_back))
        sources = [mine, across, trade(mine, 4), trade(across, 4)]
    place = held_at(jnp.arange(n_slab, dtype=jnp.int32)) * samples
    near = held_at((slab + jnp.array([n_slab - 1, 1], jnp.int32)) % n_slab)

    team_cells = all_planes * lanes
    piece, closure, g2z, fcol = pl.pallas_call(
        functools.partial(closure_kernel, nz, lanes, len(sources)),
        grid=(samples,),
        out_shape=(
            shape((rows + 16, hid), BF16),
            shape((samples, all_planes, 16, lanes // 2), BF16),
            shape((samples, 3, block, team_cells), BF16),
            shape((samples, 256, team_cells), BF16),
        ),
        in_specs=[SMEM] + [VMEM] * (2 + len(sources)),
        out_specs=(
            VMEM,
            VMEM,
            VMEM,
            VMEM,
        ),
        scratch_shapes=[
            pltpu.VMEM((size, 16, cells), BF16),
            pltpu.VMEM((3, 16, team_cells), F32),
            pltpu.VMEM((8, team_cells), F32),
            pltpu.VMEM((8, team_cells), F32),
            pltpu.VMEM((hid, team_cells), BF16),
            pltpu.VMEM((3, block, team_cells), F32),
            pltpu.VMEM((rows, hid), F32),
            pltpu.VMEM((16, block), F32),
        ],
        compiler_params=params(30 if all_planes <= 8 else 58),
        cost_estimate=cost(9e9),
        name="closure",
    )(place, wt, packed, *sources)

    def first_part(lo, count, fcol, g2z):
        return pl.pallas_call(
            functools.partial(first_kernel, nz, lanes, lo),
            grid=(count,),
            out_shape=shape((256, hid), F32),
            in_specs=[VMEM] * 4,
            out_specs=VMEM,
            compiler_params=params(18 if all_planes <= 8 else 58),
            cost_estimate=cost(7.6e9 * count / samples),
            name="first",
        )(packed, w_back, fcol, g2z)

    if fast:
        core, y = slab & 1, slab >> 1

        def chip(at):
            at = at % 8
            return (0, at) if at < 4 else (1, 7 - at)

        def device(at, c):
            y, z = chip(at)
            return (2 * y + c) * n_rep + z

        def around(v, by):
            return lax.ppermute(v, team, [(device(at, c), device(at + by, c)) for at in range(8) for c in range(2)])

        def tie(*values):
            return lax.optimization_barrier(values)

        position = jnp.where(y == 0, rep, 7 - rep)
        theirs, their_z = everyone // n_rep, everyone % n_rep
        apart = (jnp.where(theirs < 2, their_z, 7 - their_z) - position) % 8
        piece_place = jnp.where(apart < 4, 2 * apart, 2 * (8 - apart) - 1)
        piece_place = jnp.where(apart == 0, 0, piece_place) + 8 * ((theirs ^ slab) & 1)
        piece_place = piece_place.astype(jnp.int32)
        f1, b1 = around(piece, 1), around(piece, -1)
        half_one = first_part(0, samples // 2, fcol, g2z)
        f1, b1, half_one, fcol, g2z, piece_place, near = tie(f1, b1, half_one, fcol, g2z, piece_place, near)
        f2, b2 = around(f1, 1), around(b1, -1)
        half_two = first_part(samples // 2, samples - samples // 2, fcol, g2z)
        f2, b2, half_two = tie(f2, b2, half_two)
        f3, b3 = around(f2, 1), around(b2, -1)

        message, keep, kept = pl.pallas_call(
            split_kernel,
            out_shape=(shape((384, hid), F32), shape((128, hid), F32), shape((256, hid), F32)),
            in_specs=[SMEM] + [VMEM] * 3,
            out_specs=(VMEM,) * 3,
            compiler_params=params(4),
            name="split",
        )(core[None], half_one, half_two, closure)
        got = trade(message, 4)
        message, kept = pl.pallas_call(
            merge_kernel,
            out_shape=(shape((256, hid), BF16), shape((128, hid), F32)),
            in_specs=[SMEM] + [VMEM] * 3,
            out_specs=(VMEM,) * 2,
            compiler_params=params(4),
            name="merge",
        )(y[None], got, keep, kept)
        got = trade(message, 8)
        f4 = around(f3, 1)
        kept, *messages = pl.pallas_call(
            fan_kernel,
            out_shape=(shape((32, hid), F32),) + (shape((160, hid), BF16),) * 3,
            in_specs=[VMEM] * 3,
            out_specs=(VMEM,) * 4,
            compiler_params=params(4),
            name="fan",
        )(got, message, kept)
        got = [trade(message, mask) for mask, message in zip((1, 2, 3), messages)]
        own, own_closure = pl.pallas_call(
            total_kernel,
            out_shape=(shape((128, hid), F32), shape((32, hid), F32)),
            in_specs=[VMEM] * 5,
            out_specs=(VMEM,) * 2,
            compiler_params=params(4),
            name="total",
        )(messages[0], kept, *got)
        other = trade(own, 4)
        halo = sources
        pieces = [piece, f1, b1, f2, b2, f3, b3, f4]
        pieces = [v[None] for v in pieces + [trade(v, 4) for v in pieces]]
    else:
        raw_first = first_part(0, samples, fcol, g2z)
        core = jnp.zeros((), jnp.int32)
        if not joined:
            raw_first = lax.psum(raw_first, "rep")
            body = lax.psum(piece[:rows].astype(F32), "rep")
            extra = lax.psum(piece[rows:].astype(F32), "rep")
            squares = jnp.sum(body * body)
            high = squares.astype(BF16).astype(F32)
            extra = extra.at[8, 0].set(high).at[8, 1].set(squares - high)
            piece = jnp.concatenate([body, extra], 0).astype(BF16)
        raw_first = lax.psum(raw_first, team)
        own, other = raw_first[:128], raw_first[128:]
        pieces = [lax.all_gather(piece, team)]
        piece_place = everyone
        part = closure.reshape(samples, n_slab, planes * 16, lanes // 2)
        part = jnp.swapaxes(part, 0, 1).reshape(size, planes * 16, lanes // 2).astype(F32)
        own_closure = lax.psum_scatter(part, team, scatter_dimension=0)
        halo = [sources[0].reshape(n_slab, samples, 16, cells)[:, sample]]
    new_fields = pl.pallas_call(
        functools.partial(step_kernel, nz),
        out_shape=shape(fields.shape, F32),
        in_specs=[SMEM] + [VMEM] * (2 + len(halo)),
        out_specs=VMEM,
        compiler_params=params(6),
        name="step",
    )(near, own_state, own_closure, *halo)

    weight_count = w_in.size + w_mid.size + w_out.size
    grad_middle, grad_first, grad_last = pl.pallas_call(
        functools.partial(finish_kernel, len(pieces), weight_count),
        out_shape=(shape((27, hid, hid), F32), shape((9, 27, hid), F32), shape((cout, hid), F32)),
        in_specs=[SMEM] * 2 + [VMEM] * (2 + len(pieces)),
        out_specs=(ANY, VMEM, VMEM),
        scratch_shapes=[
            pltpu.VMEM((size, rows + 16, hid), BF16),
            pltpu.VMEM((27, hid, hid), F32),
            pltpu.SemaphoreType.DMA((27,)),
        ],
        compiler_params=params(24),
        name="finish",
    )(piece_place, core[None], own, other, *pieces)
    return (new_fields, jnp.transpose(grad_first, (1, 0, 2)), grad_middle, grad_last.T)


def solution(mesh):
    placed = (
        P(("groups", "rep"), None, "slab", None, None),
        P(("groups", "rep"), "slab"),
        P(("groups", "rep"), None, "slab"),
        P(("groups", "rep"), "slab"),
        P(("groups", "rep"), "slab"),
        P(("groups", "rep"), "slab"),
        P(),
        P(),
        P(),
        P(("groups", "rep"), None, "slab", None, None),
    )
    return jax.shard_map(
        shards,
        mesh=mesh,
        in_specs=placed,
        out_specs=(
            P(("groups", "rep"), None, "slab", None, None),
            P("groups", None, None),
            P("groups", None, None),
            P("groups", None),
        ),
        check_vma=False,
    )
```
